128 devices in a mesh: section: 2 (over x_lo), replica: 4 (over x_hi, core), shard: 16 (over z, y).
Axes of the slice: x: 4 (x_hi: 2, x_lo: 2; x = x_hi * 2 + x_lo), y: 4, z: 4, core: 2. Of those that a mesh axis runs over, the one named last changes fastest.
Arguments:
- layer_input: bfloat16 [2, 64, 128, 1024], P(None, ('replica', 'shard')), may hold values from -6 to 6
- cotangent: bfloat16 [2, 64, 128, 1024], P(None, ('replica', 'shard')), may hold values from -6 to 6
- project_weight: bfloat16 [2, 1024, 3072], P('section', 'shard'), may hold values from -0.1875 to 0.1875
- output_weight: bfloat16 [2, 1024, 1024], P('section', 'shard'), may hold values from -0.5 to 0.5
- up_weight: bfloat16 [2, 1024, 4096], P('section', 'shard'), may hold values from -0.1875 to 0.1875
- down_weight: bfloat16 [2, 4096, 1024], P('section', 'shard'), may hold values from -0.09375 to 0.09375
- query_bias: bfloat16 [2, 1024], P('section', 'shard'), may hold values from -3 to 3
- value_bias: bfloat16 [2, 1024], P('section', 'shard'), may hold values from -3 to 3
- output_bias: bfloat16 [2, 1024], P('section', 'shard'), may hold values from -3 to 3
- up_bias: bfloat16 [2, 4096], P('section', 'shard'), may hold values from -3 to 3
- down_bias: bfloat16 [2, 1024], P('section', 'shard'), may hold values from -3 to 3
- first_gain: bfloat16 [2, 1024], P('section', 'shard'), may hold values from 0.5 to 1.5
- first_shift: bfloat16 [2, 1024], P('section', 'shard'), may hold values from -2 to 2
- second_gain: bfloat16 [2, 1024], P('section', 'shard'), may hold values from 0.5 to 1.5
- second_shift: bfloat16 [2, 1024], P('section', 'shard'), may hold values from -2 to 2
Outputs:
- layer_output: bfloat16 [2, 2, 64, 128, 1024], P('section', None, ('replica', 'shard'))
- input_grad: bfloat16 [2, 2, 64, 128, 1024], P('section', None, ('replica', 'shard'))
- project_grad: float32 [2, 1024, 3072], P('section', 'shard')
- output_grad: float32 [2, 1024, 1024], P('section', 'shard')
- up_grad: float32 [2, 1024, 4096], P('section', 'shard')
- down_grad: float32 [2, 4096, 1024], P('section', 'shard')
- query_bias_grad: float32 [2, 1024], P('section', 'shard')
- value_bias_grad: float32 [2, 1024], P('section', 'shard')
- output_bias_grad: float32 [2, 1024], P('section', 'shard')
- up_bias_grad: float32 [2, 4096], P('section', 'shard')
- down_bias_grad: float32 [2, 1024], P('section', 'shard')
- first_gain_grad: float32 [2, 1024], P('section', 'shard')
- first_shift_grad: float32 [2, 1024], P('section', 'shard')
- second_gain_grad: float32 [2, 1024], P('section', 'shard')
- second_shift_grad: float32 [2, 1024], P('section', 'shard')
The draws below stay inside these ranges and needn't reach their ends.
All inputs are finite; a program needn't handle non-finite values.
Results may differ from the reference program's by a relative error of at most 0.02.
Values may be sent and summed in bfloat16 or wider, within the bound.
No kernel may reach another device: no remote copies, remote signals or barrier semaphores. Data moves between devices by JAX's collectives and lax.ppermute only.
A program may use at most 192 MiB of HBM per device.

```python
import jax
import jax.numpy as jnp
from jax import lax

D = 1024
FF = 4096
HEADS = 16
HEAD_DIM = 64
LEN = 128
MICRO = 2
SEQS = 64


def block_scale(own_key, extent, cuts, least, high):
    def one(axis_at, shards_of):
        draws = jax.random.uniform(jax.random.fold_in(jax.random.fold_in(own_key, 6), axis_at), (shards_of,), jnp.float32, least / len(cuts), high / len(cuts))
        return jnp.repeat(jnp.exp(draws), extent[axis_at] // shards_of).reshape((-1,) + (1,) * (len(extent) - axis_at - 1))

    gain = one(*cuts[0])
    for cut in cuts[1:]:
        gain = gain * one(*cut)
    return gain


def normal_values(stream_key, dims, scale, most, shards=(), kind=jnp.bfloat16):
    loudness = block_scale(stream_key, dims, shards, -0.22, 0.18) if shards else 1.0
    array = jax.random.normal(stream_key, dims, jnp.float32) * scale * loudness
    return jnp.minimum(jnp.maximum(array, -most), most).astype(kind)


def setup_inputs(seed: int = 0) -> dict:
    seeds = jax.random.split(jax.random.key(seed), 16)
    return {
        "layer_input": normal_values(seeds[0], (MICRO, SEQS, LEN, D), 1.0, 6.0, ((1, 64),)),
        "cotangent": normal_values(seeds[1], (MICRO, SEQS, LEN, D), 1.0, 6.0, ((1, 64),)),
        "project_weight": normal_values(seeds[2], (2, D, 3 * D), D ** -0.5, 0.1875, ((0, 2), (1, 16))),
        "output_weight": normal_values(seeds[3], (2, D, D), (D // 8) ** -0.5, 0.5, ((0, 2), (1, 16))),
        "up_weight": normal_values(seeds[4], (2, D, FF), D ** -0.5, 0.1875, ((0, 2), (1, 16))),
        "down_weight": normal_values(seeds[5], (2, FF, D), FF ** -0.5, 0.09375, ((0, 2), (1, 16))),
        "query_bias": normal_values(seeds[6], (2, D), 0.5, 3.0, ((0, 2), (1, 16))),
        "value_bias": normal_values(seeds[7], (2, D), 0.5, 3.0, ((0, 2), (1, 16))),
        "output_bias": normal_values(seeds[8], (2, D), 0.5, 3.0, ((0, 2), (1, 16))),
        "up_bias": normal_values(seeds[9], (2, FF), 0.5, 3.0, ((0, 2), (1, 16))),
        "down_bias": normal_values(seeds[10], (2, D), 0.5, 3.0, ((0, 2), (1, 16))),
        "first_gain": jnp.clip(1.0 + 0.1 * jax.random.normal(seeds[11], (2, D), jnp.float32), 0.5, 1.5).astype(jnp.bfloat16),
        "first_shift": normal_values(seeds[12], (2, D), 0.3, 2.0, ((0, 2), (1, 16))),
        "second_gain": jnp.clip(1.0 + 0.1 * jax.random.normal(seeds[13], (2, D), jnp.float32), 0.5, 1.5).astype(jnp.bfloat16),
        "second_shift": normal_values(seeds[14], (2, D), 0.3, 2.0, ((0, 2), (1, 16))),
    }


EPSILON = 1e-06
HIGHEST = lax.Precision.HIGHEST

@jax.custom_vjp
def low(v):
    return lax.optimization_barrier(v.astype(jnp.bfloat16)).astype(jnp.float32)

@jax.custom_vjp
def low_back(v):
    return v

def low_keep(v):
    return (low(v), None)

def low_pass(kept, grad):
    return (grad,)

def back_keep(v):
    return (v, None)

def back_low(kept, grad):
    return (low(grad),)
low.defvjp(low_keep, low_pass)
low_back.defvjp(back_keep, back_low)

def norm_layer(totals, gain_row, shift_row):
    average = lax.optimization_barrier(jnp.mean(totals, -1, keepdims=True))
    centred = totals - average
    variance = lax.optimization_barrier(jnp.mean(centred * centred, -1, keepdims=True))
    return centred * lax.rsqrt(variance + EPSILON) * gain_row + shift_row

def product(left, right):
    return jnp.dot(left, right, precision=HIGHEST)

def encoder_layer(inputs, weights):
    project, output, upward, downward, query_row, value_row, output_row, up_row, down_row, gain_one, shift_one, gain_two, shift_two = weights
    width = output.shape[0]
    biases = jnp.concatenate([query_row, jnp.zeros((width,), jnp.float32), value_row])
    packed = low(low_back(product(inputs, project) + biases))
    heads_view = packed.reshape(-1, LEN, 3, HEADS, HEAD_DIM)
    queries = heads_view[:, :, 0]
    keys_all = heads_view[:, :, 1]
    values_all = heads_view[:, :, 2]
    scores = low_back(jnp.einsum('sqhe,skhe->shqk', queries, keys_all, precision=HIGHEST) * HEAD_DIM ** (-0.5))
    soft = low(jax.nn.softmax(scores, axis=-1))
    attended = jnp.einsum('shqk,skhe->sqhe', soft, values_all, precision=HIGHEST).reshape(-1, width)
    attended = low(low_back(attended))
    branch = low_back(product(attended, output) + output_row)
    hidden = norm_layer(inputs + branch, gain_one, shift_one)
    upper = low_back(product(low(hidden), upward) + up_row)
    activated = low(jax.nn.gelu(upper, approximate=False))
    lower_branch = low_back(product(activated, downward) + down_row)
    return norm_layer(hidden + lower_branch, gain_two, shift_two)

def reference(layer_input, cotangent, project_weight, output_weight, up_weight, down_weight, query_bias, value_bias, output_bias, up_bias, down_bias, first_gain, first_shift, second_gain, second_shift):
    params = (project_weight, output_weight, up_weight, down_weight, query_bias, value_bias, output_bias, up_bias, down_bias, first_gain, first_shift, second_gain, second_shift)
    as_float = [param.astype(jnp.float32) for param in params]
    first_params = tuple((param[0] for param in as_float))
    second_params = tuple((param[1] for param in as_float))
    width = layer_input.shape[-1]
    start_rows = layer_input.astype(jnp.float32).reshape(-1, width)

    def forward(start, carry_zero, first_set, second_set):
        first_result = encoder_layer(start, first_set)
        passed = low(low_back(first_result + carry_zero))
        return (first_result, encoder_layer(passed, second_set))
    zero_rows = jnp.zeros_like(start_rows)
    (first_result, second_result), pullback = jax.vjp(forward, start_rows, zero_rows, first_params, second_params)
    start_grad, passed_grad, first_grads, second_grads = pullback((jnp.zeros_like(first_result), cotangent.astype(jnp.float32).reshape(-1, width)))
    shape = layer_input.shape
    layer_output = jnp.stack([first_result.reshape(shape), second_result.reshape(shape)]).astype(jnp.bfloat16)
    input_grad = jnp.stack([start_grad.reshape(shape), passed_grad.reshape(shape)]).astype(jnp.bfloat16)
    grads = tuple((jnp.stack([first_piece, second_piece]) for first_piece, second_piece in zip(first_grads, second_grads)))
    return (layer_output, input_grad, grads[0], grads[1], grads[2], grads[3], grads[4], grads[5], grads[6], grads[7], grads[8], grads[9], grads[10], grads[11], grads[12])
```

```python
import jax
import jax.numpy as jnp
from jax import lax
from jax.sharding import Mesh
from jax.sharding import PartitionSpec as P

HEADS = 16
HEAD_DIM = 64
LEN = 128
WIDTH = 1024
HIDDEN = 4096
SCALE = HEAD_DIM ** (-0.5)
EPSILON = 1e-06

F32 = jnp.float32
BF16 = jnp.bfloat16


def matmul(left, right):
    return jnp.dot(left, right, preferred_element_type=F32)


def matmul_back(left, right):
    return lax.dot_general(left, right, (((1,), (1,)), ((), ())), preferred_element_type=F32)


def matmul_rows(left, right):
    return lax.dot_general(left, right, (((0,), (0,)), ((), ())), preferred_element_type=F32)


def gelu_exact(values):
    return jax.nn.gelu(values, approximate=False)


def swap_cores(value):
    return lax.ppermute(value, "core", [(0, 1), (1, 0)])


def swap_far(value):
    return lax.ppermute(value, "far", [(0, 1), (1, 0)])


def norm_forward(totals, gain_row, shift_row):
    average = jnp.mean(totals, -1, keepdims=True)
    centred = totals - average
    inverse = lax.rsqrt(jnp.mean(centred * centred, -1, keepdims=True) + EPSILON)
    normed = centred * inverse
    return (normed * gain_row + shift_row, normed, inverse)


def norm_backward(upstream, normed, inverse, gain_row):
    scaled = upstream * gain_row
    return inverse * (
        scaled
        - jnp.mean(scaled, -1, keepdims=True)
        - normed * jnp.mean(scaled * normed, -1, keepdims=True)
    )


def gather_weights(project, output, upward, downward, vectors):
    core = lax.axis_index("core")
    half = lax.dynamic_slice_in_dim(
        jnp.concatenate([project, output, upward], 1), core * 32, 32, 0
    )
    down = lax.dynamic_slice_in_dim(downward, core * 128, 128, 0)
    down = down.reshape(4, 32, WIDTH).transpose(1, 0, 2).reshape(32, HIDDEN)
    flat = jnp.concatenate(vectors).reshape(6, 128)
    extra = jnp.concatenate([flat, jnp.zeros((26, 128), BF16)], 0)
    packed = jnp.concatenate([half, down, extra], 1)
    whole = lax.all_gather(packed, ("z", "y", "core"), axis=0, tiled=True)
    rows = whole[:, 12288:].reshape(16, 64, 128)[:, :6].astype(F32)
    pairs = rows[:, :4].reshape(16, 8, 64).transpose(1, 0, 2).reshape(8, WIDTH)
    ups = rows[:, 4:].reshape(HIDDEN)
    down_whole = (
        whole[:, 8192:12288]
        .reshape(32, 32, 4, WIDTH)
        .transpose(0, 2, 1, 3)
        .reshape(HIDDEN, WIDTH)
    )
    return (
        (whole[:, :3072], whole[:, 3072:4096], whole[:, 4096:8192], down_whole),
        (pairs, ups),
    )


def layer_forward(rows16, weights, vectors):
    project, output, upward, downward = weights
    pairs, ups = vectors
    query_row, value_row, output_row, down_row, gain_one, shift_one, gain_two, shift_two = pairs
    biases = jnp.concatenate([query_row, jnp.zeros((WIDTH,), F32), value_row])
    packed = (matmul(rows16, project) + biases).astype(BF16)
    heads_view = packed.reshape(-1, LEN, 3, HEADS, HEAD_DIM)
    scores = (
        jnp.einsum(
            "sqhe,skhe->shqk", heads_view[:, :, 0], heads_view[:, :, 1], preferred_element_type=F32
        )
        * SCALE
    )
    log_totals = jax.nn.logsumexp(scores, axis=-1, keepdims=True)
    soft16 = jnp.exp(scores - log_totals).astype(BF16)
    attended = (
        jnp.einsum("shqk,skhe->sqhe", soft16, heads_view[:, :, 2], preferred_element_type=F32)
        .reshape(-1, WIDTH)
        .astype(BF16)
    )
    residual_one = rows16.astype(F32) + (matmul(attended, output) + output_row)
    hidden, normed_one, inverse_one = norm_forward(residual_one, gain_one, shift_one)
    hidden16 = hidden.astype(BF16)
    upper = matmul(hidden16, upward) + ups
    active16 = gelu_exact(upper).astype(BF16)
    residual_two = hidden + (matmul(active16, downward) + down_row)
    result, normed_two, inverse_two = norm_forward(residual_two, gain_two, shift_two)
    kept = (
        rows16,
        packed,
        log_totals,
        attended,
        normed_one,
        inverse_one,
        hidden16,
        upper,
        active16,
        normed_two,
        inverse_two,
    )
    return (result.astype(BF16), kept)


def layer_backward(upstream, kept, weights, vectors):
    project, output, upward, downward = weights
    pairs, ups = vectors
    query_row, value_row, output_row, down_row, gain_one, shift_one, gain_two, shift_two = pairs
    (
        rows16,
        packed,
        log_totals,
        attended,
        normed_one,
        inverse_one,
        hidden16,
        upper,
        active16,
        normed_two,
        inverse_two,
    ) = kept
    upstream = upstream.astype(F32)
    gain_two_grad = jnp.sum(upstream * normed_two, 0)
    shift_two_grad = jnp.sum(upstream, 0)
    total_two_grad = norm_backward(upstream, normed_two, inverse_two, gain_two)
    down_grad16 = total_two_grad.astype(BF16)
    active_grad = matmul_back(down_grad16, downward)
    upper_grad16 = jax.vjp(gelu_exact, upper)[1](active_grad)[0].astype(BF16)
    hidden_grad = matmul_back(upper_grad16, upward) + total_two_grad
    gain_one_grad = jnp.sum(hidden_grad * normed_one, 0)
    shift_one_grad = jnp.sum(hidden_grad, 0)
    total_grad = norm_backward(hidden_grad, normed_one, inverse_one, gain_one)
    branch_grad16 = total_grad.astype(BF16)
    attended_grad16 = (
        matmul_back(branch_grad16, output).astype(BF16).reshape(-1, LEN, HEADS, HEAD_DIM)
    )
    heads_view = packed.reshape(-1, LEN, 3, HEADS, HEAD_DIM)
    queries = heads_view[:, :, 0]
    keys_all = heads_view[:, :, 1]
    values_all = heads_view[:, :, 2]
    scores = jnp.einsum("sqhe,skhe->shqk", queries, keys_all, preferred_element_type=F32) * SCALE
    soft = jnp.exp(scores - log_totals)
    soft16 = soft.astype(BF16)
    values_grad = jnp.einsum(
        "shqk,sqhe->skhe", soft16, attended_grad16, preferred_element_type=F32
    )
    soft_grad = jnp.einsum(
        "sqhe,skhe->shqk", attended_grad16, values_all, preferred_element_type=F32
    )
    scores_grad16 = (
        soft * (soft_grad - jnp.sum(soft_grad * soft, -1, keepdims=True))
    ).astype(BF16)
    queries_grad = (
        jnp.einsum("shqk,skhe->sqhe", scores_grad16, keys_all, preferred_element_type=F32) * SCALE
    )
    keys_grad = (
        jnp.einsum("shqk,sqhe->skhe", scores_grad16, queries, preferred_element_type=F32) * SCALE
    )
    packed_grad16 = (
        jnp.stack([queries_grad, keys_grad, values_grad], 2).reshape(-1, 3 * WIDTH).astype(BF16)
    )
    rows_grad = matmul_back(packed_grad16, project) + total_grad
    packed_sums = jnp.sum(packed_grad16.astype(F32), 0)
    vector_grads = (
        jnp.stack(
            [
                packed_sums[:WIDTH],
                packed_sums[2 * WIDTH :],
                jnp.sum(branch_grad16.astype(F32), 0),
                jnp.sum(down_grad16.astype(F32), 0),
                gain_one_grad,
                shift_one_grad,
                gain_two_grad,
                shift_two_grad,
            ]
        ),
        jnp.sum(upper_grad16.astype(F32), 0),
    )
    pieces = (
        (rows16, packed_grad16),
        (attended, branch_grad16),
        (hidden16, upper_grad16),
        (active16, down_grad16),
    )
    return (rows_grad.astype(BF16), pieces, vector_grads)


def reduce_grads(pieces, vector_grads):
    core = lax.axis_index("core")

    def half(array, which):
        width = array.shape[1] // 2
        return lax.dynamic_slice_in_dim(array, which * width, width, 1)

    def block(left, right, which):
        return matmul_rows(left, half(right, which))

    others = [swap_cores(block(left, right, 1 - core).astype(BF16)) for left, right in pieces]
    sums = [
        (block(left, right, core) + other.astype(F32)).astype(BF16)
        for (left, right), other in zip(pieces, others)
    ]
    project, output, upward, downward = sums
    parts = [
        *(project.reshape(16, 64, 3, 512)[:, :, k] for k in range(3)),
        output.reshape(16, 64, 512),
        *(upward.reshape(16, 64, 4, 512)[:, :, k] for k in range(4)),
        downward.reshape(16, 256, 512),
    ]
    pairs, ups = vector_grads
    first = pairs.reshape(8, 16, 64).transpose(1, 0, 2).reshape(16, 1, 512)
    second = jnp.concatenate([ups.reshape(16, 1, 256), jnp.zeros((16, 1, 256), F32)], 2)
    extra = jnp.concatenate([first, second, jnp.zeros((16, 14, 512), F32)], 1).astype(BF16)
    packed = jnp.concatenate([*parts, extra], 1).reshape(16 * 784, 512)
    owned = lax.psum_scatter(packed, ("z", "y"), scatter_dimension=0, tiled=True)
    owned = lax.optimization_barrier(owned)
    total = owned.astype(F32) + swap_far(owned).astype(F32)
    total = lax.optimization_barrier(total)
    other = swap_cores(total)
    low = jnp.where(core == 0, total, other)
    high = jnp.where(core == 0, other, total)

    def columns(start, count, rows=64):
        left = [low[start + k * rows : start + (k + 1) * rows] for k in range(count)]
        right = [high[start + k * rows : start + (k + 1) * rows] for k in range(count)]
        return jnp.concatenate(left + right, 1)[None]

    vectors = (total[768:770] + other[768:770]).reshape(1024)
    narrow = [vectors[64 * k : 64 * (k + 1)][None] for k in range(8)]
    query, value, output_b, down_b, gain_one, shift_one, gain_two, shift_two = narrow
    return (
        columns(0, 3),
        columns(192, 1),
        columns(256, 4),
        columns(512, 1, 256),
        query,
        value,
        output_b,
        vectors[512:768][None],
        down_b,
        gain_one,
        shift_one,
        gain_two,
        shift_two,
    )


def on_device(
    layer_input,
    cotangent,
    project_weight,
    output_weight,
    up_weight,
    down_weight,
    query_bias,
    value_bias,
    output_bias,
    up_bias,
    down_bias,
    first_gain,
    first_shift,
    second_gain,
    second_shift,
):
    first_section = lax.axis_index("section") == 0
    weights, vectors = gather_weights(
        project_weight[0],
        output_weight[0],
        up_weight[0],
        down_weight[0],
        (
            query_bias[0],
            value_bias[0],
            output_bias[0],
            down_bias[0],
            first_gain[0],
            first_shift[0],
            second_gain[0],
            second_shift[0],
            up_bias[0],
        ),
    )
    shape = layer_input.shape
    own_rows = layer_input.reshape(-1, WIDTH)
    own_grad = cotangent.reshape(-1, WIDTH)

    early, _ = layer_forward(own_rows, weights, vectors)
    received = lax.ppermute(early, "section", [(0, 1)])
    rows16 = jnp.where(first_section, own_rows, received)
    result, kept = layer_forward(rows16, weights, vectors)

    early_grad, _, _ = layer_backward(own_grad, kept, weights, vectors)
    back = lax.ppermute(early_grad, "section", [(1, 0)])
    upstream = jnp.where(first_section, back, own_grad)
    rows_grad, pieces, vector_grads = layer_backward(upstream, kept, weights, vectors)
    return (
        result.reshape(1, *shape),
        rows_grad.reshape(1, *shape),
        *reduce_grads(pieces, vector_grads),
    )


def solution(mesh):
    devices = mesh.devices.reshape(2, 2, 2, 4, 4)
    fine = Mesh(devices, ("section", "far", "core", "z", "y"))
    shard = ("z", "y")
    seqs = P(None, ("far", "core", "z", "y"), None, None)
    matrix = P("section", shard, None)
    vector = P("section", shard)
    rows = P("section", None, ("far", "core", "z", "y"), None, None)
    return jax.shard_map(
        on_device,
        mesh=fine,
        in_specs=(seqs, seqs, *([matrix] * 4), *([vector] * 9)),
        out_specs=(rows, rows, *([matrix] * 4), *([vector] * 9)),
        check_vma=False,
    )
```

```python
import jax
import jax.numpy as jnp
from jax import lax
from jax.experimental import pallas as pl
from jax.experimental.pallas import tpu as pltpu
from jax.sharding import Mesh
from jax.sharding import PartitionSpec as P

HEADS = 16
HEAD_DIM = 64
LEN = 128
ROWS = 256
WIDTH = 1024
HIDDEN = 4096
BLOCK = 512
SCALE = HEAD_DIM ** (-0.5)
EPSILON = 1e-06
ROOT_HALF = 0.5**0.5
NORMAL_PEAK = 0.3989422804014327
LIMIT = 48 * 1024 * 1024

VECTORS_AT = 12288
GATHERED = 12416
O_AT, U_AT, Z_AT, HALF_ALL = 1536, 2048, 4096, 4608
DOWN_AT, EXTRA_AT, GRAD_ALL = 4096, 6144, 6272

F32 = jnp.float32
BF16 = jnp.bfloat16


def dot(left, right):
    return jnp.dot(left, right, preferred_element_type=F32)


def dot_back(left, right):
    return lax.dot_general(left, right, (((1,), (1,)), ((), ())), preferred_element_type=F32)


def dot_rows(left, right):
    return lax.dot_general(left, right, (((0,), (0,)), ((), ())), preferred_element_type=F32)


def swap_cores(value):
    return lax.ppermute(value, "core", [(0, 1), (1, 0)])


def swap_far(value):
    return lax.ppermute(value, "far", [(0, 1), (1, 0)])


def mean(values):
    return jnp.mean(values, -1, keepdims=True)


def normalise(totals):
    centred = totals - mean(totals)
    inverse = lax.rsqrt(mean(centred * centred) + EPSILON)
    return centred * inverse, inverse


def norm_backward(upstream, normed, inverse, gain_row):
    scaled = upstream * gain_row
    return inverse * (scaled - mean(scaled) - normed * mean(scaled * normed))


def soft_of(queries, keys):
    scores = dot_back(queries, keys) * SCALE
    weights = jnp.exp(scores - jnp.max(scores, -1, keepdims=True))
    return weights / jnp.sum(weights, -1, keepdims=True)


def down_rows(block):
    return jnp.concatenate(
        [
            block[32 * part : 32 * part + 32, WIDTH * group : WIDTH * (group + 1)]
            for part in range(4)
            for group in range(4)
        ],
        0,
    )


def forward_kernel(
    x_ref, column_ref, row_ref, bias_ref, pairs_ref,
    y_ref, p_ref, c_ref, hidden_ref, e_ref, slope_ref, n_one_ref, r_one_ref, n_two_ref, r_two_ref,
    total_ref,
):
    step = pl.program_id(0)

    @pl.when(step < 6)
    def _():
        at = pl.multiple_of(step * BLOCK, BLOCK)
        p_ref[:, pl.ds(at, BLOCK)] = (dot(x_ref[...], column_ref[...]) + bias_ref[...]).astype(BF16)

    @pl.when(step == 5)
    def _():
        for seq in range(ROWS // LEN):
            rows = slice(seq * LEN, (seq + 1) * LEN)
            for pair in range(HEADS // 2):
                both = []
                for head in (2 * pair, 2 * pair + 1):
                    q, k, v = (
                        p_ref[rows, part * WIDTH + head * HEAD_DIM : part * WIDTH + (head + 1) * HEAD_DIM]
                        for part in range(3)
                    )
                    both.append(dot(soft_of(q, k).astype(BF16), v))
                c_ref[rows, pair * 128 : (pair + 1) * 128] = jnp.concatenate(both, 1).astype(BF16)

    @pl.when((step >= 6) & (step < 8))
    def _():
        at = pl.multiple_of((step - 6) * BLOCK, BLOCK)
        total_ref[:, pl.ds(at, BLOCK)] = x_ref[:, pl.ds(at, BLOCK)].astype(F32) + (
            dot(c_ref[...], column_ref[...]) + bias_ref[...]
        )

    @pl.when(step == 7)
    def _():
        normed, inverse = normalise(total_ref[...])
        n_one_ref[...] = normed
        r_one_ref[...] = jnp.broadcast_to(inverse, (ROWS, 128))
        hidden = normed * pairs_ref[4:5] + pairs_ref[5:6]
        hidden_ref[...] = hidden.astype(BF16)
        total_ref[...] = hidden + pairs_ref[3:4]

    @pl.when(step >= 8)
    def _():
        upper = dot(hidden_ref[...], column_ref[...]) + bias_ref[...]
        share = 0.5 * (1.0 + lax.erf(upper * ROOT_HALF))
        active = (upper * share).astype(BF16)
        e_ref[...] = active
        slope_ref[...] = (
            share + upper * (NORMAL_PEAK * jnp.exp(-0.5 * upper * upper))
        ).astype(BF16)
        total_ref[...] += dot(active, down_rows(row_ref[...]))

    @pl.when(step == 15)
    def _():
        normed, inverse = normalise(total_ref[...])
        n_two_ref[...] = normed
        r_two_ref[...] = jnp.broadcast_to(inverse, (ROWS, 128))
        y_ref[...] = (normed * pairs_ref[6:7] + pairs_ref[7:8]).astype(BF16)


def whole(shape):
    return pl.BlockSpec(shape, lambda step: (0,) * len(shape))


def shaped(*dims, kind=BF16):
    return jax.ShapeDtypeStruct(dims, kind)


def layer_forward(rows16, gathered, biases, pairs):
    later = lambda step: (0, jnp.maximum(step - 8, 0))
    return pl.pallas_call(
        forward_kernel,
        grid=(16,),
        in_specs=[
            whole((ROWS, WIDTH)),
            pl.BlockSpec((WIDTH, BLOCK), lambda step: (0, step)),
            pl.BlockSpec((128, HIDDEN), lambda step: (jnp.maximum(step - 8, 0), 2)),
            pl.BlockSpec((1, BLOCK), lambda step: (0, step)),
            whole((8, WIDTH)),
        ],
        out_specs=[
            whole((ROWS, WIDTH)),
            whole((ROWS, 3 * WIDTH)),
            whole((ROWS, WIDTH)),
            whole((ROWS, WIDTH)),
            pl.BlockSpec((ROWS, BLOCK), later),
            pl.BlockSpec((ROWS, BLOCK), later),
            whole((ROWS, WIDTH)),
            whole((ROWS, 128)),
            whole((ROWS, WIDTH)),
            whole((ROWS, 128)),
        ],
        out_shape=[
            shaped(ROWS, WIDTH),
            shaped(ROWS, 3 * WIDTH),
            shaped(ROWS, WIDTH),
            shaped(ROWS, WIDTH),
            shaped(ROWS, HIDDEN),
            shaped(ROWS, HIDDEN),
            shaped(ROWS, WIDTH, kind=F32),
            shaped(ROWS, 128, kind=F32),
            shaped(ROWS, WIDTH, kind=F32),
            shaped(ROWS, 128, kind=F32),
        ],
        scratch_shapes=[pltpu.VMEM((ROWS, WIDTH), F32)],
        compiler_params=pltpu.CompilerParams(vmem_limit_bytes=LIMIT),
        cost_estimate=pl.CostEstimate(
            flops=2 * ROWS * 12 * WIDTH * WIDTH, bytes_accessed=32 << 20, transcendentals=0
        ),
        name="layer_forward",
    )(rows16, gathered, gathered, biases, pairs)


def backward_kernel(
    upstream_ref, column_ref, row_ref, pairs_ref, p_ref, slope_ref,
    n_one_ref, r_one_ref, n_two_ref, r_two_ref,
    x_grad_ref, halves_ref, pair_grads_ref, up_grads_ref,
    z_ref, o_ref, p_grad_ref, branch_ref, total_ref,
):
    step = pl.program_id(0)

    def column_sums(values):
        return jnp.sum(values, 0, keepdims=True)

    @pl.when(step == 0)
    def _():
        upstream = upstream_ref[...].astype(F32)
        normed = n_two_ref[...]
        pair_grads_ref[6:7] = column_sums(upstream * normed)
        pair_grads_ref[7:8] = column_sums(upstream)
        grad = norm_backward(upstream, normed, r_two_ref[:, 0:1], pairs_ref[6:7])
        total_ref[...] = grad
        rounded = grad.astype(BF16)
        z_ref[...] = rounded
        pair_grads_ref[3:4] = column_sums(rounded.astype(F32))
        halves_ref[0, :, Z_AT:] = rounded[:, :512]
        halves_ref[1, :, Z_AT:] = rounded[:, 512:]

    @pl.when(step < 8)
    def _():
        active_grad = dot_back(z_ref[...], down_rows(row_ref[...]))
        upper_grad = (active_grad * slope_ref[...].astype(F32)).astype(BF16)
        up_grads_ref[...] = column_sums(upper_grad.astype(F32))
        at = pl.multiple_of(U_AT + lax.rem(step, 4) * BLOCK, BLOCK)
        halves_ref[step // 4, :, pl.ds(at, BLOCK)] = upper_grad
        total_ref[...] += dot_back(upper_grad, column_ref[...])

    @pl.when(step == 7)
    def _():
        hidden_grad = total_ref[...]
        normed = n_one_ref[...]
        pair_grads_ref[4:5] = column_sums(hidden_grad * normed)
        pair_grads_ref[5:6] = column_sums(hidden_grad)
        grad = norm_backward(hidden_grad, normed, r_one_ref[:, 0:1], pairs_ref[4:5])
        branch_ref[...] = grad
        rounded = grad.astype(BF16)
        o_ref[...] = rounded
        pair_grads_ref[2:3] = column_sums(rounded.astype(F32))
        halves_ref[0, :, O_AT:U_AT] = rounded[:, :512]
        halves_ref[1, :, O_AT:U_AT] = rounded[:, 512:]

    @pl.when(step == 8)
    def _():
        total_ref[...] = dot_back(o_ref[:, :BLOCK], column_ref[...])

    @pl.when(step == 9)
    def _():
        attended_grad = (total_ref[...] + dot_back(o_ref[:, BLOCK:], column_ref[...])).astype(BF16)
        z_ref[...] = attended_grad
        for seq in range(ROWS // LEN):
            rows = slice(seq * LEN, (seq + 1) * LEN)
            for pair in range(HEADS // 2):
                both = []
                for head in (2 * pair, 2 * pair + 1):
                    lanes = slice(head * HEAD_DIM, (head + 1) * HEAD_DIM)
                    q, k, v = (
                        p_ref[rows, part * WIDTH + head * HEAD_DIM : part * WIDTH + (head + 1) * HEAD_DIM]
                        for part in range(3)
                    )
                    grad = z_ref[rows, lanes]
                    soft = soft_of(q, k)
                    value_grad = dot_rows(soft.astype(BF16), grad)
                    soft_grad = dot_back(grad, v)
                    weighed = soft_grad * soft
                    scores_grad = (
                        weighed - soft * jnp.sum(weighed, -1, keepdims=True)
                    ).astype(BF16)
                    both.append(
                        (
                            dot(scores_grad, k) * SCALE,
                            dot_rows(scores_grad, q) * SCALE,
                            value_grad,
                        )
                    )
                for part in range(3):
                    p_grad_ref[
                        rows, part * WIDTH + pair * 128 : part * WIDTH + (pair + 1) * 128
                    ] = jnp.concatenate([both[0][part], both[1][part]], 1).astype(BF16)
        halves_ref[0, :, :O_AT] = p_grad_ref[:, :O_AT]
        halves_ref[1, :, :O_AT] = p_grad_ref[:, O_AT:]
        pair_grads_ref[0:1] = column_sums(p_grad_ref[:, :WIDTH].astype(F32))
        pair_grads_ref[1:2] = column_sums(p_grad_ref[:, 2 * WIDTH :].astype(F32))
        total_ref[...] = branch_ref[...]

    @pl.when(step >= 10)
    def _():
        at = pl.multiple_of((step - 10) * BLOCK, BLOCK)
        total_ref[...] += dot_back(p_grad_ref[:, pl.ds(at, BLOCK)], column_ref[...])

    @pl.when(step == 15)
    def _():
        x_grad_ref[...] = total_ref[...].astype(BF16)


def layer_backward(upstream, gathered, pairs, kept):
    p, slope, n_one, r_one, n_two, r_two = kept
    early = lambda step: (0, jnp.minimum(step, 7))
    column = lambda step: (0, jnp.where(step < 8, step + 8, jnp.where(step < 10, step - 2, step - 10)))
    return pl.pallas_call(
        backward_kernel,
        grid=(16,),
        in_specs=[
            whole((ROWS, WIDTH)),
            pl.BlockSpec((WIDTH, BLOCK), column),
            pl.BlockSpec((128, HIDDEN), lambda step: (jnp.minimum(step, 7), 2)),
            whole((8, WIDTH)),
            whole((ROWS, 3 * WIDTH)),
            pl.BlockSpec((ROWS, BLOCK), early),
            whole((ROWS, WIDTH)),
            whole((ROWS, 128)),
            whole((ROWS, WIDTH)),
            whole((ROWS, 128)),
        ],
        out_specs=[
            whole((ROWS, WIDTH)),
            whole((2, ROWS, HALF_ALL)),
            whole((8, WIDTH)),
            pl.BlockSpec((1, BLOCK), early),
        ],
        out_shape=[
            shaped(ROWS, WIDTH),
            shaped(2, ROWS, HALF_ALL),
            shaped(8, WIDTH, kind=F32),
            shaped(1, HIDDEN, kind=F32),
        ],
        scratch_shapes=[
            pltpu.VMEM((ROWS, WIDTH), BF16),
            pltpu.VMEM((ROWS, WIDTH), BF16),
            pltpu.VMEM((ROWS, 3 * WIDTH), BF16),
            pltpu.VMEM((ROWS, WIDTH), F32),
            pltpu.VMEM((ROWS, WIDTH), F32),
        ],
        compiler_params=pltpu.CompilerParams(vmem_limit_bytes=LIMIT),
        cost_estimate=pl.CostEstimate(
            flops=2 * ROWS * 12 * WIDTH * WIDTH, bytes_accessed=32 << 20, transcendentals=0
        ),
        name="layer_backward",
    )(upstream, gathered, gathered, pairs, p, slope, n_one, r_one, n_two, r_two)


def weight_grads_kernel(x_ref, c_ref, h_ref, e_ref, lefts_ref, x2_ref, c2_ref, h2_ref, e2_ref, rights_ref, extra_ref, out_ref):
    def product(one_ref, two_ref, at, end):
        return (
            dot_rows(one_ref[...], lefts_ref[:, at:end])
            + dot_rows(two_ref[...], rights_ref[:, at:end])
        ).astype(BF16)

    out_ref[:, :O_AT] = product(x_ref, x2_ref, 0, O_AT)
    out_ref[:, O_AT:U_AT] = product(c_ref, c2_ref, O_AT, U_AT)
    out_ref[:, U_AT:Z_AT] = product(h_ref, h2_ref, U_AT, Z_AT)
    down = product(e_ref, e2_ref, Z_AT, HALF_ALL)
    for part in range(4):
        for group in range(4):
            at = part * 256 + group * 64
            out_ref[
                part * 64 : part * 64 + 64, DOWN_AT + group * 512 : DOWN_AT + (group + 1) * 512
            ] = down[at : at + 64]
    out_ref[:, EXTRA_AT:] = extra_ref[...]


def weight_grads(own, own_half, other, other_half, extra):
    narrow = pl.BlockSpec((ROWS, 256), lambda step: (0, step))
    wide = pl.BlockSpec((ROWS, 1024), lambda step: (0, step))
    tokens = [narrow, narrow, narrow, wide, whole((ROWS, HALF_ALL))]
    return pl.pallas_call(
        weight_grads_kernel,
        grid=(4,),
        in_specs=[*tokens, *tokens, pl.BlockSpec((256, 128), lambda step: (step, 0))],
        out_specs=pl.BlockSpec((256, GRAD_ALL), lambda step: (step, 0)),
        out_shape=shaped(WIDTH, GRAD_ALL),
        compiler_params=pltpu.CompilerParams(vmem_limit_bytes=LIMIT),
        cost_estimate=pl.CostEstimate(
            flops=2 * ROWS * 12 * WIDTH * WIDTH, bytes_accessed=24 << 20, transcendentals=0
        ),
        name="weight_grads",
    )(*own, own_half, *other, other_half, extra)


def finish_kernel(low_ref, high_ref, project_ref, output_ref, up_ref, down_ref):
    for half, ref in enumerate((low_ref, high_ref)):
        project_ref[:, half * 1536 : (half + 1) * 1536] = ref[:, :O_AT]
        output_ref[:, half * 512 : (half + 1) * 512] = ref[:, O_AT:U_AT]
        up_ref[:, half * 2048 : (half + 1) * 2048] = ref[:, U_AT:Z_AT]
        for group in range(4):
            at = DOWN_AT + group * 512
            down_ref[group * 64 : group * 64 + 64, half * 512 : (half + 1) * 512] = ref[
                :, at : at + 512
            ]


def finish(low, high):
    return pl.pallas_call(
        finish_kernel,
        out_shape=[
            shaped(64, 3 * WIDTH, kind=F32),
            shaped(64, WIDTH, kind=F32),
            shaped(64, HIDDEN, kind=F32),
            shaped(256, WIDTH, kind=F32),
        ],
        compiler_params=pltpu.CompilerParams(vmem_limit_bytes=LIMIT),
        name="finish",
    )(low, high)


def gather_weights(project, output, upward, downward, vectors):
    core = lax.axis_index("core")
    half = lax.dynamic_slice_in_dim(
        jnp.concatenate([project, output, upward], 1), core * 32, 32, 0
    )
    down = lax.dynamic_slice_in_dim(downward, core * 128, 128, 0)
    down = down.reshape(4, 32, WIDTH).transpose(1, 0, 2).reshape(32, HIDDEN)
    flat = jnp.concatenate(vectors).reshape(6, 128)
    extra = jnp.concatenate([flat, jnp.zeros((26, 128), BF16)], 0)
    packed = jnp.concatenate([half, down, extra], 1)
    gathered = lax.all_gather(packed, ("z", "y", "core"), axis=0, tiled=True)
    rows = gathered[:, VECTORS_AT:].reshape(16, 64, 128)[:, :6].astype(F32)
    pairs = rows[:, :4].reshape(16, 8, 64).transpose(1, 0, 2).reshape(8, WIDTH)
    ups = rows[:, 4:].reshape(1, HIDDEN)
    biases = jnp.concatenate(
        [pairs[0:1], jnp.zeros((1, WIDTH), F32), pairs[1:2], pairs[2:3], ups], 1
    )
    return gathered, biases, pairs


def reduce_grads(own, halves, other, pair_grads, up_grads):
    core = lax.axis_index("core")
    other_half = swap_cores(lax.dynamic_index_in_dim(halves, 1 - core, 0, keepdims=False))
    own_half = lax.dynamic_index_in_dim(halves, core, 0, keepdims=False)
    rows = jnp.concatenate(
        [
            pair_grads.reshape(8, 16, 64).transpose(1, 0, 2).reshape(16, 4, 128),
            up_grads.reshape(16, 2, 128),
        ],
        1,
    ).astype(BF16)
    extra = jnp.concatenate([rows, jnp.zeros((16, 58, 128), BF16)], 1).reshape(WIDTH, 128)
    packed = weight_grads(own, own_half, other, other_half, extra)
    owned = lax.psum_scatter(packed, ("z", "y"), scatter_dimension=0, tiled=True)
    owned = lax.optimization_barrier(owned)
    total = owned.astype(F32) + swap_far(owned).astype(F32)
    total = lax.optimization_barrier(total)
    sibling = swap_cores(total)
    low = jnp.where(core == 0, total, sibling)
    high = jnp.where(core == 0, sibling, total)
    project, output, upward, downward = finish(low, high)
    vectors = (total[:6, EXTRA_AT:] + sibling[:6, EXTRA_AT:]).reshape(768)
    narrow = [vectors[64 * k : 64 * (k + 1)][None] for k in range(8)]
    query, value, output_b, down_b, gain_one, shift_one, gain_two, shift_two = narrow
    return (
        project[None],
        output[None],
        upward[None],
        downward[None],
        query,
        value,
        output_b,
        vectors[512:768][None],
        down_b,
        gain_one,
        shift_one,
        gain_two,
        shift_two,
    )


def on_device(
    layer_input,
    cotangent,
    project_weight,
    output_weight,
    up_weight,
    down_weight,
    query_bias,
    value_bias,
    output_bias,
    up_bias,
    down_bias,
    first_gain,
    first_shift,
    second_gain,
    second_shift,
):
    first_section = lax.axis_index("section") == 0
    gathered, biases, pairs = gather_weights(
        project_weight[0],
        output_weight[0],
        up_weight[0],
        down_weight[0],
        (
            query_bias[0],
            value_bias[0],
            output_bias[0],
            down_bias[0],
            first_gain[0],
            first_shift[0],
            second_gain[0],
            second_shift[0],
            up_bias[0],
        ),
    )
    shape = layer_input.shape
    own_rows = layer_input.reshape(-1, WIDTH)
    own_grad = cotangent.reshape(-1, WIDTH)

    early = layer_forward(own_rows, gathered, biases, pairs)[0]
    received = lax.ppermute(early, "section", [(0, 1)])
    rows16 = jnp.where(first_section, own_rows, received)
    result, p, c, hidden, e, slope, n_one, r_one, n_two, r_two = layer_forward(
        rows16, gathered, biases, pairs
    )
    kept = (p, slope, n_one, r_one, n_two, r_two)
    own = (rows16, c, hidden, e)
    other = tuple(swap_cores(array) for array in own)

    early_grad = layer_backward(own_grad, gathered, pairs, kept)[0]
    back = lax.ppermute(early_grad, "section", [(1, 0)])
    upstream = jnp.where(first_section, back, own_grad)
    rows_grad, halves, pair_grads, up_grads = layer_backward(upstream, gathered, pairs, kept)
    return (
        result.reshape(1, *shape),
        rows_grad.reshape(1, *shape),
        *reduce_grads(own, halves, other, pair_grads, up_grads),
    )


def solution(mesh):
    devices = mesh.devices.reshape(2, 2, 2, 4, 4)
    fine = Mesh(devices, ("section", "far", "core", "z", "y"))
    shard = ("z", "y")
    seqs = P(None, ("far", "core", "z", "y"), None, None)
    matrix = P("section", shard, None)
    vector = P("section", shard)
    rows = P("section", None, ("far", "core", "z", "y"), None, None)
    return jax.shard_map(
        on_device,
        mesh=fine,
        in_specs=(seqs, seqs, *([matrix] * 4), *([vector] * 9)),
        out_specs=(rows, rows, *([matrix] * 4), *([vector] * 9)),
        check_vma=False,
    )
```

```python
import functools

import jax
import jax.numpy as jnp
from jax import lax
from jax.experimental import pallas as pl
from jax.experimental.pallas import tpu as pltpu
from jax.sharding import Mesh
from jax.sharding import PartitionSpec as P

HEADS = 16
HEAD_DIM = 64
LEN = 128
ROWS = 256
WIDTH = 1024
HIDDEN = 4096
BLOCK = 1024
SCALE = HEAD_DIM ** (-0.5)
EPSILON = 1e-06
ROOT_HALF = 0.5**0.5
NORMAL_PEAK = 0.3989422804014327
LIMIT = 48 * 1024 * 1024

VECTORS_AT = 12288
GATHERED = 12416
Z_AT, HIDDEN_HALF = 2048, 2560
O_AT, ATTENTION_HALF = 1536, 2048
DOWN_AT, HIDDEN_ALL = 2048, 4096
EXTRA_AT, ATTENTION_ALL, CUT = 2048, 2176, 1024

F32 = jnp.float32
BF16 = jnp.bfloat16


def dot(left, right):
    return jnp.dot(left, right, preferred_element_type=F32)


def dot_back(left, right):
    return lax.dot_general(left, right, (((1,), (1,)), ((), ())), preferred_element_type=F32)


def dot_rows(left, right):
    return lax.dot_general(left, right, (((0,), (0,)), ((), ())), preferred_element_type=F32)


def swap_cores(value):
    return lax.ppermute(value, "core", [(0, 1), (1, 0)])


def swap_far(value):
    return lax.ppermute(value, "far", [(0, 1), (1, 0)])


def mean(values):
    return jnp.mean(values, -1, keepdims=True)


def normalise(totals):
    centred = totals - mean(totals)
    inverse = lax.rsqrt(mean(centred * centred) + EPSILON)
    return centred * inverse, inverse


def norm_backward(upstream, normed, inverse, gain_row):
    scaled = upstream * gain_row
    return inverse * (scaled - mean(scaled) - normed * mean(scaled * normed))


def stacked(values):
    low = lax.broadcasted_iota(jnp.int32, values.shape, 1) < HEAD_DIM
    zeros = jnp.zeros_like(values)
    return jnp.concatenate([jnp.where(low, values, zeros), jnp.where(low, zeros, values)], 0)


def beside(values):
    low = lax.broadcasted_iota(jnp.int32, (LEN, 128), 1) < HEAD_DIM
    return jnp.where(low, values[:LEN], values[LEN:])


def soft_of(queries, keys):
    scores = dot_back(queries, keys)
    weights = jnp.exp((scores - jnp.max(scores, -1, keepdims=True)) * SCALE)
    return weights * (1.0 / jnp.sum(weights, -1, keepdims=True))


def pair_of(ref, rows, part, pair):
    at = part * WIDTH + pair * 128
    return ref[rows, at : at + 128]


def down_rows(block):
    return jnp.concatenate(
        [
            block[32 * part : 32 * part + 32, WIDTH * group : WIDTH * (group + 1)]
            for part in range(8)
            for group in range(4)
        ],
        0,
    )


def forward_kernel(keep, x_ref, column_ref, row_ref, bias_ref, pairs_ref, y_ref, p_ref, c_ref, hidden_ref, *others):
    step = pl.program_id(0)
    total_ref = others[-1]
    if keep:
        e_ref, slope_ref, n_one_ref, r_one_ref, n_two_ref, r_two_ref = others[:-1]

    @pl.when(step < 3)
    def _():
        at = pl.multiple_of(step * BLOCK, BLOCK)
        p_ref[:, pl.ds(at, BLOCK)] = (dot(x_ref[...], column_ref[...]) + bias_ref[...]).astype(BF16)

    @pl.when(step == 3)
    def _():
        for seq in range(ROWS // LEN):
            rows = slice(seq * LEN, (seq + 1) * LEN)
            for pair in range(HEADS // 2):
                q, k, v = (pair_of(p_ref, rows, part, pair) for part in range(3))
                soft = soft_of(stacked(q), k).astype(BF16)
                c_ref[rows, pair * 128 : (pair + 1) * 128] = beside(dot(soft, v)).astype(BF16)
        normed, inverse = normalise(
            x_ref[...].astype(F32) + (dot(c_ref[...], column_ref[...]) + bias_ref[...])
        )
        hidden = normed * pairs_ref[4:5] + pairs_ref[5:6]
        hidden_ref[...] = hidden.astype(BF16)
        total_ref[...] = hidden + pairs_ref[3:4]
        if keep:
            n_one_ref[...] = normed
            r_one_ref[...] = jnp.broadcast_to(inverse, (ROWS, 128))

    @pl.when(step >= 4)
    def _():
        upper = dot(hidden_ref[...], column_ref[...]) + bias_ref[...]
        share = 0.5 * (1.0 + lax.erf(upper * ROOT_HALF))
        active = (upper * share).astype(BF16)
        if keep:
            e_ref[...] = active
            slope_ref[...] = (
                share + upper * (NORMAL_PEAK * jnp.exp(-0.5 * upper * upper))
            ).astype(BF16)
        total_ref[...] += dot(active, down_rows(row_ref[...]))

    @pl.when(step == 7)
    def _():
        normed, inverse = normalise(total_ref[...])
        y_ref[...] = (normed * pairs_ref[6:7] + pairs_ref[7:8]).astype(BF16)
        if keep:
            n_two_ref[...] = normed
            r_two_ref[...] = jnp.broadcast_to(inverse, (ROWS, 128))


def whole(shape):
    return pl.BlockSpec(shape, lambda step: (0,) * len(shape))


def shaped(*dims, kind=BF16):
    return jax.ShapeDtypeStruct(dims, kind)


def layer_forward(rows16, gathered, biases, pairs, keep):
    later = lambda step: (0, jnp.maximum(step - 4, 0))
    results = [
        (whole((ROWS, WIDTH)), shaped(ROWS, WIDTH)),
        (whole((ROWS, 3 * WIDTH)), shaped(ROWS, 3 * WIDTH)),
        (whole((ROWS, WIDTH)), shaped(ROWS, WIDTH)),
        (whole((ROWS, WIDTH)), shaped(ROWS, WIDTH)),
    ]
    scratch = [pltpu.VMEM((ROWS, WIDTH), F32)]
    if keep:
        results += [
            (pl.BlockSpec((ROWS, BLOCK), later), shaped(ROWS, HIDDEN)),
            (pl.BlockSpec((ROWS, BLOCK), later), shaped(ROWS, HIDDEN)),
            (whole((ROWS, WIDTH)), shaped(ROWS, WIDTH, kind=F32)),
            (whole((ROWS, 128)), shaped(ROWS, 128, kind=F32)),
            (whole((ROWS, WIDTH)), shaped(ROWS, WIDTH, kind=F32)),
            (whole((ROWS, 128)), shaped(ROWS, 128, kind=F32)),
        ]
    else:
        scratch = [pltpu.VMEM(shape.shape, BF16) for _, shape in results[1:]] + scratch
        results = results[:1]
    return pl.pallas_call(
        functools.partial(forward_kernel, keep),
        grid=(8,),
        in_specs=[
            whole((ROWS, WIDTH)),
            pl.BlockSpec((WIDTH, BLOCK), lambda step: (0, step)),
            pl.BlockSpec((256, HIDDEN), lambda step: (jnp.maximum(step - 4, 0), 2)),
            pl.BlockSpec((1, BLOCK), lambda step: (0, step)),
            whole((8, WIDTH)),
        ],
        out_specs=[spec for spec, _ in results],
        out_shape=[shape for _, shape in results],
        scratch_shapes=scratch,
        compiler_params=pltpu.CompilerParams(vmem_limit_bytes=LIMIT),
        cost_estimate=pl.CostEstimate(
            flops=2 * ROWS * 12 * WIDTH * WIDTH, bytes_accessed=32 << 20, transcendentals=0
        ),
        name="layer_forward",
    )(rows16, gathered, gathered, biases, pairs)


def column_sums(values):
    return jnp.sum(values, 0, keepdims=True)


def put_half(core, half, mine_ref, theirs_ref, columns, values):
    @pl.when(core == half)
    def _():
        mine_ref[:, columns] = values

    @pl.when(core != half)
    def _():
        theirs_ref[:, columns] = values


def hidden_begin(keep, core, upstream_ref, pairs_ref, n_two_ref, r_two_ref, z_ref, total_ref, kept):
    upstream = upstream_ref[...].astype(F32)
    normed = n_two_ref[...]
    grad = norm_backward(upstream, normed, r_two_ref[:, 0:1], pairs_ref[6:7])
    total_ref[...] = grad
    rounded = grad.astype(BF16)
    z_ref[...] = rounded
    if keep:
        mine_ref, theirs_ref, pair_grads_ref, _ = kept
        pair_grads_ref[6:7] = column_sums(upstream * normed)
        pair_grads_ref[7:8] = column_sums(upstream)
        pair_grads_ref[3:4] = column_sums(rounded.astype(F32))
        for half in range(2):
            put_half(
                core, half, mine_ref, theirs_ref, pl.ds(Z_AT, 512),
                rounded[:, half * 512 : half * 512 + 512],
            )


def hidden_step(keep, core, step, column_ref, row_ref, slope_ref, z_ref, total_ref, kept):
    active_grad = dot_back(z_ref[...], down_rows(row_ref[...]))
    upper_grad = (active_grad * slope_ref[...].astype(F32)).astype(BF16)
    if keep:
        mine_ref, theirs_ref, _, up_grads_ref = kept
        up_grads_ref[...] = column_sums(upper_grad.astype(F32))
        at = pl.multiple_of(lax.rem(step, 2) * BLOCK, BLOCK)
        put_half(core, step // 2, mine_ref, theirs_ref, pl.ds(at, BLOCK), upper_grad)
    total_ref[...] += dot_back(upper_grad, column_ref[...])


def hidden_end(keep, pairs_ref, n_one_ref, r_one_ref, total_ref, kept):
    hidden_grad = total_ref[...]
    normed = n_one_ref[...]
    grad = norm_backward(hidden_grad, normed, r_one_ref[:, 0:1], pairs_ref[4:5])
    if keep:
        pair_grads_ref = kept[2]
        pair_grads_ref[4:5] = column_sums(hidden_grad * normed)
        pair_grads_ref[5:6] = column_sums(hidden_grad)
    return grad


def attention_step(keep, core, grad, column_ref, p_ref, z_ref, p_grad_ref, total_ref, kept):
    rounded = grad.astype(BF16)
    z_ref[...] = dot_back(rounded, column_ref[...]).astype(BF16)
    for seq in range(ROWS // LEN):
        rows = slice(seq * LEN, (seq + 1) * LEN)
        for pair in range(HEADS // 2):
            q, k, v = (pair_of(p_ref, rows, part, pair) for part in range(3))
            q_two = stacked(q)
            grad_two = stacked(pair_of(z_ref, rows, 0, pair))
            soft = soft_of(q_two, k)
            soft_grad = dot_back(grad_two, v)
            weighed = soft_grad * soft
            scores_grad = (weighed - soft * jnp.sum(weighed, -1, keepdims=True)).astype(BF16)
            grads = (
                beside(dot(scores_grad, k)) * SCALE,
                dot_rows(scores_grad, q_two) * SCALE,
                dot_rows(soft.astype(BF16), grad_two),
            )
            for part in range(3):
                at = part * WIDTH + pair * 128
                p_grad_ref[rows, at : at + 128] = grads[part].astype(BF16)
    if keep:
        mine_ref, theirs_ref, pair_grads_ref = kept
        for half in range(2):
            put_half(
                core, half, mine_ref, theirs_ref, pl.ds(0, O_AT),
                p_grad_ref[:, half * O_AT : (half + 1) * O_AT],
            )
            put_half(
                core, half, mine_ref, theirs_ref, pl.ds(O_AT, 512),
                rounded[:, half * 512 : half * 512 + 512],
            )
        pair_grads_ref[0:1] = column_sums(p_grad_ref[:, :WIDTH].astype(F32))
        pair_grads_ref[1:2] = column_sums(p_grad_ref[:, 2 * WIDTH :].astype(F32))
        pair_grads_ref[2:3] = column_sums(rounded.astype(F32))
    total_ref[...] = grad


def project_step(step, column_ref, p_grad_ref, total_ref):
    at = pl.multiple_of(step * BLOCK, BLOCK)
    total_ref[...] += dot_back(p_grad_ref[:, pl.ds(at, BLOCK)], column_ref[...])


def through_kernel(
    upstream_ref, column_ref, row_ref, pairs_ref, p_ref, slope_ref,
    n_one_ref, r_one_ref, n_two_ref, r_two_ref, x_grad_ref, z_ref, p_grad_ref, total_ref
):
    step = pl.program_id(0)

    @pl.when(step == 0)
    def _():
        hidden_begin(False, None, upstream_ref, pairs_ref, n_two_ref, r_two_ref, z_ref, total_ref, None)

    @pl.when(step < 4)
    def _():
        hidden_step(False, None, step, column_ref, row_ref, slope_ref, z_ref, total_ref, None)

    @pl.when(step == 4)
    def _():
        grad = hidden_end(False, pairs_ref, n_one_ref, r_one_ref, total_ref, None)
        attention_step(False, None, grad, column_ref, p_ref, z_ref, p_grad_ref, total_ref, None)

    @pl.when(step >= 5)
    def _():
        project_step(step - 5, column_ref, p_grad_ref, total_ref)

    @pl.when(step == 7)
    def _():
        x_grad_ref[...] = total_ref[...].astype(BF16)


def cost(share):
    return pl.CostEstimate(
        flops=int(2 * ROWS * 12 * WIDTH * WIDTH * share),
        bytes_accessed=int(share * (32 << 20)),
        transcendentals=0,
    )


def layer_through(upstream, gathered, pairs, kept):
    p, slope, n_one, r_one, n_two, r_two = kept
    column = lambda step: (0, jnp.where(step < 4, step + 4, jnp.where(step < 5, 3, step - 5)))
    return pl.pallas_call(
        through_kernel,
        grid=(8,),
        in_specs=[
            whole((ROWS, WIDTH)),
            pl.BlockSpec((WIDTH, BLOCK), column),
            pl.BlockSpec((256, HIDDEN), lambda step: (jnp.minimum(step, 3), 2)),
            whole((8, WIDTH)),
            whole((ROWS, 3 * WIDTH)),
            pl.BlockSpec((ROWS, BLOCK), lambda step: (0, jnp.minimum(step, 3))),
            whole((ROWS, WIDTH)),
            whole((ROWS, 128)),
            whole((ROWS, WIDTH)),
            whole((ROWS, 128)),
        ],
        out_specs=whole((ROWS, WIDTH)),
        out_shape=shaped(ROWS, WIDTH),
        scratch_shapes=[
            pltpu.VMEM((ROWS, WIDTH), BF16),
            pltpu.VMEM((ROWS, 3 * WIDTH), BF16),
            pltpu.VMEM((ROWS, WIDTH), F32),
        ],
        compiler_params=pltpu.CompilerParams(vmem_limit_bytes=LIMIT),
        cost_estimate=cost(1.0),
        name="layer_through",
    )(upstream, gathered, gathered, pairs, p, slope, n_one, r_one, n_two, r_two)


def hidden_kernel(
    core_ref, upstream_ref, column_ref, row_ref, pairs_ref, slope_ref,
    n_one_ref, r_one_ref, n_two_ref, r_two_ref,
    branch_ref, mine_ref, theirs_ref, pair_grads_ref, up_grads_ref, z_ref, total_ref
):
    step = pl.program_id(0)
    core = core_ref[0]
    kept = (mine_ref, theirs_ref, pair_grads_ref, up_grads_ref)

    @pl.when(step == 0)
    def _():
        pair_grads_ref[...] = jnp.zeros_like(pair_grads_ref)
        hidden_begin(True, core, upstream_ref, pairs_ref, n_two_ref, r_two_ref, z_ref, total_ref, kept)

    hidden_step(True, core, step, column_ref, row_ref, slope_ref, z_ref, total_ref, kept)

    @pl.when(step == 3)
    def _():
        branch_ref[...] = hidden_end(True, pairs_ref, n_one_ref, r_one_ref, total_ref, kept)


def hidden_backward(core, upstream, gathered, pairs, kept):
    _, slope, n_one, r_one, n_two, r_two = kept
    return pl.pallas_call(
        hidden_kernel,
        grid=(4,),
        in_specs=[
            pl.BlockSpec(memory_space=pltpu.SMEM),
            whole((ROWS, WIDTH)),
            pl.BlockSpec((WIDTH, BLOCK), lambda step: (0, step + 4)),
            pl.BlockSpec((256, HIDDEN), lambda step: (step, 2)),
            whole((8, WIDTH)),
            pl.BlockSpec((ROWS, BLOCK), lambda step: (0, step)),
            whole((ROWS, WIDTH)),
            whole((ROWS, 128)),
            whole((ROWS, WIDTH)),
            whole((ROWS, 128)),
        ],
        out_specs=[
            whole((ROWS, WIDTH)),
            whole((ROWS, HIDDEN_HALF)),
            whole((ROWS, HIDDEN_HALF)),
            whole((8, WIDTH)),
            pl.BlockSpec((1, BLOCK), lambda step: (0, step)),
        ],
        out_shape=[
            shaped(ROWS, WIDTH, kind=F32),
            shaped(ROWS, HIDDEN_HALF),
            shaped(ROWS, HIDDEN_HALF),
            shaped(8, WIDTH, kind=F32),
            shaped(1, HIDDEN, kind=F32),
        ],
        scratch_shapes=[pltpu.VMEM((ROWS, WIDTH), BF16), pltpu.VMEM((ROWS, WIDTH), F32)],
        compiler_params=pltpu.CompilerParams(vmem_limit_bytes=LIMIT),
        cost_estimate=cost(0.6),
        name="hidden_backward",
    )(core, upstream, gathered, gathered, pairs, slope, n_one, r_one, n_two, r_two)


def attention_kernel(
    core_ref, branch_ref, column_ref, p_ref,
    x_grad_ref, mine_ref, theirs_ref, pair_grads_ref, z_ref, p_grad_ref, total_ref
):
    step = pl.program_id(0)
    kept = (mine_ref, theirs_ref, pair_grads_ref)

    @pl.when(step == 0)
    def _():
        pair_grads_ref[...] = jnp.zeros_like(pair_grads_ref)
        attention_step(
            True, core_ref[0], branch_ref[...], column_ref, p_ref, z_ref, p_grad_ref, total_ref, kept
        )

    @pl.when(step >= 1)
    def _():
        project_step(step - 1, column_ref, p_grad_ref, total_ref)

    @pl.when(step == 3)
    def _():
        x_grad_ref[...] = total_ref[...].astype(BF16)


def attention_backward(core, branch, gathered, p):
    return pl.pallas_call(
        attention_kernel,
        grid=(4,),
        in_specs=[
            pl.BlockSpec(memory_space=pltpu.SMEM),
            whole((ROWS, WIDTH)),
            pl.BlockSpec((WIDTH, BLOCK), lambda step: (0, jnp.where(step < 1, 3, step - 1))),
            whole((ROWS, 3 * WIDTH)),
        ],
        out_specs=[
            whole((ROWS, WIDTH)),
            whole((ROWS, ATTENTION_HALF)),
            whole((ROWS, ATTENTION_HALF)),
            whole((8, WIDTH)),
        ],
        out_shape=[
            shaped(ROWS, WIDTH),
            shaped(ROWS, ATTENTION_HALF),
            shaped(ROWS, ATTENTION_HALF),
            shaped(8, WIDTH, kind=F32),
        ],
        scratch_shapes=[
            pltpu.VMEM((ROWS, WIDTH), BF16),
            pltpu.VMEM((ROWS, 3 * WIDTH), BF16),
            pltpu.VMEM((ROWS, WIDTH), F32),
        ],
        compiler_params=pltpu.CompilerParams(vmem_limit_bytes=LIMIT),
        cost_estimate=cost(0.5),
        name="attention_backward",
    )(core, branch, gathered, p)


def product(left_refs, right_refs, at, end):
    return (
        dot_rows(left_refs[0][...], right_refs[0][:, at:end])
        + dot_rows(left_refs[1][...], right_refs[1][:, at:end])
    ).astype(BF16)


def hidden_grads_kernel(h_ref, e_ref, left_ref, h2_ref, e2_ref, right_ref, out_ref):
    both = (left_ref, right_ref)
    out_ref[:, :DOWN_AT] = product((h_ref, h2_ref), both, 0, Z_AT)
    down = product((e_ref, e2_ref), both, Z_AT, HIDDEN_HALF)
    for part in range(4):
        for group in range(4):
            at = part * 256 + group * 64
            out_ref[
                part * 64 : part * 64 + 64, DOWN_AT + group * 512 : DOWN_AT + (group + 1) * 512
            ] = down[at : at + 64]


def attention_grads_kernel(x_ref, c_ref, left_ref, x2_ref, c2_ref, right_ref, extra_ref, out_ref):
    both = (left_ref, right_ref)
    out_ref[:, :O_AT] = product((x_ref, x2_ref), both, 0, O_AT)
    out_ref[:, O_AT:EXTRA_AT] = product((c_ref, c2_ref), both, O_AT, ATTENTION_HALF)
    out_ref[:, EXTRA_AT:] = extra_ref[...]


NARROW = pl.BlockSpec((ROWS, 256), lambda step: (0, step))
WIDE = pl.BlockSpec((ROWS, 1024), lambda step: (0, step))


def hidden_grads(own, own_half, other, other_half):
    tokens = [NARROW, WIDE, whole((ROWS, HIDDEN_HALF))]
    return pl.pallas_call(
        hidden_grads_kernel,
        grid=(4,),
        in_specs=[*tokens, *tokens],
        out_specs=pl.BlockSpec((256, HIDDEN_ALL), lambda step: (step, 0)),
        out_shape=shaped(WIDTH, HIDDEN_ALL),
        compiler_params=pltpu.CompilerParams(vmem_limit_bytes=LIMIT),
        cost_estimate=cost(0.7),
        name="hidden_grads",
    )(*own, own_half, *other, other_half)


def attention_grads(own, own_half, other, other_half, extra):
    tokens = [NARROW, NARROW, whole((ROWS, ATTENTION_HALF))]
    return pl.pallas_call(
        attention_grads_kernel,
        grid=(4,),
        in_specs=[*tokens, *tokens, pl.BlockSpec((256, 128), lambda step: (step, 0))],
        out_specs=pl.BlockSpec((256, ATTENTION_ALL), lambda step: (step, 0)),
        out_shape=shaped(WIDTH, ATTENTION_ALL),
        compiler_params=pltpu.CompilerParams(vmem_limit_bytes=LIMIT),
        cost_estimate=cost(0.35),
        name="attention_grads",
    )(*own, own_half, *other, other_half, extra)


def finish_kernel(
    core_ref, hidden_ref, hidden2_ref, attention_ref, attention2_ref,
    project_ref, output_ref, up_ref, down_ref
):
    def place(half, hidden, attention):
        project_ref[:, half * 1536 : (half + 1) * 1536] = attention[:, :O_AT]
        output_ref[:, half * 512 : (half + 1) * 512] = attention[:, O_AT:EXTRA_AT]
        up_ref[:, half * 2048 : (half + 1) * 2048] = hidden[:, :DOWN_AT]
        for group in range(4):
            at = DOWN_AT + group * 512
            down_ref[group * 64 : group * 64 + 64, half * 512 : (half + 1) * 512] = hidden[
                :, at : at + 512
            ]

    for core in range(2):

        @pl.when(core_ref[0] == core)
        def _():
            place(core, hidden_ref, attention_ref)
            place(1 - core, hidden2_ref, attention2_ref)


def finish(core, *totals):
    vmem = pl.BlockSpec(memory_space=pltpu.VMEM)
    return pl.pallas_call(
        finish_kernel,
        in_specs=[pl.BlockSpec(memory_space=pltpu.SMEM)] + [vmem] * 4,
        out_specs=[vmem] * 4,
        out_shape=[
            shaped(64, 3 * WIDTH, kind=F32),
            shaped(64, WIDTH, kind=F32),
            shaped(64, HIDDEN, kind=F32),
            shaped(256, WIDTH, kind=F32),
        ],
        compiler_params=pltpu.CompilerParams(vmem_limit_bytes=LIMIT),
        name="finish",
    )(core, *totals)


def gather_weights(project, output, upward, downward, vectors):
    core = lax.axis_index("core")
    half = lax.dynamic_slice_in_dim(
        jnp.concatenate([project, output, upward], 1), core * 32, 32, 0
    )
    down = lax.dynamic_slice_in_dim(downward, core * 128, 128, 0)
    down = down.reshape(4, 32, WIDTH).transpose(1, 0, 2).reshape(32, HIDDEN)
    flat = jnp.concatenate(vectors).reshape(6, 128)
    extra = jnp.concatenate([flat, jnp.zeros((26, 128), BF16)], 0)
    packed = jnp.concatenate([half, down, extra], 1)
    gathered = lax.all_gather(packed, ("z", "y", "core"), axis=0, tiled=True)
    rows = gathered[:, VECTORS_AT:].reshape(16, 64, 128)[:, :6].astype(F32)
    pairs = rows[:, :4].reshape(16, 8, 64).transpose(1, 0, 2).reshape(8, WIDTH)
    ups = rows[:, 4:].reshape(1, HIDDEN)
    biases = jnp.concatenate(
        [pairs[0:1], jnp.zeros((1, WIDTH), F32), pairs[1:2], pairs[2:3], ups], 1
    )
    return gathered, biases, pairs


def sum_to_owner(blocks, axis, dim):
    at = lax.axis_index(axis)

    def block(steps):
        return lax.dynamic_index_in_dim(blocks, lax.rem(at + steps, 4), dim, keepdims=False)

    total = block(0).astype(F32)
    for steps in (2, 1, 3):
        sent = lax.ppermute(block(steps), axis, [(i, (i + steps) % 4) for i in range(4)])
        total += sent.astype(F32)
    return total


def scatter_direct(packed):
    blocks = packed.reshape(4, 4, 64, packed.shape[1])
    left = sum_to_owner(blocks[..., :CUT], "z", 0).astype(BF16)
    right = sum_to_owner(blocks[..., CUT:], "y", 1).astype(BF16)
    return jnp.concatenate(
        [sum_to_owner(left, "y", 0).astype(BF16), sum_to_owner(right, "z", 0).astype(BF16)], 1
    )


def over_replicas(owned):
    owned = lax.optimization_barrier(owned)
    total = owned.astype(F32) + swap_far(owned).astype(F32)
    total = lax.optimization_barrier(total)
    return total, swap_cores(total)


def gradients(core, own, other, upstream, gathered, pairs, kept):
    rows16, c, hidden, e = own
    rows16_2, c_2, hidden_2, e_2 = other
    branch, mine, theirs, pair_grads, up_grads = hidden_backward(
        core, upstream, gathered, pairs, kept
    )
    packed = hidden_grads((hidden, e), mine, (hidden_2, e_2), swap_cores(theirs))
    owned = lax.psum_scatter(packed, ("z", "y"), scatter_dimension=0, tiled=True)

    rows_grad, mine, theirs, more_grads = attention_backward(core, branch, gathered, kept[0])
    pair_grads = pair_grads + more_grads
    rows = jnp.concatenate(
        [
            pair_grads.reshape(8, 16, 64).transpose(1, 0, 2).reshape(16, 4, 128),
            up_grads.reshape(16, 2, 128),
        ],
        1,
    ).astype(BF16)
    extra = jnp.concatenate([rows, jnp.zeros((16, 58, 128), BF16)], 1).reshape(WIDTH, 128)
    direct = attention_grads((rows16, c), mine, (rows16_2, c_2), swap_cores(theirs), extra)
    attention, attention2 = over_replicas(scatter_direct(direct))
    hidden, hidden2 = over_replicas(owned)
    project, output, upward, downward = finish(core, hidden, hidden2, attention, attention2)
    vectors = (attention[:6, EXTRA_AT:] + attention2[:6, EXTRA_AT:]).reshape(768)
    narrow = [vectors[64 * k : 64 * (k + 1)][None] for k in range(8)]
    query, value, output_b, down_b, gain_one, shift_one, gain_two, shift_two = narrow
    return rows_grad, (
        project[None],
        output[None],
        upward[None],
        downward[None],
        query,
        value,
        output_b,
        vectors[512:768][None],
        down_b,
        gain_one,
        shift_one,
        gain_two,
        shift_two,
    )


def on_device(
    layer_input,
    cotangent,
    project_weight,
    output_weight,
    up_weight,
    down_weight,
    query_bias,
    value_bias,
    output_bias,
    up_bias,
    down_bias,
    first_gain,
    first_shift,
    second_gain,
    second_shift,
):
    first_section = lax.axis_index("section") == 0
    gathered, biases, pairs = gather_weights(
        project_weight[0],
        output_weight[0],
        up_weight[0],
        down_weight[0],
        (
            query_bias[0],
            value_bias[0],
            output_bias[0],
            down_bias[0],
            first_gain[0],
            first_shift[0],
            second_gain[0],
            second_shift[0],
            up_bias[0],
        ),
    )
    shape = layer_input.shape
    own_rows = layer_input.reshape(-1, WIDTH)
    own_grad = cotangent.reshape(-1, WIDTH)

    early = layer_forward(own_rows, gathered, biases, pairs, False)[0]
    received = lax.ppermute(early, "section", [(0, 1)])
    rows16 = jnp.where(first_section, own_rows, received)
    result, p, c, hidden, e, slope, n_one, r_one, n_two, r_two = layer_forward(
        rows16, gathered, biases, pairs, True
    )
    kept = (p, slope, n_one, r_one, n_two, r_two)
    own = (rows16, c, hidden, e)
    other = tuple(swap_cores(array) for array in own)

    early_grad = layer_through(own_grad, gathered, pairs, kept)
    back = lax.ppermute(early_grad, "section", [(1, 0)])
    upstream = jnp.where(first_section, back, own_grad)
    core = lax.axis_index("core").astype(jnp.int32).reshape(1)
    rows_grad, grads = gradients(core, own, other, upstream, gathered, pairs, kept)
    return (result.reshape(1, *shape), rows_grad.reshape(1, *shape), *grads)


def solution(mesh):
    devices = mesh.devices.reshape(2, 2, 2, 4, 4)
    fine = Mesh(devices, ("section", "far", "core", "z", "y"))
    shard = ("z", "y")
    seqs = P(None, ("far", "core", "z", "y"), None, None)
    matrix = P("section", shard, None)
    vector = P("section", shard)
    rows = P("section", None, ("far", "core", "z", "y"), None, None)
    return jax.shard_map(
        on_device,
        mesh=fine,
        in_specs=(seqs, seqs, *([matrix] * 4), *([vector] * 9)),
        out_specs=(rows, rows, *([matrix] * 4), *([vector] * 9)),
        check_vma=False,
    )
```

```python
import functools

import jax
import jax.numpy as jnp
from jax import lax
from jax.experimental import pallas as pl
from jax.experimental.pallas import tpu as pltpu
from jax.sharding import Mesh
from jax.sharding import PartitionSpec as P

HEADS = 16
HEAD_DIM = 64
LEN = 128
ROWS = 256
WIDTH = 1024
HIDDEN = 4096
BLOCK = 1024
SCALE = HEAD_DIM ** (-0.5)
EPSILON = 1e-06
ROOT_HALF = 0.5**0.5
NORMAL_PEAK = 0.3989422804014327
LIMIT = 48 * 1024 * 1024

VECTORS_AT = 12288
GATHERED = 12416
Z_AT, O_AT, FIRST_HALF = 2048, 2560, 3072
DOWN_AT, OUTPUT_AT, FIRST_ALL = 2048, 4096, 4608
EXTRA_AT, LAST_ALL, FAR_HALF, CUT = 1536, 1792, 896, 384

F32 = jnp.float32
BF16 = jnp.bfloat16


def dot(left, right):
    return jnp.dot(left, right, preferred_element_type=F32)


def dot_back(left, right):
    return lax.dot_general(left, right, (((1,), (1,)), ((), ())), preferred_element_type=F32)


def dot_rows(left, right):
    return lax.dot_general(left, right, (((0,), (0,)), ((), ())), preferred_element_type=F32)


def swap_cores(value):
    return lax.ppermute(value, "core", [(0, 1), (1, 0)])


def swap_far(value):
    return lax.ppermute(value, "far", [(0, 1), (1, 0)])


def mean(values):
    return jnp.mean(values, -1, keepdims=True)


def normalise(totals):
    centred = totals - mean(totals)
    inverse = lax.rsqrt(mean(centred * centred) + EPSILON)
    return centred * inverse, inverse


def norm_backward(upstream, normed, inverse, gain_row):
    scaled = upstream * gain_row
    return inverse * (scaled - mean(scaled) - normed * mean(scaled * normed))


def stacked(values):
    low = lax.broadcasted_iota(jnp.int32, values.shape, 1) < HEAD_DIM
    zeros = jnp.zeros_like(values)
    return jnp.concatenate([jnp.where(low, values, zeros), jnp.where(low, zeros, values)], 0)


def beside(values):
    low = lax.broadcasted_iota(jnp.int32, (LEN, 128), 1) < HEAD_DIM
    return jnp.where(low, values[:LEN], values[LEN:])


def soft_of(queries, keys):
    scores = dot_back(queries, keys)
    weights = jnp.exp((scores - jnp.max(scores, -1, keepdims=True)) * SCALE)
    return weights * (1.0 / jnp.sum(weights, -1, keepdims=True))


def pair_of(ref, rows, part, pair):
    at = part * WIDTH + pair * 128
    return ref[rows, at : at + 128]


def down_rows(block):
    return jnp.concatenate(
        [
            block[32 * part : 32 * part + 32, WIDTH * group : WIDTH * (group + 1)]
            for part in range(8)
            for group in range(4)
        ],
        0,
    )


def forward_kernel(keep, x_ref, column_ref, row_ref, bias_ref, pairs_ref, y_ref, p_ref, c_ref, hidden_ref, *others):
    step = pl.program_id(0)
    total_ref = others[-1]
    if keep:
        e_ref, slope_ref, n_one_ref, r_one_ref, n_two_ref, r_two_ref = others[:-1]

    @pl.when(step < 3)
    def _():
        at = pl.multiple_of(step * BLOCK, BLOCK)
        p_ref[:, pl.ds(at, BLOCK)] = (dot(x_ref[...], column_ref[...]) + bias_ref[...]).astype(BF16)

    @pl.when(step == 3)
    def _():
        for seq in range(ROWS // LEN):
            rows = slice(seq * LEN, (seq + 1) * LEN)
            softs = [
                soft_of(stacked(pair_of(p_ref, rows, 0, pair)), pair_of(p_ref, rows, 1, pair)).astype(BF16)
                for pair in range(HEADS // 2)
            ]
            for pair, soft in enumerate(softs):
                c_ref[rows, pair * 128 : (pair + 1) * 128] = beside(
                    dot(soft, pair_of(p_ref, rows, 2, pair))
                ).astype(BF16)
        normed, inverse = normalise(
            x_ref[...].astype(F32) + (dot(c_ref[...], column_ref[...]) + bias_ref[...])
        )
        hidden = normed * pairs_ref[4:5] + pairs_ref[5:6]
        hidden_ref[...] = hidden.astype(BF16)
        total_ref[...] = hidden + pairs_ref[3:4]
        if keep:
            n_one_ref[...] = normed
            r_one_ref[...] = jnp.broadcast_to(inverse, (ROWS, 128))

    @pl.when(step >= 4)
    def _():
        upper = dot(hidden_ref[...], column_ref[...]) + bias_ref[...]
        share = 0.5 * (1.0 + lax.erf(upper * ROOT_HALF))
        active = (upper * share).astype(BF16)
        if keep:
            e_ref[...] = active
            slope_ref[...] = (
                share + upper * (NORMAL_PEAK * jnp.exp(-0.5 * upper * upper))
            ).astype(BF16)
        total_ref[...] += dot(active, down_rows(row_ref[...]))

    @pl.when(step == 7)
    def _():
        normed, inverse = normalise(total_ref[...])
        y_ref[...] = (normed * pairs_ref[6:7] + pairs_ref[7:8]).astype(BF16)
        if keep:
            n_two_ref[...] = normed
            r_two_ref[...] = jnp.broadcast_to(inverse, (ROWS, 128))


def whole(shape):
    return pl.BlockSpec(shape, lambda step: (0,) * len(shape))


def shaped(*dims, kind=BF16):
    return jax.ShapeDtypeStruct(dims, kind)


def layer_forward(rows16, gathered, biases, pairs, keep):
    later = lambda step: (0, jnp.maximum(step - 4, 0))
    results = [
        (whole((ROWS, WIDTH)), shaped(ROWS, WIDTH)),
        (whole((ROWS, 3 * WIDTH)), shaped(ROWS, 3 * WIDTH)),
        (whole((ROWS, WIDTH)), shaped(ROWS, WIDTH)),
        (whole((ROWS, WIDTH)), shaped(ROWS, WIDTH)),
    ]
    scratch = [pltpu.VMEM((ROWS, WIDTH), F32)]
    if keep:
        results += [
            (pl.BlockSpec((ROWS, BLOCK), later), shaped(ROWS, HIDDEN)),
            (pl.BlockSpec((ROWS, BLOCK), later), shaped(ROWS, HIDDEN)),
            (whole((ROWS, WIDTH)), shaped(ROWS, WIDTH, kind=F32)),
            (whole((ROWS, 128)), shaped(ROWS, 128, kind=F32)),
            (whole((ROWS, WIDTH)), shaped(ROWS, WIDTH, kind=F32)),
            (whole((ROWS, 128)), shaped(ROWS, 128, kind=F32)),
        ]
    else:
        scratch = [pltpu.VMEM(shape.shape, BF16) for _, shape in results[1:]] + scratch
        results = results[:1]
    return pl.pallas_call(
        functools.partial(forward_kernel, keep),
        grid=(8,),
        in_specs=[
            whole((ROWS, WIDTH)),
            pl.BlockSpec((WIDTH, BLOCK), lambda step: (0, step)),
            pl.BlockSpec((256, HIDDEN), lambda step: (jnp.maximum(step - 4, 0), 2)),
            pl.BlockSpec((1, BLOCK), lambda step: (0, step)),
            whole((8, WIDTH)),
        ],
        out_specs=[spec for spec, _ in results],
        out_shape=[shape for _, shape in results],
        scratch_shapes=scratch,
        compiler_params=pltpu.CompilerParams(vmem_limit_bytes=LIMIT),
        cost_estimate=pl.CostEstimate(
            flops=2 * ROWS * 12 * WIDTH * WIDTH, bytes_accessed=32 << 20, transcendentals=0
        ),
        name="layer_forward",
    )(rows16, gathered, gathered, biases, pairs)


def column_sums(values):
    return jnp.sum(values, 0, keepdims=True)


def put_half(core, half, mine_ref, theirs_ref, columns, values):
    @pl.when(core == half)
    def _():
        mine_ref[:, columns] = values

    @pl.when(core != half)
    def _():
        theirs_ref[:, columns] = values


def hidden_begin(keep, core, upstream_ref, pairs_ref, n_two_ref, r_two_ref, z_ref, total_ref, kept):
    upstream = upstream_ref[...].astype(F32)
    normed = n_two_ref[...]
    grad = norm_backward(upstream, normed, r_two_ref[:, 0:1], pairs_ref[6:7])
    total_ref[...] = grad
    rounded = grad.astype(BF16)
    z_ref[...] = rounded
    if keep:
        mine_ref, theirs_ref, pair_grads_ref, _ = kept
        pair_grads_ref[6:7] = column_sums(upstream * normed)
        pair_grads_ref[7:8] = column_sums(upstream)
        pair_grads_ref[3:4] = column_sums(rounded.astype(F32))
        for half in range(2):
            put_half(
                core, half, mine_ref, theirs_ref, pl.ds(Z_AT, 512),
                rounded[:, half * 512 : half * 512 + 512],
            )


def hidden_step(keep, core, step, column_ref, row_ref, slope_ref, z_ref, total_ref, kept):
    active_grad = dot_back(z_ref[...], down_rows(row_ref[...]))
    upper_grad = (active_grad * slope_ref[...].astype(F32)).astype(BF16)
    if keep:
        mine_ref, theirs_ref, _, up_grads_ref = kept
        up_grads_ref[...] = column_sums(upper_grad.astype(F32))
        at = pl.multiple_of(lax.rem(step, 2) * BLOCK, BLOCK)
        put_half(core, step // 2, mine_ref, theirs_ref, pl.ds(at, BLOCK), upper_grad)
    total_ref[...] += dot_back(upper_grad, column_ref[...])


def hidden_end(keep, core, pairs_ref, n_one_ref, r_one_ref, total_ref, kept):
    hidden_grad = total_ref[...]
    normed = n_one_ref[...]
    grad = norm_backward(hidden_grad, normed, r_one_ref[:, 0:1], pairs_ref[4:5])
    if keep:
        mine_ref, theirs_ref, pair_grads_ref, _ = kept
        pair_grads_ref[4:5] = column_sums(hidden_grad * normed)
        pair_grads_ref[5:6] = column_sums(hidden_grad)
        rounded = grad.astype(BF16)
        pair_grads_ref[2:3] = column_sums(rounded.astype(F32))
        for half in range(2):
            put_half(
                core, half, mine_ref, theirs_ref, pl.ds(O_AT, 512),
                rounded[:, half * 512 : half * 512 + 512],
            )
    return grad


def attention_step(keep, core, grad, column_ref, p_ref, z_ref, p_grad_ref, total_ref, kept):
    rounded = grad.astype(BF16)
    z_ref[...] = dot_back(rounded, column_ref[...]).astype(BF16)
    for seq in range(ROWS // LEN):
        rows = slice(seq * LEN, (seq + 1) * LEN)
        pairs = range(HEADS // 2)
        softs = [
            soft_of(stacked(pair_of(p_ref, rows, 0, pair)), pair_of(p_ref, rows, 1, pair))
            for pair in pairs
        ]
        soft_grads = [
            dot_back(stacked(pair_of(z_ref, rows, 0, pair)), pair_of(p_ref, rows, 2, pair))
            for pair in pairs
        ]
        scores_grads = []
        for soft, soft_grad in zip(softs, soft_grads):
            weighed = soft_grad * soft
            scores_grads.append(
                (weighed - soft * jnp.sum(weighed, -1, keepdims=True)).astype(BF16)
            )
        for pair in pairs:
            grads = (
                beside(dot(scores_grads[pair], pair_of(p_ref, rows, 1, pair))) * SCALE,
                dot_rows(scores_grads[pair], stacked(pair_of(p_ref, rows, 0, pair))) * SCALE,
                dot_rows(softs[pair].astype(BF16), stacked(pair_of(z_ref, rows, 0, pair))),
            )
            for part in range(3):
                at = part * WIDTH + pair * 128
                p_grad_ref[rows, at : at + 128] = grads[part].astype(BF16)
    if keep:
        mine_ref, theirs_ref, pair_grads_ref = kept
        for half in range(2):
            put_half(
                core, half, mine_ref, theirs_ref, pl.ds(0, EXTRA_AT),
                p_grad_ref[:, half * EXTRA_AT : (half + 1) * EXTRA_AT],
            )
        pair_grads_ref[0:1] = column_sums(p_grad_ref[:, :WIDTH].astype(F32))
        pair_grads_ref[1:2] = column_sums(p_grad_ref[:, 2 * WIDTH :].astype(F32))
    total_ref[...] = grad


def project_step(step, column_ref, p_grad_ref, total_ref):
    at = pl.multiple_of(step * BLOCK, BLOCK)
    total_ref[...] += dot_back(p_grad_ref[:, pl.ds(at, BLOCK)], column_ref[...])


def through_kernel(
    upstream_ref, column_ref, row_ref, pairs_ref, p_ref, slope_ref,
    n_one_ref, r_one_ref, n_two_ref, r_two_ref, x_grad_ref, z_ref, p_grad_ref, total_ref
):
    step = pl.program_id(0)

    @pl.when(step == 0)
    def _():
        hidden_begin(False, None, upstream_ref, pairs_ref, n_two_ref, r_two_ref, z_ref, total_ref, None)

    @pl.when(step < 4)
    def _():
        hidden_step(False, None, step, column_ref, row_ref, slope_ref, z_ref, total_ref, None)

    @pl.when(step == 4)
    def _():
        grad = hidden_end(False, None, pairs_ref, n_one_ref, r_one_ref, total_ref, None)
        attention_step(False, None, grad, column_ref, p_ref, z_ref, p_grad_ref, total_ref, None)

    @pl.when(step >= 5)
    def _():
        project_step(step - 5, column_ref, p_grad_ref, total_ref)

    @pl.when(step == 7)
    def _():
        x_grad_ref[...] = total_ref[...].astype(BF16)


def cost(share):
    return pl.CostEstimate(
        flops=int(2 * ROWS * 12 * WIDTH * WIDTH * share),
        bytes_accessed=int(share * (32 << 20)),
        transcendentals=0,
    )


SMALL = pl.CostEstimate(flops=1, bytes_accessed=1, transcendentals=0)


def layer_through(upstream, gathered, pairs, kept):
    p, slope, n_one, r_one, n_two, r_two = kept
    column = lambda step: (0, jnp.where(step < 4, step + 4, jnp.where(step < 5, 3, step - 5)))
    return pl.pallas_call(
        through_kernel,
        grid=(8,),
        in_specs=[
            whole((ROWS, WIDTH)),
            pl.BlockSpec((WIDTH, BLOCK), column),
            pl.BlockSpec((256, HIDDEN), lambda step: (jnp.minimum(step, 3), 2)),
            whole((8, WIDTH)),
            whole((ROWS, 3 * WIDTH)),
            pl.BlockSpec((ROWS, BLOCK), lambda step: (0, jnp.minimum(step, 3))),
            whole((ROWS, WIDTH)),
            whole((ROWS, 128)),
            whole((ROWS, WIDTH)),
            whole((ROWS, 128)),
        ],
        out_specs=whole((ROWS, WIDTH)),
        out_shape=shaped(ROWS, WIDTH),
        scratch_shapes=[
            pltpu.VMEM((ROWS, WIDTH), BF16),
            pltpu.VMEM((ROWS, 3 * WIDTH), BF16),
            pltpu.VMEM((ROWS, WIDTH), F32),
        ],
        compiler_params=pltpu.CompilerParams(vmem_limit_bytes=LIMIT),
        cost_estimate=cost(1.0),
        name="layer_through",
    )(upstream, gathered, gathered, pairs, p, slope, n_one, r_one, n_two, r_two)


def hidden_kernel(
    core_ref, upstream_ref, column_ref, row_ref, pairs_ref, slope_ref,
    n_one_ref, r_one_ref, n_two_ref, r_two_ref,
    branch_ref, mine_ref, theirs_ref, pair_grads_ref, up_grads_ref, z_ref, total_ref
):
    step = pl.program_id(0)
    core = core_ref[0]
    kept = (mine_ref, theirs_ref, pair_grads_ref, up_grads_ref)

    @pl.when(step == 0)
    def _():
        pair_grads_ref[...] = jnp.zeros_like(pair_grads_ref)
        hidden_begin(True, core, upstream_ref, pairs_ref, n_two_ref, r_two_ref, z_ref, total_ref, kept)

    hidden_step(True, core, step, column_ref, row_ref, slope_ref, z_ref, total_ref, kept)

    @pl.when(step == 3)
    def _():
        branch_ref[...] = hidden_end(True, core, pairs_ref, n_one_ref, r_one_ref, total_ref, kept)


def hidden_backward(core, upstream, gathered, pairs, kept):
    _, slope, n_one, r_one, n_two, r_two = kept
    return pl.pallas_call(
        hidden_kernel,
        grid=(4,),
        in_specs=[
            pl.BlockSpec(memory_space=pltpu.SMEM),
            whole((ROWS, WIDTH)),
            pl.BlockSpec((WIDTH, BLOCK), lambda step: (0, step + 4)),
            pl.BlockSpec((256, HIDDEN), lambda step: (step, 2)),
            whole((8, WIDTH)),
            pl.BlockSpec((ROWS, BLOCK), lambda step: (0, step)),
            whole((ROWS, WIDTH)),
            whole((ROWS, 128)),
            whole((ROWS, WIDTH)),
            whole((ROWS, 128)),
        ],
        out_specs=[
            whole((ROWS, WIDTH)),
            whole((ROWS, FIRST_HALF)),
            whole((ROWS, FIRST_HALF)),
            whole((8, WIDTH)),
            pl.BlockSpec((1, BLOCK), lambda step: (0, step)),
        ],
        out_shape=[
            shaped(ROWS, WIDTH, kind=F32),
            shaped(ROWS, FIRST_HALF),
            shaped(ROWS, FIRST_HALF),
            shaped(8, WIDTH, kind=F32),
            shaped(1, HIDDEN, kind=F32),
        ],
        scratch_shapes=[pltpu.VMEM((ROWS, WIDTH), BF16), pltpu.VMEM((ROWS, WIDTH), F32)],
        compiler_params=pltpu.CompilerParams(vmem_limit_bytes=LIMIT),
        cost_estimate=cost(0.6),
        name="hidden_backward",
    )(core, upstream, gathered, gathered, pairs, slope, n_one, r_one, n_two, r_two)


def attention_kernel(
    core_ref, branch_ref, column_ref, p_ref,
    x_grad_ref, mine_ref, theirs_ref, pair_grads_ref, z_ref, p_grad_ref, total_ref
):
    step = pl.program_id(0)
    kept = (mine_ref, theirs_ref, pair_grads_ref)

    @pl.when(step == 0)
    def _():
        pair_grads_ref[...] = jnp.zeros_like(pair_grads_ref)
        attention_step(
            True, core_ref[0], branch_ref[...], column_ref, p_ref, z_ref, p_grad_ref, total_ref, kept
        )

    @pl.when(step >= 1)
    def _():
        project_step(step - 1, column_ref, p_grad_ref, total_ref)

    @pl.when(step == 3)
    def _():
        x_grad_ref[...] = total_ref[...].astype(BF16)


def attention_backward(core, branch, gathered, p):
    return pl.pallas_call(
        attention_kernel,
        grid=(4,),
        in_specs=[
            pl.BlockSpec(memory_space=pltpu.SMEM),
            whole((ROWS, WIDTH)),
            pl.BlockSpec((WIDTH, BLOCK), lambda step: (0, jnp.where(step < 1, 3, step - 1))),
            whole((ROWS, 3 * WIDTH)),
        ],
        out_specs=[
            whole((ROWS, WIDTH)),
            whole((ROWS, EXTRA_AT)),
            whole((ROWS, EXTRA_AT)),
            whole((8, WIDTH)),
        ],
        out_shape=[
            shaped(ROWS, WIDTH),
            shaped(ROWS, EXTRA_AT),
            shaped(ROWS, EXTRA_AT),
            shaped(8, WIDTH, kind=F32),
        ],
        scratch_shapes=[
            pltpu.VMEM((ROWS, WIDTH), BF16),
            pltpu.VMEM((ROWS, 3 * WIDTH), BF16),
            pltpu.VMEM((ROWS, WIDTH), F32),
        ],
        compiler_params=pltpu.CompilerParams(vmem_limit_bytes=LIMIT),
        cost_estimate=cost(0.5),
        name="attention_backward",
    )(core, branch, gathered, p)


def product(left_refs, right_refs, at=0, end=None):
    return (
        dot_rows(left_refs[0][...], right_refs[0][:, at:end])
        + dot_rows(left_refs[1][...], right_refs[1][:, at:end])
    ).astype(BF16)


def first_grads_kernel(h_ref, e_ref, c_ref, left_ref, h2_ref, e2_ref, c2_ref, right_ref, out_ref):
    both = (left_ref, right_ref)
    out_ref[:, :DOWN_AT] = product((h_ref, h2_ref), both, 0, Z_AT)
    down = product((e_ref, e2_ref), both, Z_AT, O_AT)
    for part in range(4):
        for group in range(4):
            at = part * 256 + group * 64
            out_ref[
                part * 64 : part * 64 + 64, DOWN_AT + group * 512 : DOWN_AT + (group + 1) * 512
            ] = down[at : at + 64]
    out_ref[:, OUTPUT_AT:] = product((c_ref, c2_ref), both, O_AT, FIRST_HALF)


NARROW = pl.BlockSpec((ROWS, 256), lambda step: (0, step))
WIDE = pl.BlockSpec((ROWS, 1024), lambda step: (0, step))


def first_grads(own, own_half, other, other_half):
    tokens = [NARROW, WIDE, NARROW, whole((ROWS, FIRST_HALF))]
    return pl.pallas_call(
        first_grads_kernel,
        grid=(4,),
        in_specs=[*tokens, *tokens],
        out_specs=pl.BlockSpec((256, FIRST_ALL), lambda step: (step, 0)),
        out_shape=shaped(WIDTH, FIRST_ALL),
        compiler_params=pltpu.CompilerParams(vmem_limit_bytes=LIMIT),
        cost_estimate=cost(0.7),
        name="first_grads",
    )(*own, own_half, *other, other_half)


def last_grads_kernel(far_ref, x_ref, left_ref, x2_ref, right_ref, extra_ref, near_out, far_out):
    both = (left_ref, right_ref)
    low = product((x_ref, x2_ref), both, 0, FAR_HALF)
    high = product((x_ref, x2_ref), both, FAR_HALF, EXTRA_AT)
    at = EXTRA_AT - FAR_HALF

    def put(low_ref, high_ref):
        low_ref[...] = low
        high_ref[:, :at] = high
        high_ref[:, at : at + 128] = extra_ref[...]
        high_ref[:, at + 128 :] = jnp.zeros((256, LAST_ALL - EXTRA_AT - 128), BF16)

    @pl.when(far_ref[0] == 0)
    def _():
        put(near_out, far_out)

    @pl.when(far_ref[0] != 0)
    def _():
        put(far_out, near_out)


def last_grads(far, own, own_half, other, other_half, extra):
    tokens = [NARROW, whole((ROWS, EXTRA_AT))]
    rows = lambda step: (step, 0)
    return pl.pallas_call(
        last_grads_kernel,
        grid=(4,),
        in_specs=[
            pl.BlockSpec(memory_space=pltpu.SMEM), *tokens, *tokens, pl.BlockSpec((256, 128), rows)
        ],
        out_specs=[pl.BlockSpec((256, FAR_HALF), rows)] * 2,
        out_shape=[shaped(WIDTH, FAR_HALF)] * 2,
        compiler_params=pltpu.CompilerParams(vmem_limit_bytes=LIMIT),
        cost_estimate=cost(0.35),
        name="last_grads",
    )(far, own, own_half, other, other_half, extra)


def split_kernel(place_ref, near_ref, far_ref, *refs):
    left_out, right_out = refs[:4], refs[4:8]
    for k in range(4):
        rows = pl.ds(pl.multiple_of(lax.rem(place_ref[0] + k, 4) * 256, 256), 256)
        left_out[k][...] = (
            near_ref[rows, :CUT].astype(F32) + far_ref[rows, :CUT].astype(F32)
        ).astype(BF16)
        for z in range(4):
            at = z * 256 + lax.rem(place_ref[1] + k, 4) * 64
            rows = pl.ds(pl.multiple_of(at, 64), 64)
            right_out[k][z] = (
                near_ref[rows, CUT:].astype(F32) + far_ref[rows, CUT:].astype(F32)
            ).astype(BF16)


def split(place, near, far):
    vmem = pl.BlockSpec(memory_space=pltpu.VMEM)
    results = pl.pallas_call(
        split_kernel,
        in_specs=[pl.BlockSpec(memory_space=pltpu.SMEM), vmem, vmem],
        out_specs=[vmem] * 8,
        out_shape=[shaped(256, CUT)] * 4 + [shaped(4, 64, FAR_HALF - CUT)] * 4,
        compiler_params=pltpu.CompilerParams(vmem_limit_bytes=LIMIT),
        cost_estimate=cost(0.1),
        name="split",
    )(place, near, far)
    return results[:4], results[4:]


def halfway_kernel(place_ref, *refs):
    lefts, rights = refs[:4], refs[4:8]
    left_out, right_out = refs[8:12], refs[12:16]
    left_ref, right_ref = refs[16:]

    def total(parts):
        return sum([part[...].astype(F32) for part in parts[1:]], parts[0][...].astype(F32)).astype(BF16)

    left_ref[...] = total(lefts)
    right_ref[...] = total(rights)
    for k in range(4):
        y = pl.multiple_of(lax.rem(place_ref[1] + k, 4) * 64, 64)
        left_out[k][...] = left_ref[pl.ds(y, 64)]
        right_out[k][...] = right_ref[lax.rem(place_ref[0] + k, 4)]


def halfway(place, lefts, rights):
    width = rights[0].shape[2]
    vmem = pl.BlockSpec(memory_space=pltpu.VMEM)
    results = pl.pallas_call(
        halfway_kernel,
        in_specs=[pl.BlockSpec(memory_space=pltpu.SMEM)] + [vmem] * 8,
        out_specs=[vmem] * 8,
        out_shape=[shaped(64, CUT)] * 4 + [shaped(64, width)] * 4,
        scratch_shapes=[pltpu.VMEM((256, CUT), BF16), pltpu.VMEM((4, 64, width), BF16)],
        compiler_params=pltpu.CompilerParams(vmem_limit_bytes=LIMIT),
        cost_estimate=cost(0.1),
        name="halfway",
    )(place, *lefts, *rights)
    return results[:4], results[4:]


def finish_kernel(
    core_ref, far_ref, first_in, first2_in, near_in, near2_in, away_in, away2_in,
    project_ref, output_ref, up_ref, down_ref
):
    def put(half, first, low, high):
        at = half * EXTRA_AT
        project_ref[:, at : at + FAR_HALF] = low[...].astype(F32)
        project_ref[:, at + FAR_HALF : at + EXTRA_AT] = high[:, : EXTRA_AT - FAR_HALF].astype(F32)
        output_ref[:, half * 512 : (half + 1) * 512] = first[:, OUTPUT_AT:]
        up_ref[:, half * 2048 : (half + 1) * 2048] = first[:, :DOWN_AT]
        for group in range(4):
            at = DOWN_AT + group * 512
            down_ref[group * 64 : group * 64 + 64, half * 512 : (half + 1) * 512] = first[
                :, at : at + 512
            ]

    for core in range(2):
        for far in range(2):

            @pl.when((core_ref[0] == core) & (far_ref[0] == far))
            def _():
                for half, first, near, away in (
                    (core, first_in, near_in, away_in),
                    (1 - core, first2_in, near2_in, away2_in),
                ):
                    put(half, first, *((near, away) if far == 0 else (away, near)))


def finish(core, far, *totals):
    vmem = pl.BlockSpec(memory_space=pltpu.VMEM)
    smem = pl.BlockSpec(memory_space=pltpu.SMEM)
    return pl.pallas_call(
        finish_kernel,
        in_specs=[smem, smem] + [vmem] * 6,
        out_specs=[vmem] * 4,
        out_shape=[
            shaped(64, 3 * WIDTH, kind=F32),
            shaped(64, WIDTH, kind=F32),
            shaped(64, HIDDEN, kind=F32),
            shaped(256, WIDTH, kind=F32),
        ],
        compiler_params=pltpu.CompilerParams(vmem_limit_bytes=LIMIT),
        name="finish",
    )(core, far, *totals)


def gather_weights(project, output, upward, downward, vectors):
    core = lax.axis_index("core")
    half = lax.dynamic_slice_in_dim(
        jnp.concatenate([project, output, upward], 1), core * 32, 32, 0
    )
    down = lax.dynamic_slice_in_dim(downward, core * 128, 128, 0)
    down = down.reshape(4, 32, WIDTH).transpose(1, 0, 2).reshape(32, HIDDEN)
    flat = jnp.concatenate(vectors).reshape(6, 128)
    extra = jnp.concatenate([flat, jnp.zeros((26, 128), BF16)], 0)
    packed = jnp.concatenate([half, down, extra], 1)
    gathered = lax.all_gather(packed, ("z", "y", "core"), axis=0, tiled=True)
    rows = gathered[:, VECTORS_AT:].reshape(16, 64, 128)[:, :6].astype(F32)
    pairs = rows[:, :4].reshape(16, 8, 64).transpose(1, 0, 2).reshape(8, WIDTH)
    ups = rows[:, 4:].reshape(1, HIDDEN)
    biases = jnp.concatenate(
        [pairs[0:1], jnp.zeros((1, WIDTH), F32), pairs[1:2], pairs[2:3], ups], 1
    )
    return gathered, biases, pairs


def send_around(blocks, axis):
    return [blocks[0]] + [
        lax.ppermute(blocks[k], axis, [(i, (i + k) % 4) for i in range(4)]) for k in (1, 2, 3)
    ]


def after_kernel(value_ref, earlier_ref, out_ref):
    pass


def after(value, earlier):
    memory = pl.BlockSpec(memory_space=pl.ANY)
    return pl.pallas_call(
        after_kernel,
        in_specs=[memory, memory],
        out_specs=memory,
        out_shape=jax.ShapeDtypeStruct(value.shape, value.dtype),
        input_output_aliases={0: 0},
        cost_estimate=SMALL,
        name="after",
    )(value, earlier)


def scatter_direct(place, lefts, rights):
    lefts, rights = halfway(place, send_around(lefts, "z"), send_around(rights, "y"))
    middle = lefts[0]

    def total(parts):
        return sum(part.astype(F32) for part in parts).astype(BF16)

    owned = jnp.concatenate([total(send_around(lefts, "y")), total(send_around(rights, "z"))], 1)
    return lax.optimization_barrier(owned), middle


def over_replicas(owned, earlier):
    owned = lax.optimization_barrier(owned)
    total = owned.astype(F32) + after(swap_far(owned), earlier).astype(F32)
    total = lax.optimization_barrier(total)
    return total, swap_cores(total)


def gradients(core, own, other, upstream, gathered, pairs, kept):
    rows16, c, hidden, e = own
    rows16_2, c_2, hidden_2, e_2 = other
    place = jnp.stack([lax.axis_index("z"), lax.axis_index("y")]).astype(jnp.int32)
    far = lax.axis_index("far").astype(jnp.int32).reshape(1)
    branch, mine, theirs, pair_grads, up_grads = hidden_backward(
        core, upstream, gathered, pairs, kept
    )
    packed = first_grads((hidden, e, c), mine, (hidden_2, e_2, c_2), swap_cores(theirs))
    owned = lax.psum_scatter(packed, ("z", "y"), scatter_dimension=0, tiled=True)

    rows_grad, mine, theirs, more_grads = attention_backward(core, branch, gathered, kept[0])
    pair_grads = pair_grads + more_grads
    rows = jnp.concatenate(
        [
            pair_grads.reshape(8, 16, 64).transpose(1, 0, 2).reshape(16, 4, 128),
            up_grads.reshape(16, 2, 128),
        ],
        1,
    ).astype(BF16)
    extra = jnp.concatenate([rows, jnp.zeros((16, 58, 128), BF16)], 1).reshape(WIDTH, 128)
    near_part, far_part = last_grads(far, rows16, mine, rows16_2, swap_cores(theirs), extra)
    near, middle = scatter_direct(place, *split(place, near_part, swap_far(far_part)))
    away = swap_far(near)
    near2, away2 = swap_cores(near), swap_cores(away)
    first, first2 = over_replicas(after(owned, middle), away)
    project, output, upward, downward = finish(
        core, far, first, first2, near, near2, away, away2
    )
    at = EXTRA_AT - FAR_HALF
    sums = [
        (one[:6, at : at + 128].astype(F32) + two[:6, at : at + 128].astype(F32))
        for one, two in ((near, near2), (away, away2))
    ]
    vectors = jnp.where(far[0] == 1, *sums).reshape(768)
    narrow = [vectors[64 * k : 64 * (k + 1)][None] for k in range(8)]
    query, value, output_b, down_b, gain_one, shift_one, gain_two, shift_two = narrow
    return rows_grad, (
        project[None],
        output[None],
        upward[None],
        downward[None],
        query,
        value,
        output_b,
        vectors[512:768][None],
        down_b,
        gain_one,
        shift_one,
        gain_two,
        shift_two,
    )


def on_device(
    layer_input,
    cotangent,
    project_weight,
    output_weight,
    up_weight,
    down_weight,
    query_bias,
    value_bias,
    output_bias,
    up_bias,
    down_bias,
    first_gain,
    first_shift,
    second_gain,
    second_shift,
):
    first_section = lax.axis_index("section") == 0
    gathered, biases, pairs = gather_weights(
        project_weight[0],
        output_weight[0],
        up_weight[0],
        down_weight[0],
        (
            query_bias[0],
            value_bias[0],
            output_bias[0],
            down_bias[0],
            first_gain[0],
            first_shift[0],
            second_gain[0],
            second_shift[0],
            up_bias[0],
        ),
    )
    shape = layer_input.shape
    own_rows = layer_input.reshape(-1, WIDTH)
    own_grad = cotangent.reshape(-1, WIDTH)

    early = layer_forward(own_rows, gathered, biases, pairs, False)[0]
    received = lax.ppermute(early, "section", [(0, 1)])
    rows16 = jnp.where(first_section, own_rows, received)
    result, p, c, hidden, e, slope, n_one, r_one, n_two, r_two = layer_forward(
        rows16, gathered, biases, pairs, True
    )
    kept = (p, slope, n_one, r_one, n_two, r_two)
    own = (rows16, c, hidden, e)
    other = tuple(swap_cores(array) for array in own)

    early_grad = layer_through(own_grad, gathered, pairs, kept)
    back = lax.ppermute(early_grad, "section", [(1, 0)])
    upstream = jnp.where(first_section, back, own_grad)
    core = lax.axis_index("core").astype(jnp.int32).reshape(1)
    rows_grad, grads = gradients(core, own, other, upstream, gathered, pairs, kept)
    return (result.reshape(1, *shape), rows_grad.reshape(1, *shape), *grads)


def solution(mesh):
    devices = mesh.devices.reshape(2, 2, 2, 4, 4)
    fine = Mesh(devices, ("section", "far", "core", "z", "y"))
    shard = ("z", "y")
    seqs = P(None, ("far", "core", "z", "y"), None, None)
    matrix = P("section", shard, None)
    vector = P("section", shard)
    rows = P("section", None, ("far", "core", "z", "y"), None, None)
    return jax.shard_map(
        on_device,
        mesh=fine,
        in_specs=(seqs, seqs, *([matrix] * 4), *([vector] * 9)),
        out_specs=(rows, rows, *([matrix] * 4), *([vector] * 9)),
        check_vma=False,
    )
```

```python
import functools

import jax
import jax.numpy as jnp
from jax import lax
from jax.experimental import pallas as pl
from jax.experimental.pallas import tpu as pltpu
from jax.sharding import Mesh
from jax.sharding import PartitionSpec as P

HEADS = 16
HEAD_DIM = 64
LEN = 128
ROWS = 256
WIDTH = 1024
HIDDEN = 4096
BLOCK = 1024
SCALE = HEAD_DIM ** (-0.5)
EPSILON = 1e-06
ROOT_HALF = 0.5**0.5
NORMAL_PEAK = 0.3989422804014327
LIMIT = 48 * 1024 * 1024

VECTORS_AT = 12288
GATHERED = 12416
Z_AT, O_AT, FIRST_HALF = 2048, 2560, 3072
DOWN_AT, OUTPUT_AT, FIRST_ALL = 2048, 4096, 4608
QUARTER, LAST_ALL, CUT = 768, 896, 384

F32 = jnp.float32
BF16 = jnp.bfloat16


def dot(left, right):
    return jnp.dot(left, right, preferred_element_type=F32)


def dot_back(left, right):
    return lax.dot_general(left, right, (((1,), (1,)), ((), ())), preferred_element_type=F32)


def dot_rows(left, right):
    return lax.dot_general(left, right, (((0,), (0,)), ((), ())), preferred_element_type=F32)


def swap_cores(value):
    return lax.ppermute(value, "core", [(0, 1), (1, 0)])


def swap_both(value):
    return lax.ppermute(value, ("far", "core"), [(0, 3), (1, 2), (2, 1), (3, 0)])


def swap_far(value):
    return lax.ppermute(value, "far", [(0, 1), (1, 0)])


def mean(values):
    return jnp.mean(values, -1, keepdims=True)


def normalise(totals):
    centred = totals - mean(totals)
    inverse = lax.rsqrt(mean(centred * centred) + EPSILON)
    return centred * inverse, inverse


def norm_backward(upstream, normed, inverse, gain_row):
    scaled = upstream * gain_row
    return inverse * (scaled - mean(scaled) - normed * mean(scaled * normed))


def stacked(values):
    low = lax.broadcasted_iota(jnp.int32, values.shape, 1) < HEAD_DIM
    zeros = jnp.zeros_like(values)
    return jnp.concatenate([jnp.where(low, values, zeros), jnp.where(low, zeros, values)], 0)


def beside(values):
    low = lax.broadcasted_iota(jnp.int32, (LEN, 128), 1) < HEAD_DIM
    return jnp.where(low, values[:LEN], values[LEN:])


def soft_of(queries, keys):
    scores = dot_back(queries, keys)
    weights = jnp.exp((scores - jnp.max(scores, -1, keepdims=True)) * SCALE)
    return weights * (1.0 / jnp.sum(weights, -1, keepdims=True))


def pair_of(ref, rows, part, pair):
    at = part * WIDTH + pair * 128
    return ref[rows, at : at + 128]


def down_rows(block):
    return jnp.concatenate(
        [
            block[32 * part : 32 * part + 32, WIDTH * group : WIDTH * (group + 1)]
            for part in range(8)
            for group in range(4)
        ],
        0,
    )


def forward_kernel(keep, x_ref, column_ref, row_ref, bias_ref, pairs_ref, y_ref, p_ref, c_ref, hidden_ref, *others):
    step = pl.program_id(0)
    total_ref = others[-1]
    if keep:
        e_ref, slope_ref, n_one_ref, r_one_ref, n_two_ref, r_two_ref = others[:-1]

    @pl.when(step < 3)
    def _():
        at = pl.multiple_of(step * BLOCK, BLOCK)
        p_ref[:, pl.ds(at, BLOCK)] = (dot(x_ref[...], column_ref[...]) + bias_ref[...]).astype(BF16)

    @pl.when(step == 3)
    def _():
        for seq in range(ROWS // LEN):
            rows = slice(seq * LEN, (seq + 1) * LEN)
            softs = [
                soft_of(stacked(pair_of(p_ref, rows, 0, pair)), pair_of(p_ref, rows, 1, pair)).astype(BF16)
                for pair in range(HEADS // 2)
            ]
            for pair, soft in enumerate(softs):
                c_ref[rows, pair * 128 : (pair + 1) * 128] = beside(
                    dot(soft, pair_of(p_ref, rows, 2, pair))
                ).astype(BF16)
        normed, inverse = normalise(
            x_ref[...].astype(F32) + (dot(c_ref[...], column_ref[...]) + bias_ref[...])
        )
        hidden = normed * pairs_ref[4:5] + pairs_ref[5:6]
        hidden_ref[...] = hidden.astype(BF16)
        total_ref[...] = hidden + pairs_ref[3:4]
        if keep:
            n_one_ref[...] = normed
            r_one_ref[...] = jnp.broadcast_to(inverse, (ROWS, 128))

    @pl.when(step >= 4)
    def _():
        upper = dot(hidden_ref[...], column_ref[...]) + bias_ref[...]
        share = 0.5 * (1.0 + lax.erf(upper * ROOT_HALF))
        active = (upper * share).astype(BF16)
        if keep:
            e_ref[...] = active
            slope_ref[...] = (
                share + upper * (NORMAL_PEAK * jnp.exp(-0.5 * upper * upper))
            ).astype(BF16)
        total_ref[...] += dot(active, down_rows(row_ref[...]))

    @pl.when(step == 7)
    def _():
        normed, inverse = normalise(total_ref[...])
        y_ref[...] = (normed * pairs_ref[6:7] + pairs_ref[7:8]).astype(BF16)
        if keep:
            n_two_ref[...] = normed
            r_two_ref[...] = jnp.broadcast_to(inverse, (ROWS, 128))


def whole(shape):
    return pl.BlockSpec(shape, lambda step: (0,) * len(shape))


def shaped(*dims, kind=BF16):
    return jax.ShapeDtypeStruct(dims, kind)


def layer_forward(rows16, gathered, biases, pairs, keep):
    later = lambda step: (0, jnp.maximum(step - 4, 0))
    results = [
        (whole((ROWS, WIDTH)), shaped(ROWS, WIDTH)),
        (whole((ROWS, 3 * WIDTH)), shaped(ROWS, 3 * WIDTH)),
        (whole((ROWS, WIDTH)), shaped(ROWS, WIDTH)),
        (whole((ROWS, WIDTH)), shaped(ROWS, WIDTH)),
    ]
    scratch = [pltpu.VMEM((ROWS, WIDTH), F32)]
    if keep:
        results += [
            (pl.BlockSpec((ROWS, BLOCK), later), shaped(ROWS, HIDDEN)),
            (pl.BlockSpec((ROWS, BLOCK), later), shaped(ROWS, HIDDEN)),
            (whole((ROWS, WIDTH)), shaped(ROWS, WIDTH, kind=F32)),
            (whole((ROWS, 128)), shaped(ROWS, 128, kind=F32)),
            (whole((ROWS, WIDTH)), shaped(ROWS, WIDTH, kind=F32)),
            (whole((ROWS, 128)), shaped(ROWS, 128, kind=F32)),
        ]
    else:
        scratch = [pltpu.VMEM(shape.shape, BF16) for _, shape in results[1:]] + scratch
        results = results[:1]
    return pl.pallas_call(
        functools.partial(forward_kernel, keep),
        grid=(8,),
        in_specs=[
            whole((ROWS, WIDTH)),
            pl.BlockSpec((WIDTH, BLOCK), lambda step: (0, step)),
            pl.BlockSpec((256, HIDDEN), lambda step: (jnp.maximum(step - 4, 0), 2)),
            pl.BlockSpec((1, BLOCK), lambda step: (0, step)),
            whole((8, WIDTH)),
        ],
        out_specs=[spec for spec, _ in results],
        out_shape=[shape for _, shape in results],
        scratch_shapes=scratch,
        compiler_params=pltpu.CompilerParams(vmem_limit_bytes=LIMIT),
        cost_estimate=pl.CostEstimate(
            flops=2 * ROWS * 12 * WIDTH * WIDTH, bytes_accessed=32 << 20, transcendentals=0
        ),
        name="layer_forward",
    )(rows16, gathered, gathered, biases, pairs)


def column_sums(values):
    return jnp.sum(values, 0, keepdims=True)


def put_half(core, half, mine_ref, theirs_ref, columns, values):
    @pl.when(core == half)
    def _():
        mine_ref[:, columns] = values

    @pl.when(core != half)
    def _():
        theirs_ref[:, columns] = values


def hidden_begin(keep, core, upstream_ref, pairs_ref, n_two_ref, r_two_ref, z_ref, total_ref, kept):
    upstream = upstream_ref[...].astype(F32)
    normed = n_two_ref[...]
    grad = norm_backward(upstream, normed, r_two_ref[:, 0:1], pairs_ref[6:7])
    total_ref[...] = grad
    rounded = grad.astype(BF16)
    z_ref[...] = rounded
    if keep:
        mine_ref, theirs_ref, pair_grads_ref, _ = kept
        pair_grads_ref[6:7] = column_sums(upstream * normed)
        pair_grads_ref[7:8] = column_sums(upstream)
        pair_grads_ref[3:4] = column_sums(rounded.astype(F32))
        for half in range(2):
            put_half(
                core, half, mine_ref, theirs_ref, pl.ds(Z_AT, 512),
                rounded[:, half * 512 : half * 512 + 512],
            )


def hidden_step(keep, core, step, column_ref, row_ref, slope_ref, z_ref, total_ref, kept):
    active_grad = dot_back(z_ref[...], down_rows(row_ref[...]))
    upper_grad = (active_grad * slope_ref[...].astype(F32)).astype(BF16)
    if keep:
        mine_ref, theirs_ref, _, up_grads_ref = kept
        up_grads_ref[...] = column_sums(upper_grad.astype(F32))
        at = pl.multiple_of(lax.rem(step, 2) * BLOCK, BLOCK)
        put_half(core, step // 2, mine_ref, theirs_ref, pl.ds(at, BLOCK), upper_grad)
    total_ref[...] += dot_back(upper_grad, column_ref[...])


def hidden_end(keep, core, pairs_ref, n_one_ref, r_one_ref, total_ref, kept):
    hidden_grad = total_ref[...]
    normed = n_one_ref[...]
    grad = norm_backward(hidden_grad, normed, r_one_ref[:, 0:1], pairs_ref[4:5])
    if keep:
        mine_ref, theirs_ref, pair_grads_ref, _ = kept
        pair_grads_ref[4:5] = column_sums(hidden_grad * normed)
        pair_grads_ref[5:6] = column_sums(hidden_grad)
        rounded = grad.astype(BF16)
        pair_grads_ref[2:3] = column_sums(rounded.astype(F32))
        for half in range(2):
            put_half(
                core, half, mine_ref, theirs_ref, pl.ds(O_AT, 512),
                rounded[:, half * 512 : half * 512 + 512],
            )
    return grad


def attention_step(keep, device, grad, column_ref, p_ref, z_ref, p_grad_ref, total_ref, kept):
    rounded = grad.astype(BF16)
    z_ref[...] = dot_back(rounded, column_ref[...]).astype(BF16)
    for seq in range(ROWS // LEN):
        rows = slice(seq * LEN, (seq + 1) * LEN)
        pairs = range(HEADS // 2)
        softs = [
            soft_of(stacked(pair_of(p_ref, rows, 0, pair)), pair_of(p_ref, rows, 1, pair))
            for pair in pairs
        ]
        soft_grads = [
            dot_back(stacked(pair_of(z_ref, rows, 0, pair)), pair_of(p_ref, rows, 2, pair))
            for pair in pairs
        ]
        scores_grads = []
        for soft, soft_grad in zip(softs, soft_grads):
            weighed = soft_grad * soft
            scores_grads.append(
                (weighed - soft * jnp.sum(weighed, -1, keepdims=True)).astype(BF16)
            )
        for pair in pairs:
            grads = (
                beside(dot(scores_grads[pair], pair_of(p_ref, rows, 1, pair))) * SCALE,
                dot_rows(scores_grads[pair], stacked(pair_of(p_ref, rows, 0, pair))) * SCALE,
                dot_rows(softs[pair].astype(BF16), stacked(pair_of(z_ref, rows, 0, pair))),
            )
            for part in range(3):
                at = part * WIDTH + pair * 128
                p_grad_ref[rows, at : at + 128] = grads[part].astype(BF16)
    if keep:
        *quarter_refs, pair_grads_ref = kept
        for owner in range(4):
            values = p_grad_ref[:, owner * QUARTER : (owner + 1) * QUARTER]
            for own in range(4):

                @pl.when(device == own)
                def _():
                    quarter_refs[owner ^ own][...] = values

        pair_grads_ref[0:1] = column_sums(p_grad_ref[:, :WIDTH].astype(F32))
        pair_grads_ref[1:2] = column_sums(p_grad_ref[:, 2 * WIDTH :].astype(F32))
    total_ref[...] = grad


def project_step(step, column_ref, p_grad_ref, total_ref):
    at = pl.multiple_of(step * BLOCK, BLOCK)
    total_ref[...] += dot_back(p_grad_ref[:, pl.ds(at, BLOCK)], column_ref[...])


def through_kernel(
    upstream_ref, column_ref, row_ref, pairs_ref, p_ref, slope_ref,
    n_one_ref, r_one_ref, n_two_ref, r_two_ref, x_grad_ref, z_ref, p_grad_ref, total_ref
):
    step = pl.program_id(0)

    @pl.when(step == 0)
    def _():
        hidden_begin(False, None, upstream_ref, pairs_ref, n_two_ref, r_two_ref, z_ref, total_ref, None)

    @pl.when(step < 4)
    def _():
        hidden_step(False, None, step, column_ref, row_ref, slope_ref, z_ref, total_ref, None)

    @pl.when(step == 4)
    def _():
        grad = hidden_end(False, None, pairs_ref, n_one_ref, r_one_ref, total_ref, None)
        attention_step(False, None, grad, column_ref, p_ref, z_ref, p_grad_ref, total_ref, None)

    @pl.when(step >= 5)
    def _():
        project_step(step - 5, column_ref, p_grad_ref, total_ref)

    @pl.when(step == 7)
    def _():
        x_grad_ref[...] = total_ref[...].astype(BF16)


def cost(share):
    return pl.CostEstimate(
        flops=int(2 * ROWS * 12 * WIDTH * WIDTH * share),
        bytes_accessed=int(share * (32 << 20)),
        transcendentals=0,
    )


SMALL = pl.CostEstimate(flops=1, bytes_accessed=1, transcendentals=0)


def layer_through(upstream, gathered, pairs, kept):
    p, slope, n_one, r_one, n_two, r_two = kept
    column = lambda step: (0, jnp.where(step < 4, step + 4, jnp.where(step < 5, 3, step - 5)))
    return pl.pallas_call(
        through_kernel,
        grid=(8,),
        in_specs=[
            whole((ROWS, WIDTH)),
            pl.BlockSpec((WIDTH, BLOCK), column),
            pl.BlockSpec((256, HIDDEN), lambda step: (jnp.minimum(step, 3), 2)),
            whole((8, WIDTH)),
            whole((ROWS, 3 * WIDTH)),
            pl.BlockSpec((ROWS, BLOCK), lambda step: (0, jnp.minimum(step, 3))),
            whole((ROWS, WIDTH)),
            whole((ROWS, 128)),
            whole((ROWS, WIDTH)),
            whole((ROWS, 128)),
        ],
        out_specs=whole((ROWS, WIDTH)),
        out_shape=shaped(ROWS, WIDTH),
        scratch_shapes=[
            pltpu.VMEM((ROWS, WIDTH), BF16),
            pltpu.VMEM((ROWS, 3 * WIDTH), BF16),
            pltpu.VMEM((ROWS, WIDTH), F32),
        ],
        compiler_params=pltpu.CompilerParams(vmem_limit_bytes=LIMIT),
        cost_estimate=cost(1.0),
        name="layer_through",
    )(upstream, gathered, gathered, pairs, p, slope, n_one, r_one, n_two, r_two)


def hidden_kernel(
    core_ref, upstream_ref, column_ref, row_ref, pairs_ref, slope_ref,
    n_one_ref, r_one_ref, n_two_ref, r_two_ref,
    branch_ref, mine_ref, theirs_ref, pair_grads_ref, up_grads_ref, z_ref, total_ref
):
    step = pl.program_id(0)
    core = core_ref[0]
    kept = (mine_ref, theirs_ref, pair_grads_ref, up_grads_ref)

    @pl.when(step == 0)
    def _():
        pair_grads_ref[...] = jnp.zeros_like(pair_grads_ref)
        hidden_begin(True, core, upstream_ref, pairs_ref, n_two_ref, r_two_ref, z_ref, total_ref, kept)

    hidden_step(True, core, step, column_ref, row_ref, slope_ref, z_ref, total_ref, kept)

    @pl.when(step == 3)
    def _():
        branch_ref[...] = hidden_end(True, core, pairs_ref, n_one_ref, r_one_ref, total_ref, kept)


def hidden_backward(core, upstream, gathered, pairs, kept):
    _, slope, n_one, r_one, n_two, r_two = kept
    return pl.pallas_call(
        hidden_kernel,
        grid=(4,),
        in_specs=[
            pl.BlockSpec(memory_space=pltpu.SMEM),
            whole((ROWS, WIDTH)),
            pl.BlockSpec((WIDTH, BLOCK), lambda step: (0, step + 4)),
            pl.BlockSpec((256, HIDDEN), lambda step: (step, 2)),
            whole((8, WIDTH)),
            pl.BlockSpec((ROWS, BLOCK), lambda step: (0, step)),
            whole((ROWS, WIDTH)),
            whole((ROWS, 128)),
            whole((ROWS, WIDTH)),
            whole((ROWS, 128)),
        ],
        out_specs=[
            whole((ROWS, WIDTH)),
            whole((ROWS, FIRST_HALF)),
            whole((ROWS, FIRST_HALF)),
            whole((8, WIDTH)),
            pl.BlockSpec((1, BLOCK), lambda step: (0, step)),
        ],
        out_shape=[
            shaped(ROWS, WIDTH, kind=F32),
            shaped(ROWS, FIRST_HALF),
            shaped(ROWS, FIRST_HALF),
            shaped(8, WIDTH, kind=F32),
            shaped(1, HIDDEN, kind=F32),
        ],
        scratch_shapes=[pltpu.VMEM((ROWS, WIDTH), BF16), pltpu.VMEM((ROWS, WIDTH), F32)],
        compiler_params=pltpu.CompilerParams(vmem_limit_bytes=LIMIT),
        cost_estimate=cost(0.6),
        name="hidden_backward",
    )(core, upstream, gathered, gathered, pairs, slope, n_one, r_one, n_two, r_two)


def attention_kernel(
    device_ref, branch_ref, column_ref, p_ref,
    x_grad_ref, mine_ref, far_ref, core_ref, both_ref, pair_grads_ref, z_ref, p_grad_ref, total_ref
):
    step = pl.program_id(0)
    kept = (mine_ref, far_ref, core_ref, both_ref, pair_grads_ref)

    @pl.when(step == 0)
    def _():
        pair_grads_ref[...] = jnp.zeros_like(pair_grads_ref)
        attention_step(
            True, device_ref[0], branch_ref[...], column_ref, p_ref, z_ref, p_grad_ref, total_ref, kept
        )

    @pl.when(step >= 1)
    def _():
        project_step(step - 1, column_ref, p_grad_ref, total_ref)

    @pl.when(step == 3)
    def _():
        x_grad_ref[...] = total_ref[...].astype(BF16)


def attention_backward(device, branch, gathered, p):
    return pl.pallas_call(
        attention_kernel,
        grid=(4,),
        in_specs=[
            pl.BlockSpec(memory_space=pltpu.SMEM),
            whole((ROWS, WIDTH)),
            pl.BlockSpec((WIDTH, BLOCK), lambda step: (0, jnp.where(step < 1, 3, step - 1))),
            whole((ROWS, 3 * WIDTH)),
        ],
        out_specs=[whole((ROWS, WIDTH))] + [whole((ROWS, QUARTER))] * 4 + [whole((8, WIDTH))],
        out_shape=[shaped(ROWS, WIDTH)] + [shaped(ROWS, QUARTER)] * 4 + [shaped(8, WIDTH, kind=F32)],
        scratch_shapes=[
            pltpu.VMEM((ROWS, WIDTH), BF16),
            pltpu.VMEM((ROWS, 3 * WIDTH), BF16),
            pltpu.VMEM((ROWS, WIDTH), F32),
        ],
        compiler_params=pltpu.CompilerParams(vmem_limit_bytes=LIMIT),
        cost_estimate=cost(0.5),
        name="attention_backward",
    )(device, branch, gathered, p)


def product(left_refs, right_refs, at=0, end=None):
    return (
        dot_rows(left_refs[0][...], right_refs[0][:, at:end])
        + dot_rows(left_refs[1][...], right_refs[1][:, at:end])
    ).astype(BF16)


def first_grads_kernel(h_ref, e_ref, c_ref, left_ref, h2_ref, e2_ref, c2_ref, right_ref, out_ref):
    both = (left_ref, right_ref)
    out_ref[:, :DOWN_AT] = product((h_ref, h2_ref), both, 0, Z_AT)
    down = product((e_ref, e2_ref), both, Z_AT, O_AT)
    for part in range(4):
        for group in range(4):
            at = part * 256 + group * 64
            out_ref[
                part * 64 : part * 64 + 64, DOWN_AT + group * 512 : DOWN_AT + (group + 1) * 512
            ] = down[at : at + 64]
    out_ref[:, OUTPUT_AT:] = product((c_ref, c2_ref), both, O_AT, FIRST_HALF)


NARROW = pl.BlockSpec((ROWS, 256), lambda step: (0, step))
WIDE = pl.BlockSpec((ROWS, 1024), lambda step: (0, step))


def first_grads(own, own_half, other, other_half):
    tokens = [NARROW, WIDE, NARROW, whole((ROWS, FIRST_HALF))]
    return pl.pallas_call(
        first_grads_kernel,
        grid=(4,),
        in_specs=[*tokens, *tokens],
        out_specs=pl.BlockSpec((256, FIRST_ALL), lambda step: (step, 0)),
        out_shape=shaped(WIDTH, FIRST_ALL),
        compiler_params=pltpu.CompilerParams(vmem_limit_bytes=LIMIT),
        cost_estimate=cost(0.7),
        name="first_grads",
    )(*own, own_half, *other, other_half)


def last_grads_kernel(place_ref, *refs):
    lefts, rights, extra_ref = refs[:4], refs[4:8], refs[8]
    left_out, right_out, block_ref = refs[9:13], refs[13:17], refs[17]

    def part(rows, columns):
        return sum(
            dot_rows(left[:, rows], right[:, columns]) for left, right in zip(lefts, rights)
        ).astype(BF16)

    for k in range(4):
        rows = pl.ds(pl.multiple_of(lax.rem(place_ref[0] + k, 4) * 256, 256), 256)
        left_out[k][...] = part(rows, slice(0, CUT))
    for z in range(4):
        rows = slice(z * 256, z * 256 + 256)
        block_ref[:, : QUARTER - CUT] = part(rows, slice(CUT, QUARTER))
        block_ref[:, QUARTER - CUT :] = extra_ref[rows]
        for k in range(4):
            y = pl.multiple_of(lax.rem(place_ref[1] + k, 4) * 64, 64)
            right_out[k][z] = block_ref[pl.ds(y, 64)]


def last_grads(place, lefts, rights, extra):
    vmem = pl.BlockSpec(memory_space=pltpu.VMEM)
    results = pl.pallas_call(
        last_grads_kernel,
        in_specs=[pl.BlockSpec(memory_space=pltpu.SMEM)] + [vmem] * 9,
        out_specs=[vmem] * 8,
        out_shape=[shaped(256, CUT)] * 4 + [shaped(4, 64, LAST_ALL - CUT)] * 4,
        scratch_shapes=[pltpu.VMEM((256, LAST_ALL - CUT), BF16)],
        compiler_params=pltpu.CompilerParams(vmem_limit_bytes=LIMIT),
        cost_estimate=cost(0.35),
        name="last_grads",
    )(place, *lefts, *rights, extra)
    return results[:4], results[4:]


def halfway_kernel(place_ref, *refs):
    lefts, rights = refs[:4], refs[4:8]
    left_out, right_out = refs[8:12], refs[12:16]
    left_ref, right_ref = refs[16:]

    def total(parts):
        return sum([part[...].astype(F32) for part in parts[1:]], parts[0][...].astype(F32)).astype(BF16)

    left_ref[...] = total(lefts)
    right_ref[...] = total(rights)
    for k in range(4):
        y = pl.multiple_of(lax.rem(place_ref[1] + k, 4) * 64, 64)
        left_out[k][...] = left_ref[pl.ds(y, 64)]
        right_out[k][...] = right_ref[lax.rem(place_ref[0] + k, 4)]


def halfway(place, lefts, rights):
    width = rights[0].shape[2]
    vmem = pl.BlockSpec(memory_space=pltpu.VMEM)
    results = pl.pallas_call(
        halfway_kernel,
        in_specs=[pl.BlockSpec(memory_space=pltpu.SMEM)] + [vmem] * 8,
        out_specs=[vmem] * 8,
        out_shape=[shaped(64, CUT)] * 4 + [shaped(64, width)] * 4,
        scratch_shapes=[pltpu.VMEM((256, CUT), BF16), pltpu.VMEM((4, 64, width), BF16)],
        compiler_params=pltpu.CompilerParams(vmem_limit_bytes=LIMIT),
        cost_estimate=cost(0.1),
        name="halfway",
    )(place, *lefts, *rights)
    return results[:4], results[4:]


def finish_kernel(
    core_ref, far_ref, first_in, first2_in, near_in, near2_in, away_in, away2_in,
    project_ref, output_ref, up_ref, down_ref
):
    def put(half, first, low, high):
        at = half * 2 * QUARTER
        project_ref[:, at : at + QUARTER] = low[:, :QUARTER].astype(F32)
        project_ref[:, at + QUARTER : at + 2 * QUARTER] = high[:, :QUARTER].astype(F32)
        output_ref[:, half * 512 : (half + 1) * 512] = first[:, OUTPUT_AT:]
        up_ref[:, half * 2048 : (half + 1) * 2048] = first[:, :DOWN_AT]
        for group in range(4):
            at = DOWN_AT + group * 512
            down_ref[group * 64 : group * 64 + 64, half * 512 : (half + 1) * 512] = first[
                :, at : at + 512
            ]

    for core in range(2):
        for far in range(2):

            @pl.when((core_ref[0] == core) & (far_ref[0] == far))
            def _():
                for half, first, near, away in (
                    (core, first_in, near_in, away_in),
                    (1 - core, first2_in, near2_in, away2_in),
                ):
                    put(half, first, *((near, away) if far == 0 else (away, near)))


def finish(core, far, *totals):
    vmem = pl.BlockSpec(memory_space=pltpu.VMEM)
    smem = pl.BlockSpec(memory_space=pltpu.SMEM)
    return pl.pallas_call(
        finish_kernel,
        in_specs=[smem, smem] + [vmem] * 6,
        out_specs=[vmem] * 4,
        out_shape=[
            shaped(64, 3 * WIDTH, kind=F32),
            shaped(64, WIDTH, kind=F32),
            shaped(64, HIDDEN, kind=F32),
            shaped(256, WIDTH, kind=F32),
        ],
        compiler_params=pltpu.CompilerParams(vmem_limit_bytes=LIMIT),
        name="finish",
    )(core, far, *totals)


def gather_weights(project, output, upward, downward, vectors):
    core = lax.axis_index("core")
    half = lax.dynamic_slice_in_dim(
        jnp.concatenate([project, output, upward], 1), core * 32, 32, 0
    )
    down = lax.dynamic_slice_in_dim(downward, core * 128, 128, 0)
    down = down.reshape(4, 32, WIDTH).transpose(1, 0, 2).reshape(32, HIDDEN)
    flat = jnp.concatenate(vectors).reshape(6, 128)
    extra = jnp.concatenate([flat, jnp.zeros((26, 128), BF16)], 0)
    packed = jnp.concatenate([half, down, extra], 1)
    gathered = lax.all_gather(packed, ("z", "y", "core"), axis=0, tiled=True)
    rows = gathered[:, VECTORS_AT:].reshape(16, 64, 128)[:, :6].astype(F32)
    pairs = rows[:, :4].reshape(16, 8, 64).transpose(1, 0, 2).reshape(8, WIDTH)
    ups = rows[:, 4:].reshape(1, HIDDEN)
    biases = jnp.concatenate(
        [pairs[0:1], jnp.zeros((1, WIDTH), F32), pairs[1:2], pairs[2:3], ups], 1
    )
    return gathered, biases, pairs


def send_around(blocks, axis):
    return [blocks[0]] + [
        lax.ppermute(blocks[k], axis, [(i, (i + k) % 4) for i in range(4)]) for k in (1, 2, 3)
    ]


def after_kernel(value_ref, earlier_ref, out_ref):
    pass


def after(value, earlier):
    memory = pl.BlockSpec(memory_space=pl.ANY)
    return pl.pallas_call(
        after_kernel,
        in_specs=[memory, memory],
        out_specs=memory,
        out_shape=jax.ShapeDtypeStruct(value.shape, value.dtype),
        input_output_aliases={0: 0},
        cost_estimate=SMALL,
        name="after",
    )(value, earlier)


def scatter_direct(place, lefts, rights):
    lefts, rights = halfway(place, send_around(lefts, "z"), send_around(rights, "y"))

    def total(parts):
        return sum(part.astype(F32) for part in parts).astype(BF16)

    owned = jnp.concatenate([total(send_around(lefts, "y")), total(send_around(rights, "z"))], 1)
    return lax.optimization_barrier(owned)


def over_replicas(owned):
    owned = lax.optimization_barrier(owned)
    total = owned.astype(F32) + swap_far(owned).astype(F32)
    total = lax.optimization_barrier(total)
    return total, swap_cores(total)


def gradients(core, own, other, upstream, gathered, pairs, kept):
    rows16, c, hidden, e = own
    rows16_2, c_2, hidden_2, e_2 = other
    place = jnp.stack([lax.axis_index("z"), lax.axis_index("y")]).astype(jnp.int32)
    far = lax.axis_index("far").astype(jnp.int32).reshape(1)
    branch, mine, theirs, pair_grads, up_grads = hidden_backward(
        core, upstream, gathered, pairs, kept
    )
    packed = first_grads((hidden, e, c), mine, (hidden_2, e_2, c_2), swap_cores(theirs))
    packed, rows16 = lax.optimization_barrier((packed, rows16))
    rows16_far = swap_far(rows16)
    rows16_both = swap_cores(rows16_far)
    owned = lax.psum_scatter(packed, ("z", "y"), scatter_dimension=0, tiled=True)

    rows_grad, mine, for_far, for_core, for_both, more_grads = attention_backward(
        core * 2 + far, branch, gathered, kept[0]
    )
    pair_grads = pair_grads + more_grads
    rows = jnp.concatenate(
        [
            pair_grads.reshape(8, 16, 64).transpose(1, 0, 2).reshape(16, 4, 128),
            up_grads.reshape(16, 2, 128),
        ],
        1,
    ).astype(BF16)
    extra = jnp.concatenate([rows, jnp.zeros((16, 58, 128), BF16)], 1).reshape(WIDTH, 128)
    quarters = (mine, swap_cores(for_core), swap_far(for_far), swap_both(for_both))
    blocks = last_grads(place, (rows16, rows16_2, rows16_far, rows16_both), quarters, extra)
    near = scatter_direct(place, *blocks)
    away = swap_far(near)
    near2, away2 = swap_cores(near), swap_cores(away)
    first, first2 = over_replicas(after(owned, away))
    project, output, upward, downward = finish(
        core, far, first, first2, near, near2, away, away2
    )
    ends = [part[:6, QUARTER:].astype(F32) for part in (near, away, near2, away2)]
    vectors = ((ends[0] + ends[1]) + (ends[2] + ends[3])).reshape(768)
    narrow = [vectors[64 * k : 64 * (k + 1)][None] for k in range(8)]
    query, value, output_b, down_b, gain_one, shift_one, gain_two, shift_two = narrow
    return rows_grad, (
        project[None],
        output[None],
        upward[None],
        downward[None],
        query,
        value,
        output_b,
        vectors[512:768][None],
        down_b,
        gain_one,
        shift_one,
        gain_two,
        shift_two,
    )


def on_device(
    layer_input,
    cotangent,
    project_weight,
    output_weight,
    up_weight,
    down_weight,
    query_bias,
    value_bias,
    output_bias,
    up_bias,
    down_bias,
    first_gain,
    first_shift,
    second_gain,
    second_shift,
):
    first_section = lax.axis_index("section") == 0
    gathered, biases, pairs = gather_weights(
        project_weight[0],
        output_weight[0],
        up_weight[0],
        down_weight[0],
        (
            query_bias[0],
            value_bias[0],
            output_bias[0],
            down_bias[0],
            first_gain[0],
            first_shift[0],
            second_gain[0],
            second_shift[0],
            up_bias[0],
        ),
    )
    shape = layer_input.shape
    own_rows = layer_input.reshape(-1, WIDTH)
    own_grad = cotangent.reshape(-1, WIDTH)

    early = layer_forward(own_rows, gathered, biases, pairs, False)[0]
    received = lax.ppermute(early, "section", [(0, 1)])
    rows16 = jnp.where(first_section, own_rows, received)
    result, p, c, hidden, e, slope, n_one, r_one, n_two, r_two = layer_forward(
        rows16, gathered, biases, pairs, True
    )
    kept = (p, slope, n_one, r_one, n_two, r_two)
    own = (rows16, c, hidden, e)
    other = tuple(swap_cores(array) for array in own)

    early_grad = layer_through(own_grad, gathered, pairs, kept)
    back = lax.ppermute(early_grad, "section", [(1, 0)])
    upstream = jnp.where(first_section, back, own_grad)
    core = lax.axis_index("core").astype(jnp.int32).reshape(1)
    rows_grad, grads = gradients(core, own, other, upstream, gathered, pairs, kept)
    return (result.reshape(1, *shape), rows_grad.reshape(1, *shape), *grads)


def solution(mesh):
    devices = mesh.devices.reshape(2, 2, 2, 4, 4)
    fine = Mesh(devices, ("section", "far", "core", "z", "y"))
    shard = ("z", "y")
    seqs = P(None, ("far", "core", "z", "y"), None, None)
    matrix = P("section", shard, None)
    vector = P("section", shard)
    rows = P("section", None, ("far", "core", "z", "y"), None, None)
    return jax.shard_map(
        on_device,
        mesh=fine,
        in_specs=(seqs, seqs, *([matrix] * 4), *([vector] * 9)),
        out_specs=(rows, rows, *([matrix] * 4), *([vector] * 9)),
        check_vma=False,
    )
```

```python
import functools

import jax
import jax.numpy as jnp
from jax import lax
from jax.experimental import pallas as pl
from jax.experimental.pallas import tpu as pltpu
from jax.sharding import Mesh
from jax.sharding import PartitionSpec as P

HEADS = 16
HEAD_DIM = 64
LEN = 128
ROWS = 256
WIDTH = 1024
HIDDEN = 4096
BLOCK = 1024
SCALE = HEAD_DIM ** (-0.5)
EPSILON = 1e-06
ROOT_HALF = 0.5**0.5
NORMAL_PEAK = 0.3989422804014327
LIMIT = 48 * 1024 * 1024

VECTORS_AT = 12288
GATHERED = 12416
Z_AT, O_AT, FIRST_HALF = 2048, 2560, 3072
DOWN_AT, OUTPUT_AT, FIRST_ALL = 2048, 4096, 4608
QUARTER, LAST_ALL, CUT = 768, 896, 384

F32 = jnp.float32
BF16 = jnp.bfloat16


def dot(left, right):
    return jnp.dot(left, right, preferred_element_type=F32)


def dot_back(left, right):
    return lax.dot_general(left, right, (((1,), (1,)), ((), ())), preferred_element_type=F32)


def dot_rows(left, right):
    return lax.dot_general(left, right, (((0,), (0,)), ((), ())), preferred_element_type=F32)


def swap_cores(value):
    return lax.ppermute(value, "core", [(0, 1), (1, 0)])


def swap_both(value):
    return lax.ppermute(value, ("far", "core"), [(0, 3), (1, 2), (2, 1), (3, 0)])


def swap_far(value):
    return lax.ppermute(value, "far", [(0, 1), (1, 0)])


def mean(values):
    return jnp.mean(values, -1, keepdims=True)


def normalise(totals):
    centred = totals - mean(totals)
    inverse = lax.rsqrt(mean(centred * centred) + EPSILON)
    return centred * inverse, inverse


def norm_backward(upstream, normed, inverse, gain_row):
    scaled = upstream * gain_row
    return inverse * (scaled - mean(scaled) - normed * mean(scaled * normed))


def stacked(values):
    low = lax.broadcasted_iota(jnp.int32, values.shape, 1) < HEAD_DIM
    zeros = jnp.zeros_like(values)
    return jnp.concatenate([jnp.where(low, values, zeros), jnp.where(low, zeros, values)], 0)


def beside(values):
    low = lax.broadcasted_iota(jnp.int32, (LEN, 128), 1) < HEAD_DIM
    return jnp.where(low, values[:LEN], values[LEN:])


def soft_of(queries, keys):
    scores = dot_back(queries, keys)
    weights = jnp.exp((scores - jnp.max(scores, -1, keepdims=True)) * SCALE)
    return weights * (1.0 / jnp.sum(weights, -1, keepdims=True))


def pair_of(ref, rows, part, pair):
    at = part * WIDTH + pair * 128
    return ref[rows, at : at + 128]


def down_rows(block):
    return jnp.concatenate(
        [
            block[32 * part : 32 * part + 32, WIDTH * group : WIDTH * (group + 1)]
            for part in range(8)
            for group in range(4)
        ],
        0,
    )


def forward_kernel(keep, x_ref, column_ref, row_ref, bias_ref, pairs_ref, y_ref, p_ref, c_ref, hidden_ref, *others):
    step = pl.program_id(0)
    total_ref = others[-1]
    if keep:
        e_ref, slope_ref, n_one_ref, r_one_ref, n_two_ref, r_two_ref = others[:-1]

    @pl.when(step < 3)
    def _():
        at = pl.multiple_of(step * BLOCK, BLOCK)
        p_ref[:, pl.ds(at, BLOCK)] = (dot(x_ref[...], column_ref[...]) + bias_ref[...]).astype(BF16)

    @pl.when(step == 3)
    def _():
        for seq in range(ROWS // LEN):
            rows = slice(seq * LEN, (seq + 1) * LEN)
            softs = [
                soft_of(stacked(pair_of(p_ref, rows, 0, pair)), pair_of(p_ref, rows, 1, pair)).astype(BF16)
                for pair in range(HEADS // 2)
            ]
            for pair, soft in enumerate(softs):
                c_ref[rows, pair * 128 : (pair + 1) * 128] = beside(
                    dot(soft, pair_of(p_ref, rows, 2, pair))
                ).astype(BF16)
        normed, inverse = normalise(
            x_ref[...].astype(F32) + (dot(c_ref[...], column_ref[...]) + bias_ref[...])
        )
        hidden = normed * pairs_ref[4:5] + pairs_ref[5:6]
        hidden_ref[...] = hidden.astype(BF16)
        total_ref[...] = hidden + pairs_ref[3:4]
        if keep:
            n_one_ref[...] = normed
            r_one_ref[...] = jnp.broadcast_to(inverse, (ROWS, 128))

    @pl.when(step >= 4)
    def _():
        upper = dot(hidden_ref[...], column_ref[...]) + bias_ref[...]
        share = 0.5 * (1.0 + lax.erf(upper * ROOT_HALF))
        active = (upper * share).astype(BF16)
        if keep:
            e_ref[...] = active
            slope_ref[...] = (
                share + upper * (NORMAL_PEAK * jnp.exp(-0.5 * upper * upper))
            ).astype(BF16)
        total_ref[...] += dot(active, down_rows(row_ref[...]))

    @pl.when(step == 7)
    def _():
        normed, inverse = normalise(total_ref[...])
        y_ref[...] = (normed * pairs_ref[6:7] + pairs_ref[7:8]).astype(BF16)
        if keep:
            n_two_ref[...] = normed
            r_two_ref[...] = jnp.broadcast_to(inverse, (ROWS, 128))


def whole(shape):
    return pl.BlockSpec(shape, lambda step: (0,) * len(shape))


def shaped(*dims, kind=BF16):
    return jax.ShapeDtypeStruct(dims, kind)


def layer_forward(rows16, gathered, biases, pairs, keep):
    later = lambda step: (0, jnp.maximum(step - 4, 0))
    results = [
        (whole((ROWS, WIDTH)), shaped(ROWS, WIDTH)),
        (whole((ROWS, 3 * WIDTH)), shaped(ROWS, 3 * WIDTH)),
        (whole((ROWS, WIDTH)), shaped(ROWS, WIDTH)),
        (whole((ROWS, WIDTH)), shaped(ROWS, WIDTH)),
    ]
    scratch = [pltpu.VMEM((ROWS, WIDTH), F32)]
    if keep:
        results += [
            (pl.BlockSpec((ROWS, BLOCK), later), shaped(ROWS, HIDDEN)),
            (pl.BlockSpec((ROWS, BLOCK), later), shaped(ROWS, HIDDEN)),
            (whole((ROWS, WIDTH)), shaped(ROWS, WIDTH, kind=F32)),
            (whole((ROWS, 128)), shaped(ROWS, 128, kind=F32)),
            (whole((ROWS, WIDTH)), shaped(ROWS, WIDTH, kind=F32)),
            (whole((ROWS, 128)), shaped(ROWS, 128, kind=F32)),
        ]
    else:
        scratch = [pltpu.VMEM(shape.shape, BF16) for _, shape in results[1:]] + scratch
        results = results[:1]
    return pl.pallas_call(
        functools.partial(forward_kernel, keep),
        grid=(8,),
        in_specs=[
            whole((ROWS, WIDTH)),
            pl.BlockSpec((WIDTH, BLOCK), lambda step: (0, step)),
            pl.BlockSpec((256, HIDDEN), lambda step: (jnp.maximum(step - 4, 0), 2)),
            pl.BlockSpec((1, BLOCK), lambda step: (0, step)),
            whole((8, WIDTH)),
        ],
        out_specs=[spec for spec, _ in results],
        out_shape=[shape for _, shape in results],
        scratch_shapes=scratch,
        compiler_params=pltpu.CompilerParams(vmem_limit_bytes=LIMIT),
        cost_estimate=pl.CostEstimate(
            flops=2 * ROWS * 12 * WIDTH * WIDTH, bytes_accessed=32 << 20, transcendentals=0
        ),
        name="layer_forward",
    )(rows16, gathered, gathered, biases, pairs)


def column_sums(values):
    return jnp.sum(values, 0, keepdims=True)


def put_half(core, half, mine_ref, theirs_ref, columns, values):
    @pl.when(core == half)
    def _():
        mine_ref[:, columns] = values

    @pl.when(core != half)
    def _():
        theirs_ref[:, columns] = values


def hidden_begin(keep, core, upstream_ref, pairs_ref, n_two_ref, r_two_ref, z_ref, total_ref, kept):
    upstream = upstream_ref[...].astype(F32)
    normed = n_two_ref[...]
    grad = norm_backward(upstream, normed, r_two_ref[:, 0:1], pairs_ref[6:7])
    total_ref[...] = grad
    rounded = grad.astype(BF16)
    z_ref[...] = rounded
    if keep:
        mine_ref, theirs_ref, pair_grads_ref, _ = kept
        pair_grads_ref[6:7] = column_sums(upstream * normed)
        pair_grads_ref[7:8] = column_sums(upstream)
        pair_grads_ref[3:4] = column_sums(rounded.astype(F32))
        for half in range(2):
            put_half(
                core, half, mine_ref, theirs_ref, pl.ds(Z_AT, 512),
                rounded[:, half * 512 : half * 512 + 512],
            )


def hidden_step(keep, core, step, column_ref, row_ref, slope_ref, z_ref, total_ref, kept):
    active_grad = dot_back(z_ref[...], down_rows(row_ref[...]))
    upper_grad = (active_grad * slope_ref[...].astype(F32)).astype(BF16)
    if keep:
        mine_ref, theirs_ref, _, up_grads_ref = kept
        up_grads_ref[...] = column_sums(upper_grad.astype(F32))
        at = pl.multiple_of(lax.rem(step, 2) * BLOCK, BLOCK)
        put_half(core, step // 2, mine_ref, theirs_ref, pl.ds(at, BLOCK), upper_grad)
    total_ref[...] += dot_back(upper_grad, column_ref[...])


def hidden_end(keep, core, pairs_ref, n_one_ref, r_one_ref, total_ref, kept):
    hidden_grad = total_ref[...]
    normed = n_one_ref[...]
    grad = norm_backward(hidden_grad, normed, r_one_ref[:, 0:1], pairs_ref[4:5])
    if keep:
        mine_ref, theirs_ref, pair_grads_ref, _ = kept
        pair_grads_ref[4:5] = column_sums(hidden_grad * normed)
        pair_grads_ref[5:6] = column_sums(hidden_grad)
        rounded = grad.astype(BF16)
        pair_grads_ref[2:3] = column_sums(rounded.astype(F32))
        for half in range(2):
            put_half(
                core, half, mine_ref, theirs_ref, pl.ds(O_AT, 512),
                rounded[:, half * 512 : half * 512 + 512],
            )
    return grad


def attention_step(keep, device, grad, column_ref, p_ref, z_ref, p_grad_ref, total_ref, kept):
    rounded = grad.astype(BF16)
    z_ref[...] = dot_back(rounded, column_ref[...]).astype(BF16)
    for seq in range(ROWS // LEN):
        rows = slice(seq * LEN, (seq + 1) * LEN)
        pairs = range(HEADS // 2)
        softs = [
            soft_of(stacked(pair_of(p_ref, rows, 0, pair)), pair_of(p_ref, rows, 1, pair))
            for pair in pairs
        ]
        soft_grads = [
            dot_back(stacked(pair_of(z_ref, rows, 0, pair)), pair_of(p_ref, rows, 2, pair))
            for pair in pairs
        ]
        scores_grads = []
        for soft, soft_grad in zip(softs, soft_grads):
            weighed = soft_grad * soft
            scores_grads.append(
                (weighed - soft * jnp.sum(weighed, -1, keepdims=True)).astype(BF16)
            )
        for pair in pairs:
            grads = (
                beside(dot(scores_grads[pair], pair_of(p_ref, rows, 1, pair))) * SCALE,
                dot_rows(scores_grads[pair], stacked(pair_of(p_ref, rows, 0, pair))) * SCALE,
                dot_rows(softs[pair].astype(BF16), stacked(pair_of(z_ref, rows, 0, pair))),
            )
            for part in range(3):
                at = part * WIDTH + pair * 128
                p_grad_ref[rows, at : at + 128] = grads[part].astype(BF16)
    if keep:
        *quarter_refs, pair_grads_ref = kept
        for owner in range(4):
            values = p_grad_ref[:, owner * QUARTER : (owner + 1) * QUARTER]
            for own in range(4):

                @pl.when(device == own)
                def _():
                    quarter_refs[owner ^ own][...] = values

        pair_grads_ref[0:1] = column_sums(p_grad_ref[:, :WIDTH].astype(F32))
        pair_grads_ref[1:2] = column_sums(p_grad_ref[:, 2 * WIDTH :].astype(F32))
    total_ref[...] = grad


def project_step(step, column_ref, p_grad_ref, total_ref):
    at = pl.multiple_of(step * BLOCK, BLOCK)
    total_ref[...] += dot_back(p_grad_ref[:, pl.ds(at, BLOCK)], column_ref[...])


def through_kernel(
    upstream_ref, column_ref, row_ref, pairs_ref, p_ref, slope_ref,
    n_one_ref, r_one_ref, n_two_ref, r_two_ref, x_grad_ref, z_ref, p_grad_ref, total_ref
):
    step = pl.program_id(0)

    @pl.when(step == 0)
    def _():
        hidden_begin(False, None, upstream_ref, pairs_ref, n_two_ref, r_two_ref, z_ref, total_ref, None)

    @pl.when(step < 4)
    def _():
        hidden_step(False, None, step, column_ref, row_ref, slope_ref, z_ref, total_ref, None)

    @pl.when(step == 4)
    def _():
        grad = hidden_end(False, None, pairs_ref, n_one_ref, r_one_ref, total_ref, None)
        attention_step(False, None, grad, column_ref, p_ref, z_ref, p_grad_ref, total_ref, None)

    @pl.when(step >= 5)
    def _():
        project_step(step - 5, column_ref, p_grad_ref, total_ref)

    @pl.when(step == 7)
    def _():
        x_grad_ref[...] = total_ref[...].astype(BF16)


def cost(share):
    return pl.CostEstimate(
        flops=int(2 * ROWS * 12 * WIDTH * WIDTH * share),
        bytes_accessed=int(share * (32 << 20)),
        transcendentals=0,
    )


SMALL = pl.CostEstimate(flops=1, bytes_accessed=1, transcendentals=0)


def layer_through(upstream, gathered, pairs, kept):
    p, slope, n_one, r_one, n_two, r_two = kept
    column = lambda step: (0, jnp.where(step < 4, step + 4, jnp.where(step < 5, 3, step - 5)))
    return pl.pallas_call(
        through_kernel,
        grid=(8,),
        in_specs=[
            whole((ROWS, WIDTH)),
            pl.BlockSpec((WIDTH, BLOCK), column),
            pl.BlockSpec((256, HIDDEN), lambda step: (jnp.minimum(step, 3), 2)),
            whole((8, WIDTH)),
            whole((ROWS, 3 * WIDTH)),
            pl.BlockSpec((ROWS, BLOCK), lambda step: (0, jnp.minimum(step, 3))),
            whole((ROWS, WIDTH)),
            whole((ROWS, 128)),
            whole((ROWS, WIDTH)),
            whole((ROWS, 128)),
        ],
        out_specs=whole((ROWS, WIDTH)),
        out_shape=shaped(ROWS, WIDTH),
        scratch_shapes=[
            pltpu.VMEM((ROWS, WIDTH), BF16),
            pltpu.VMEM((ROWS, 3 * WIDTH), BF16),
            pltpu.VMEM((ROWS, WIDTH), F32),
        ],
        compiler_params=pltpu.CompilerParams(vmem_limit_bytes=LIMIT),
        cost_estimate=cost(1.0),
        name="layer_through",
    )(upstream, gathered, gathered, pairs, p, slope, n_one, r_one, n_two, r_two)


def hidden_kernel(
    core_ref, upstream_ref, column_ref, row_ref, pairs_ref, slope_ref,
    n_one_ref, r_one_ref, n_two_ref, r_two_ref,
    branch_ref, mine_ref, theirs_ref, pair_grads_ref, up_grads_ref, z_ref, total_ref
):
    step = pl.program_id(0)
    core = core_ref[0]
    kept = (mine_ref, theirs_ref, pair_grads_ref, up_grads_ref)

    @pl.when(step == 0)
    def _():
        pair_grads_ref[...] = jnp.zeros_like(pair_grads_ref)
        hidden_begin(True, core, upstream_ref, pairs_ref, n_two_ref, r_two_ref, z_ref, total_ref, kept)

    hidden_step(True, core, step, column_ref, row_ref, slope_ref, z_ref, total_ref, kept)

    @pl.when(step == 3)
    def _():
        branch_ref[...] = hidden_end(True, core, pairs_ref, n_one_ref, r_one_ref, total_ref, kept)


def hidden_backward(core, upstream, gathered, pairs, kept):
    _, slope, n_one, r_one, n_two, r_two = kept
    return pl.pallas_call(
        hidden_kernel,
        grid=(4,),
        in_specs=[
            pl.BlockSpec(memory_space=pltpu.SMEM),
            whole((ROWS, WIDTH)),
            pl.BlockSpec((WIDTH, BLOCK), lambda step: (0, step + 4)),
            pl.BlockSpec((256, HIDDEN), lambda step: (step, 2)),
            whole((8, WIDTH)),
            pl.BlockSpec((ROWS, BLOCK), lambda step: (0, step)),
            whole((ROWS, WIDTH)),
            whole((ROWS, 128)),
            whole((ROWS, WIDTH)),
            whole((ROWS, 128)),
        ],
        out_specs=[
            whole((ROWS, WIDTH)),
            whole((ROWS, FIRST_HALF)),
            whole((ROWS, FIRST_HALF)),
            whole((8, WIDTH)),
            pl.BlockSpec((1, BLOCK), lambda step: (0, step)),
        ],
        out_shape=[
            shaped(ROWS, WIDTH, kind=F32),
            shaped(ROWS, FIRST_HALF),
            shaped(ROWS, FIRST_HALF),
            shaped(8, WIDTH, kind=F32),
            shaped(1, HIDDEN, kind=F32),
        ],
        scratch_shapes=[pltpu.VMEM((ROWS, WIDTH), BF16), pltpu.VMEM((ROWS, WIDTH), F32)],
        compiler_params=pltpu.CompilerParams(vmem_limit_bytes=LIMIT),
        cost_estimate=cost(0.6),
        name="hidden_backward",
    )(core, upstream, gathered, gathered, pairs, slope, n_one, r_one, n_two, r_two)


def attention_kernel(
    device_ref, branch_ref, column_ref, p_ref,
    x_grad_ref, mine_ref, far_ref, core_ref, both_ref, pair_grads_ref, z_ref, p_grad_ref, total_ref
):
    step = pl.program_id(0)
    kept = (mine_ref, far_ref, core_ref, both_ref, pair_grads_ref)

    @pl.when(step == 0)
    def _():
        pair_grads_ref[...] = jnp.zeros_like(pair_grads_ref)
        attention_step(
            True, device_ref[0], branch_ref[...], column_ref, p_ref, z_ref, p_grad_ref, total_ref, kept
        )

    @pl.when(step >= 1)
    def _():
        project_step(step - 1, column_ref, p_grad_ref, total_ref)

    @pl.when(step == 3)
    def _():
        x_grad_ref[...] = total_ref[...].astype(BF16)


def attention_backward(device, branch, gathered, p):
    return pl.pallas_call(
        attention_kernel,
        grid=(4,),
        in_specs=[
            pl.BlockSpec(memory_space=pltpu.SMEM),
            whole((ROWS, WIDTH)),
            pl.BlockSpec((WIDTH, BLOCK), lambda step: (0, jnp.where(step < 1, 3, step - 1))),
            whole((ROWS, 3 * WIDTH)),
        ],
        out_specs=[whole((ROWS, WIDTH))] + [whole((ROWS, QUARTER))] * 4 + [whole((8, WIDTH))],
        out_shape=[shaped(ROWS, WIDTH)] + [shaped(ROWS, QUARTER)] * 4 + [shaped(8, WIDTH, kind=F32)],
        scratch_shapes=[
            pltpu.VMEM((ROWS, WIDTH), BF16),
            pltpu.VMEM((ROWS, 3 * WIDTH), BF16),
            pltpu.VMEM((ROWS, WIDTH), F32),
        ],
        compiler_params=pltpu.CompilerParams(vmem_limit_bytes=LIMIT),
        cost_estimate=cost(0.5),
        name="attention_backward",
    )(device, branch, gathered, p)


def product(left_refs, right_refs, at=0, end=None):
    return (
        dot_rows(left_refs[0][...], right_refs[0][:, at:end])
        + dot_rows(left_refs[1][...], right_refs[1][:, at:end])
    ).astype(BF16)


def first_grads_kernel(h_ref, e_ref, c_ref, left_ref, h2_ref, e2_ref, c2_ref, right_ref, out_ref):
    both = (left_ref, right_ref)
    out_ref[:, :DOWN_AT] = product((h_ref, h2_ref), both, 0, Z_AT)
    down = product((e_ref, e2_ref), both, Z_AT, O_AT)
    for part in range(4):
        for group in range(4):
            at = part * 256 + group * 64
            out_ref[
                part * 64 : part * 64 + 64, DOWN_AT + group * 512 : DOWN_AT + (group + 1) * 512
            ] = down[at : at + 64]
    out_ref[:, OUTPUT_AT:] = product((c_ref, c2_ref), both, O_AT, FIRST_HALF)


NARROW = pl.BlockSpec((ROWS, 256), lambda step: (0, step))
WIDE = pl.BlockSpec((ROWS, 1024), lambda step: (0, step))


def first_grads(own, own_half, other, other_half):
    tokens = [NARROW, WIDE, NARROW, whole((ROWS, FIRST_HALF))]
    return pl.pallas_call(
        first_grads_kernel,
        grid=(4,),
        in_specs=[*tokens, *tokens],
        out_specs=pl.BlockSpec((256, FIRST_ALL), lambda step: (step, 0)),
        out_shape=shaped(WIDTH, FIRST_ALL),
        compiler_params=pltpu.CompilerParams(vmem_limit_bytes=LIMIT),
        cost_estimate=cost(0.7),
        name="first_grads",
    )(*own, own_half, *other, other_half)


def last_grads_kernel(place_ref, *refs):
    lefts, rights, extra_ref = refs[:4], refs[4:8], refs[8]
    left_out, right_out, block_ref = refs[9:13], refs[13:17], refs[17]

    def part(rows, columns):
        return sum(
            dot_rows(left[:, rows], right[:, columns]) for left, right in zip(lefts, rights)
        ).astype(BF16)

    for k in range(4):
        rows = pl.ds(pl.multiple_of(lax.rem(place_ref[0] + k, 4) * 256, 256), 256)
        left_out[k][...] = part(rows, slice(0, CUT))
    for z in range(4):
        rows = slice(z * 256, z * 256 + 256)
        block_ref[:, : QUARTER - CUT] = part(rows, slice(CUT, QUARTER))
        block_ref[:, QUARTER - CUT :] = extra_ref[rows]
        for k in range(4):
            y = pl.multiple_of(lax.rem(place_ref[1] + k, 4) * 64, 64)
            right_out[k][z] = block_ref[pl.ds(y, 64)]


def last_grads(place, lefts, rights, extra):
    vmem = pl.BlockSpec(memory_space=pltpu.VMEM)
    results = pl.pallas_call(
        last_grads_kernel,
        in_specs=[pl.BlockSpec(memory_space=pltpu.SMEM)] + [vmem] * 9,
        out_specs=[vmem] * 8,
        out_shape=[shaped(256, CUT)] * 4 + [shaped(4, 64, LAST_ALL - CUT)] * 4,
        scratch_shapes=[pltpu.VMEM((256, LAST_ALL - CUT), BF16)],
        compiler_params=pltpu.CompilerParams(vmem_limit_bytes=LIMIT),
        cost_estimate=cost(0.35),
        name="last_grads",
    )(place, *lefts, *rights, extra)
    return results[:4], results[4:]


def halfway_kernel(place_ref, *refs):
    lefts, rights = refs[:4], refs[4:8]
    left_out, right_out = refs[8:12], refs[12:16]
    left_ref, right_ref = refs[16:]

    def total(parts):
        return sum([part[...].astype(F32) for part in parts[1:]], parts[0][...].astype(F32)).astype(BF16)

    left_ref[...] = total(lefts)
    right_ref[...] = total(rights)
    for k in range(4):
        y = pl.multiple_of(lax.rem(place_ref[1] + k, 4) * 64, 64)
        left_out[k][...] = left_ref[pl.ds(y, 64)]
        right_out[k][...] = right_ref[lax.rem(place_ref[0] + k, 4)]


def halfway(place, lefts, rights):
    width = rights[0].shape[2]
    vmem = pl.BlockSpec(memory_space=pltpu.VMEM)
    results = pl.pallas_call(
        halfway_kernel,
        in_specs=[pl.BlockSpec(memory_space=pltpu.SMEM)] + [vmem] * 8,
        out_specs=[vmem] * 8,
        out_shape=[shaped(64, CUT)] * 4 + [shaped(64, width)] * 4,
        scratch_shapes=[pltpu.VMEM((256, CUT), BF16), pltpu.VMEM((4, 64, width), BF16)],
        compiler_params=pltpu.CompilerParams(vmem_limit_bytes=LIMIT),
        cost_estimate=cost(0.1),
        name="halfway",
    )(place, *lefts, *rights)
    return results[:4], results[4:]


def finish_kernel(
    core_ref, far_ref, first_in, first2_in, near_in, near2_in, away_in, away2_in,
    project_ref, output_ref, up_ref, down_ref
):
    def put(half, first, low, high):
        at = half * 2 * QUARTER
        project_ref[:, at : at + QUARTER] = low[:, :QUARTER].astype(F32)
        project_ref[:, at + QUARTER : at + 2 * QUARTER] = high[:, :QUARTER].astype(F32)
        output_ref[:, half * 512 : (half + 1) * 512] = first[:, OUTPUT_AT:]
        up_ref[:, half * 2048 : (half + 1) * 2048] = first[:, :DOWN_AT]
        for group in range(4):
            at = DOWN_AT + group * 512
            down_ref[group * 64 : group * 64 + 64, half * 512 : (half + 1) * 512] = first[
                :, at : at + 512
            ]

    for core in range(2):
        for far in range(2):

            @pl.when((core_ref[0] == core) & (far_ref[0] == far))
            def _():
                for half, first, near, away in (
                    (core, first_in, near_in, away_in),
                    (1 - core, first2_in, near2_in, away2_in),
                ):
                    put(half, first, *((near, away) if far == 0 else (away, near)))


def finish(core, far, *totals):
    vmem = pl.BlockSpec(memory_space=pltpu.VMEM)
    smem = pl.BlockSpec(memory_space=pltpu.SMEM)
    return pl.pallas_call(
        finish_kernel,
        in_specs=[smem, smem] + [vmem] * 6,
        out_specs=[vmem] * 4,
        out_shape=[
            shaped(64, 3 * WIDTH, kind=F32),
            shaped(64, WIDTH, kind=F32),
            shaped(64, HIDDEN, kind=F32),
            shaped(256, WIDTH, kind=F32),
        ],
        compiler_params=pltpu.CompilerParams(vmem_limit_bytes=LIMIT),
        name="finish",
    )(core, far, *totals)


def gather_weights(project, output, upward, downward, vectors):
    core = lax.axis_index("core")
    half = lax.dynamic_slice_in_dim(
        jnp.concatenate([project, output, upward], 1), core * 32, 32, 0
    )
    down = lax.dynamic_slice_in_dim(downward, core * 128, 128, 0)
    down = down.reshape(4, 32, WIDTH).transpose(1, 0, 2).reshape(32, HIDDEN)
    flat = jnp.concatenate(vectors).reshape(6, 128)
    extra = jnp.concatenate([flat, jnp.zeros((26, 128), BF16)], 0)
    packed = jnp.concatenate([half, down, extra], 1)
    gathered = lax.all_gather(packed, ("z", "y", "core"), axis=0, tiled=True)
    rows = gathered[:, VECTORS_AT:].reshape(16, 64, 128)[:, :6].astype(F32)
    pairs = rows[:, :4].reshape(16, 8, 64).transpose(1, 0, 2).reshape(8, WIDTH)
    ups = rows[:, 4:].reshape(1, HIDDEN)
    biases = jnp.concatenate(
        [pairs[0:1], jnp.zeros((1, WIDTH), F32), pairs[1:2], pairs[2:3], ups], 1
    )
    return gathered, biases, pairs


def send_around(blocks, axis):
    return [blocks[0]] + [
        lax.ppermute(blocks[k], axis, [(i, (i + k) % 4) for i in range(4)]) for k in (1, 2, 3)
    ]


def after_kernel(value_ref, earlier_ref, out_ref):
    pass


def after(value, earlier):
    memory = pl.BlockSpec(memory_space=pl.ANY)
    return pl.pallas_call(
        after_kernel,
        in_specs=[memory, memory],
        out_specs=memory,
        out_shape=jax.ShapeDtypeStruct(value.shape, value.dtype),
        input_output_aliases={0: 0},
        cost_estimate=SMALL,
        name="after",
    )(value, earlier)


def scatter_direct(place, lefts, rights):
    lefts, rights = halfway(place, send_around(lefts, "z"), send_around(rights, "y"))

    def total(parts):
        return sum(part.astype(F32) for part in parts).astype(BF16)

    owned = jnp.concatenate([total(send_around(lefts, "y")), total(send_around(rights, "z"))], 1)
    return lax.optimization_barrier(owned)


def over_replicas(owned):
    owned = lax.optimization_barrier(owned)
    total = owned.astype(F32) + swap_far(owned).astype(F32)
    total = lax.optimization_barrier(total)
    return total, swap_cores(total)


def gradients(core, first_section, result, own, other, upstream, gathered, pairs, kept):
    rows16, c, hidden, e = own
    rows16_2, c_2, hidden_2, e_2, rows16_far = other
    place = jnp.stack([lax.axis_index("z"), lax.axis_index("y")]).astype(jnp.int32)
    far = lax.axis_index("far").astype(jnp.int32).reshape(1)
    branch, mine, theirs, pair_grads, up_grads = hidden_backward(
        core, upstream, gathered, pairs, kept
    )
    packed = first_grads((hidden, e, c), mine, (hidden_2, e_2, c_2), swap_cores(theirs))
    packed, rows16_far = lax.optimization_barrier((packed, rows16_far))
    rows16_both = swap_cores(rows16_far)
    owned = lax.psum_scatter(packed, ("z", "y"), scatter_dimension=0, tiled=True)

    rows_grad, mine, for_far, for_core, for_both, more_grads = attention_backward(
        core * 2 + far, branch, gathered, kept[0]
    )
    pair_grads = pair_grads + more_grads
    rows = jnp.concatenate(
        [
            pair_grads.reshape(8, 16, 64).transpose(1, 0, 2).reshape(16, 4, 128),
            up_grads.reshape(16, 2, 128),
        ],
        1,
    ).astype(BF16)
    extra = jnp.concatenate([rows, jnp.zeros((16, 58, 128), BF16)], 1).reshape(WIDTH, 128)
    quarters = (mine, swap_cores(for_core), swap_far(for_far), swap_both(for_both))
    blocks = last_grads(place, (rows16, rows16_2, rows16_far, rows16_both), quarters, extra)
    seconds = jnp.concatenate([result[LEN:], rows_grad[LEN:]])
    blocks, seconds = lax.optimization_barrier((blocks, seconds))
    swapped = swap_far(seconds)
    near = scatter_direct(place, *blocks)
    away, swapped = lax.optimization_barrier((swap_far(near), swapped))
    result, rows_grad = (
        jnp.concatenate(
            [
                value[:LEN],
                jnp.where(first_section, value[LEN:], swapped[at * LEN : (at + 1) * LEN]),
            ]
        )
        for at, value in enumerate((result, rows_grad))
    )
    near2, away2 = swap_cores(near), swap_cores(away)
    first, first2 = over_replicas(after(owned, away))
    project, output, upward, downward = finish(
        core, far, first, first2, near, near2, away, away2
    )
    ends = [part[:6, QUARTER:].astype(F32) for part in (near, away, near2, away2)]
    vectors = ((ends[0] + ends[1]) + (ends[2] + ends[3])).reshape(768)
    narrow = [vectors[64 * k : 64 * (k + 1)][None] for k in range(8)]
    query, value, output_b, down_b, gain_one, shift_one, gain_two, shift_two = narrow
    return result, rows_grad, (
        project[None],
        output[None],
        upward[None],
        downward[None],
        query,
        value,
        output_b,
        vectors[512:768][None],
        down_b,
        gain_one,
        shift_one,
        gain_two,
        shift_two,
    )


def to_section(value, section):
    pairs = [[(0, 2), (1, 3)], [(0, 3), (1, 2)]]
    if section == 0:
        pairs = [[(target, source) for source, target in each] for each in pairs]
    return jnp.concatenate(
        [
            lax.ppermute(value[seq * LEN : (seq + 1) * LEN], ("section", "far"), pairs[seq])
            for seq in range(2)
        ]
    )


def on_device(
    layer_input,
    cotangent,
    project_weight,
    output_weight,
    up_weight,
    down_weight,
    query_bias,
    value_bias,
    output_bias,
    up_bias,
    down_bias,
    first_gain,
    first_shift,
    second_gain,
    second_shift,
):
    first_section = lax.axis_index("section") == 0
    gathered, biases, pairs = gather_weights(
        project_weight[0],
        output_weight[0],
        up_weight[0],
        down_weight[0],
        (
            query_bias[0],
            value_bias[0],
            output_bias[0],
            down_bias[0],
            first_gain[0],
            first_shift[0],
            second_gain[0],
            second_shift[0],
            up_bias[0],
        ),
    )
    shape = layer_input.shape
    own_rows = layer_input.reshape(-1, WIDTH)
    own_grad = cotangent.reshape(-1, WIDTH)
    own_grad = jnp.concatenate([own_grad[:LEN], swap_far(own_grad[LEN:])])

    early = layer_forward(own_rows, gathered, biases, pairs, False)[0]
    received = to_section(early, 1)
    rows16 = jnp.where(first_section, own_rows, received)
    result, p, c, hidden, e, slope, n_one, r_one, n_two, r_two = layer_forward(
        rows16, gathered, biases, pairs, True
    )
    kept = (p, slope, n_one, r_one, n_two, r_two)
    own = (rows16, c, hidden, e)
    other = tuple(swap_cores(array) for array in own)
    rows16_far, own_grad = lax.optimization_barrier((swap_far(rows16), own_grad))
    other = (*other, rows16_far)

    early_grad = layer_through(own_grad, gathered, pairs, kept)
    back = to_section(early_grad, 0)
    upstream = jnp.where(first_section, back, own_grad)
    core = lax.axis_index("core").astype(jnp.int32).reshape(1)
    result, rows_grad, grads = gradients(core, first_section, result, own, other, upstream, gathered, pairs, kept)
    return (result.reshape(1, *shape), rows_grad.reshape(1, *shape), *grads)


def solution(mesh):
    devices = mesh.devices.reshape(2, 2, 2, 4, 4)
    fine = Mesh(devices, ("section", "far", "core", "z", "y"))
    shard = ("z", "y")
    seqs = P(None, ("far", "core", "z", "y"), None, None)
    matrix = P("section", shard, None)
    vector = P("section", shard)
    rows = P("section", None, ("far", "core", "z", "y"), None, None)
    return jax.shard_map(
        on_device,
        mesh=fine,
        in_specs=(seqs, seqs, *([matrix] * 4), *([vector] * 9)),
        out_specs=(rows, rows, *([matrix] * 4), *([vector] * 9)),
        check_vma=False,
    )
```

```python
import functools

import jax
import jax.numpy as jnp
from jax import lax
from jax.experimental import pallas as pl
from jax.experimental.pallas import tpu as pltpu
from jax.sharding import Mesh
from jax.sharding import PartitionSpec as P

HEADS = 16
HEAD_DIM = 64
LEN = 128
ROWS = 256
WIDTH = 1024
HIDDEN = 4096
BLOCK = 1024
SCALE = HEAD_DIM ** (-0.5)
EPSILON = 1e-06
ROOT_HALF = 0.5**0.5
NORMAL_PEAK = 0.3989422804014327
LIMIT = 48 * 1024 * 1024

VECTORS_AT = 12288
GATHERED = 12416
Z_AT, O_AT, FIRST_HALF = 2048, 2560, 3072
DOWN_AT, OUTPUT_AT, FIRST_ALL = 2048, 4096, 4608
QUARTER, LAST_ALL, CUT = 768, 896, 384

F32 = jnp.float32
BF16 = jnp.bfloat16


def dot(left, right):
    return jnp.dot(left, right, preferred_element_type=F32)


def dot_back(left, right):
    return lax.dot_general(left, right, (((1,), (1,)), ((), ())), preferred_element_type=F32)


def dot_rows(left, right):
    return lax.dot_general(left, right, (((0,), (0,)), ((), ())), preferred_element_type=F32)


def swap_cores(value):
    return lax.ppermute(value, "core", [(0, 1), (1, 0)])


def swap_both(value):
    return lax.ppermute(value, ("far", "core"), [(0, 3), (1, 2), (2, 1), (3, 0)])


def swap_far(value):
    return lax.ppermute(value, "far", [(0, 1), (1, 0)])


def mean(values):
    return jnp.mean(values, -1, keepdims=True)


def normalise(totals):
    centred = totals - mean(totals)
    inverse = lax.rsqrt(mean(centred * centred) + EPSILON)
    return centred * inverse, inverse


def norm_backward(upstream, normed, inverse, gain_row):
    scaled = upstream * gain_row
    return inverse * (scaled - mean(scaled) - normed * mean(scaled * normed))


def stacked(values):
    low = lax.broadcasted_iota(jnp.int32, values.shape, 1) < HEAD_DIM
    zeros = jnp.zeros_like(values)
    return jnp.concatenate([jnp.where(low, values, zeros), jnp.where(low, zeros, values)], 0)


def beside(values):
    low = lax.broadcasted_iota(jnp.int32, (LEN, 128), 1) < HEAD_DIM
    return jnp.where(low, values[:LEN], values[LEN:])


def soft_of(queries, keys):
    scores = dot_back(queries, keys)
    weights = jnp.exp((scores - jnp.max(scores, -1, keepdims=True)) * SCALE)
    return weights * (1.0 / jnp.sum(weights, -1, keepdims=True))


def pair_of(ref, rows, part, pair):
    at = part * WIDTH + pair * 128
    return ref[rows, at : at + 128]


def down_rows(block):
    return jnp.concatenate(
        [
            block[32 * part : 32 * part + 32, WIDTH * group : WIDTH * (group + 1)]
            for part in range(8)
            for group in range(4)
        ],
        0,
    )


def forward_kernel(keep, x_ref, column_ref, row_ref, bias_ref, pairs_ref, y_ref, p_ref, c_ref, hidden_ref, *others):
    step = pl.program_id(0)
    total_ref = others[-1]
    if keep:
        e_ref, slope_ref, n_one_ref, r_one_ref, n_two_ref, r_two_ref = others[:-1]

    @pl.when(step < 3)
    def _():
        at = pl.multiple_of(step * BLOCK, BLOCK)
        p_ref[:, pl.ds(at, BLOCK)] = (dot(x_ref[...], column_ref[...]) + bias_ref[...]).astype(BF16)

    @pl.when(step == 3)
    def _():
        for seq in range(ROWS // LEN):
            rows = slice(seq * LEN, (seq + 1) * LEN)
            softs = [
                soft_of(stacked(pair_of(p_ref, rows, 0, pair)), pair_of(p_ref, rows, 1, pair)).astype(BF16)
                for pair in range(HEADS // 2)
            ]
            for pair, soft in enumerate(softs):
                c_ref[rows, pair * 128 : (pair + 1) * 128] = beside(
                    dot(soft, pair_of(p_ref, rows, 2, pair))
                ).astype(BF16)
        normed, inverse = normalise(
            x_ref[...].astype(F32) + (dot(c_ref[...], column_ref[...]) + bias_ref[...])
        )
        hidden = normed * pairs_ref[4:5] + pairs_ref[5:6]
        hidden_ref[...] = hidden.astype(BF16)
        total_ref[...] = hidden + pairs_ref[3:4]
        if keep:
            n_one_ref[...] = normed
            r_one_ref[...] = jnp.broadcast_to(inverse, (ROWS, 128))

    @pl.when(step >= 4)
    def _():
        upper = dot(hidden_ref[...], column_ref[...]) + bias_ref[...]
        share = 0.5 * (1.0 + lax.erf(upper * ROOT_HALF))
        active = (upper * share).astype(BF16)
        if keep:
            e_ref[...] = active
            slope_ref[...] = (
                share + upper * (NORMAL_PEAK * jnp.exp(-0.5 * upper * upper))
            ).astype(BF16)
        total_ref[...] += dot(active, down_rows(row_ref[...]))

    @pl.when(step == 7)
    def _():
        normed, inverse = normalise(total_ref[...])
        y_ref[...] = (normed * pairs_ref[6:7] + pairs_ref[7:8]).astype(BF16)
        if keep:
            n_two_ref[...] = normed
            r_two_ref[...] = jnp.broadcast_to(inverse, (ROWS, 128))


def whole(shape):
    return pl.BlockSpec(shape, lambda step: (0,) * len(shape))


def shaped(*dims, kind=BF16):
    return jax.ShapeDtypeStruct(dims, kind)


def layer_forward(rows16, gathered, biases, pairs, keep):
    later = lambda step: (0, jnp.maximum(step - 4, 0))
    results = [
        (whole((ROWS, WIDTH)), shaped(ROWS, WIDTH)),
        (whole((ROWS, 3 * WIDTH)), shaped(ROWS, 3 * WIDTH)),
        (whole((ROWS, WIDTH)), shaped(ROWS, WIDTH)),
        (whole((ROWS, WIDTH)), shaped(ROWS, WIDTH)),
    ]
    scratch = [pltpu.VMEM((ROWS, WIDTH), F32)]
    if keep:
        results += [
            (pl.BlockSpec((ROWS, BLOCK), later), shaped(ROWS, HIDDEN)),
            (pl.BlockSpec((ROWS, BLOCK), later), shaped(ROWS, HIDDEN)),
            (whole((ROWS, WIDTH)), shaped(ROWS, WIDTH, kind=F32)),
            (whole((ROWS, 128)), shaped(ROWS, 128, kind=F32)),
            (whole((ROWS, WIDTH)), shaped(ROWS, WIDTH, kind=F32)),
            (whole((ROWS, 128)), shaped(ROWS, 128, kind=F32)),
        ]
    else:
        scratch = [pltpu.VMEM(shape.shape, BF16) for _, shape in results[1:]] + scratch
        results = results[:1]
    return pl.pallas_call(
        functools.partial(forward_kernel, keep),
        grid=(8,),
        in_specs=[
            whole((ROWS, WIDTH)),
            pl.BlockSpec((WIDTH, BLOCK), lambda step: (0, step)),
            pl.BlockSpec((256, HIDDEN), lambda step: (jnp.maximum(step - 4, 0), 2)),
            pl.BlockSpec((1, BLOCK), lambda step: (0, step)),
            whole((8, WIDTH)),
        ],
        out_specs=[spec for spec, _ in results],
        out_shape=[shape for _, shape in results],
        scratch_shapes=scratch,
        compiler_params=pltpu.CompilerParams(vmem_limit_bytes=LIMIT),
        cost_estimate=pl.CostEstimate(
            flops=2 * ROWS * 12 * WIDTH * WIDTH, bytes_accessed=32 << 20, transcendentals=0
        ),
        name="layer_forward",
    )(rows16, gathered, gathered, biases, pairs)


def column_sums(values):
    return jnp.sum(values, 0, keepdims=True)


def put_half(core, half, mine_ref, theirs_ref, columns, values):
    @pl.when(core == half)
    def _():
        mine_ref[:, columns] = values

    @pl.when(core != half)
    def _():
        theirs_ref[:, columns] = values


def hidden_begin(keep, core, upstream_ref, pairs_ref, n_two_ref, r_two_ref, z_ref, total_ref, kept):
    upstream = upstream_ref[...].astype(F32)
    normed = n_two_ref[...]
    grad = norm_backward(upstream, normed, r_two_ref[:, 0:1], pairs_ref[6:7])
    total_ref[...] = grad
    rounded = grad.astype(BF16)
    z_ref[...] = rounded
    if keep:
        mine_ref, theirs_ref, pair_grads_ref, _ = kept
        pair_grads_ref[6:7] = column_sums(upstream * normed)
        pair_grads_ref[7:8] = column_sums(upstream)
        pair_grads_ref[3:4] = column_sums(rounded.astype(F32))
        for half in range(2):
            put_half(
                core, half, mine_ref, theirs_ref, pl.ds(Z_AT, 512),
                rounded[:, half * 512 : half * 512 + 512],
            )


def hidden_step(keep, core, step, column_ref, row_ref, slope_ref, z_ref, total_ref, kept):
    active_grad = dot_back(z_ref[...], down_rows(row_ref[...]))
    upper_grad = (active_grad * slope_ref[...].astype(F32)).astype(BF16)
    if keep:
        mine_ref, theirs_ref, _, up_grads_ref = kept
        up_grads_ref[...] = column_sums(upper_grad.astype(F32))
        at = pl.multiple_of(lax.rem(step, 2) * BLOCK, BLOCK)
        put_half(core, step // 2, mine_ref, theirs_ref, pl.ds(at, BLOCK), upper_grad)
    total_ref[...] += dot_back(upper_grad, column_ref[...])


def hidden_end(keep, core, pairs_ref, n_one_ref, r_one_ref, total_ref, kept):
    hidden_grad = total_ref[...]
    normed = n_one_ref[...]
    grad = norm_backward(hidden_grad, normed, r_one_ref[:, 0:1], pairs_ref[4:5])
    if keep:
        mine_ref, theirs_ref, pair_grads_ref, _ = kept
        pair_grads_ref[4:5] = column_sums(hidden_grad * normed)
        pair_grads_ref[5:6] = column_sums(hidden_grad)
        rounded = grad.astype(BF16)
        pair_grads_ref[2:3] = column_sums(rounded.astype(F32))
        for half in range(2):
            put_half(
                core, half, mine_ref, theirs_ref, pl.ds(O_AT, 512),
                rounded[:, half * 512 : half * 512 + 512],
            )
    return grad


def attention_step(keep, device, grad, column_ref, p_ref, z_ref, p_grad_ref, total_ref, kept):
    rounded = grad.astype(BF16)
    z_ref[...] = dot_back(rounded, column_ref[...]).astype(BF16)
    for seq in range(ROWS // LEN):
        rows = slice(seq * LEN, (seq + 1) * LEN)
        pairs = range(HEADS // 2)
        softs = [
            soft_of(stacked(pair_of(p_ref, rows, 0, pair)), pair_of(p_ref, rows, 1, pair))
            for pair in pairs
        ]
        soft_grads = [
            dot_back(stacked(pair_of(z_ref, rows, 0, pair)), pair_of(p_ref, rows, 2, pair))
            for pair in pairs
        ]
        scores_grads = []
        for soft, soft_grad in zip(softs, soft_grads):
            weighed = soft_grad * soft
            scores_grads.append(
                (weighed - soft * jnp.sum(weighed, -1, keepdims=True)).astype(BF16)
            )
        for pair in pairs:
            grads = (
                beside(dot(scores_grads[pair], pair_of(p_ref, rows, 1, pair))) * SCALE,
                dot_rows(scores_grads[pair], stacked(pair_of(p_ref, rows, 0, pair))) * SCALE,
                dot_rows(softs[pair].astype(BF16), stacked(pair_of(z_ref, rows, 0, pair))),
            )
            for part in range(3):
                at = part * WIDTH + pair * 128
                p_grad_ref[rows, at : at + 128] = grads[part].astype(BF16)
    if keep:
        *quarter_refs, pair_grads_ref = kept
        for owner in range(4):
            values = p_grad_ref[:, owner * QUARTER : (owner + 1) * QUARTER]
            for own in range(4):

                @pl.when(device == own)
                def _():
                    quarter_refs[owner ^ own][...] = values

        pair_grads_ref[0:1] = column_sums(p_grad_ref[:, :WIDTH].astype(F32))
        pair_grads_ref[1:2] = column_sums(p_grad_ref[:, 2 * WIDTH :].astype(F32))
    total_ref[...] = grad


def project_step(step, column_ref, p_grad_ref, total_ref):
    at = pl.multiple_of(step * BLOCK, BLOCK)
    total_ref[...] += dot_back(p_grad_ref[:, pl.ds(at, BLOCK)], column_ref[...])


def through_kernel(
    upstream_ref, column_ref, row_ref, pairs_ref, p_ref, slope_ref,
    n_one_ref, r_one_ref, n_two_ref, r_two_ref, x_grad_ref, z_ref, p_grad_ref, total_ref
):
    step = pl.program_id(0)

    @pl.when(step == 0)
    def _():
        hidden_begin(False, None, upstream_ref, pairs_ref, n_two_ref, r_two_ref, z_ref, total_ref, None)

    @pl.when(step < 4)
    def _():
        hidden_step(False, None, step, column_ref, row_ref, slope_ref, z_ref, total_ref, None)

    @pl.when(step == 4)
    def _():
        grad = hidden_end(False, None, pairs_ref, n_one_ref, r_one_ref, total_ref, None)
        attention_step(False, None, grad, column_ref, p_ref, z_ref, p_grad_ref, total_ref, None)

    @pl.when(step >= 5)
    def _():
        project_step(step - 5, column_ref, p_grad_ref, total_ref)

    @pl.when(step == 7)
    def _():
        x_grad_ref[...] = total_ref[...].astype(BF16)


def cost(share):
    return pl.CostEstimate(
        flops=int(2 * ROWS * 12 * WIDTH * WIDTH * share),
        bytes_accessed=int(share * (32 << 20)),
        transcendentals=0,
    )


SMALL = pl.CostEstimate(flops=1, bytes_accessed=1, transcendentals=0)


def layer_through(upstream, gathered, pairs, kept):
    p, slope, n_one, r_one, n_two, r_two = kept
    column = lambda step: (0, jnp.where(step < 4, step + 4, jnp.where(step < 5, 3, step - 5)))
    return pl.pallas_call(
        through_kernel,
        grid=(8,),
        in_specs=[
            whole((ROWS, WIDTH)),
            pl.BlockSpec((WIDTH, BLOCK), column),
            pl.BlockSpec((256, HIDDEN), lambda step: (jnp.minimum(step, 3), 2)),
            whole((8, WIDTH)),
            whole((ROWS, 3 * WIDTH)),
            pl.BlockSpec((ROWS, BLOCK), lambda step: (0, jnp.minimum(step, 3))),
            whole((ROWS, WIDTH)),
            whole((ROWS, 128)),
            whole((ROWS, WIDTH)),
            whole((ROWS, 128)),
        ],
        out_specs=whole((ROWS, WIDTH)),
        out_shape=shaped(ROWS, WIDTH),
        scratch_shapes=[
            pltpu.VMEM((ROWS, WIDTH), BF16),
            pltpu.VMEM((ROWS, 3 * WIDTH), BF16),
            pltpu.VMEM((ROWS, WIDTH), F32),
        ],
        compiler_params=pltpu.CompilerParams(vmem_limit_bytes=LIMIT),
        cost_estimate=cost(1.0),
        name="layer_through",
    )(upstream, gathered, gathered, pairs, p, slope, n_one, r_one, n_two, r_two)


def hidden_kernel(
    core_ref, upstream_ref, column_ref, row_ref, pairs_ref, slope_ref,
    n_one_ref, r_one_ref, n_two_ref, r_two_ref,
    branch_ref, mine_ref, theirs_ref, pair_grads_ref, up_grads_ref, z_ref, total_ref
):
    step = pl.program_id(0)
    core = core_ref[0]
    kept = (mine_ref, theirs_ref, pair_grads_ref, up_grads_ref)

    @pl.when(step == 0)
    def _():
        pair_grads_ref[...] = jnp.zeros_like(pair_grads_ref)
        hidden_begin(True, core, upstream_ref, pairs_ref, n_two_ref, r_two_ref, z_ref, total_ref, kept)

    hidden_step(True, core, step, column_ref, row_ref, slope_ref, z_ref, total_ref, kept)

    @pl.when(step == 3)
    def _():
        branch_ref[...] = hidden_end(True, core, pairs_ref, n_one_ref, r_one_ref, total_ref, kept)


def hidden_backward(core, upstream, gathered, pairs, kept):
    _, slope, n_one, r_one, n_two, r_two = kept
    return pl.pallas_call(
        hidden_kernel,
        grid=(4,),
        in_specs=[
            pl.BlockSpec(memory_space=pltpu.SMEM),
            whole((ROWS, WIDTH)),
            pl.BlockSpec((WIDTH, BLOCK), lambda step: (0, step + 4)),
            pl.BlockSpec((256, HIDDEN), lambda step: (step, 2)),
            whole((8, WIDTH)),
            pl.BlockSpec((ROWS, BLOCK), lambda step: (0, step)),
            whole((ROWS, WIDTH)),
            whole((ROWS, 128)),
            whole((ROWS, WIDTH)),
            whole((ROWS, 128)),
        ],
        out_specs=[
            whole((ROWS, WIDTH)),
            whole((ROWS, FIRST_HALF)),
            whole((ROWS, FIRST_HALF)),
            whole((8, WIDTH)),
            pl.BlockSpec((1, BLOCK), lambda step: (0, step)),
        ],
        out_shape=[
            shaped(ROWS, WIDTH, kind=F32),
            shaped(ROWS, FIRST_HALF),
            shaped(ROWS, FIRST_HALF),
            shaped(8, WIDTH, kind=F32),
            shaped(1, HIDDEN, kind=F32),
        ],
        scratch_shapes=[pltpu.VMEM((ROWS, WIDTH), BF16), pltpu.VMEM((ROWS, WIDTH), F32)],
        compiler_params=pltpu.CompilerParams(vmem_limit_bytes=LIMIT),
        cost_estimate=cost(0.6),
        name="hidden_backward",
    )(core, upstream, gathered, gathered, pairs, slope, n_one, r_one, n_two, r_two)


def attention_kernel(
    device_ref, branch_ref, column_ref, p_ref,
    x_grad_ref, mine_ref, far_ref, core_ref, both_ref, pair_grads_ref, z_ref, p_grad_ref, total_ref
):
    step = pl.program_id(0)
    kept = (mine_ref, far_ref, core_ref, both_ref, pair_grads_ref)

    @pl.when(step == 0)
    def _():
        pair_grads_ref[...] = jnp.zeros_like(pair_grads_ref)
        attention_step(
            True, device_ref[0], branch_ref[...], column_ref, p_ref, z_ref, p_grad_ref, total_ref, kept
        )

    @pl.when(step >= 1)
    def _():
        project_step(step - 1, column_ref, p_grad_ref, total_ref)

    @pl.when(step == 3)
    def _():
        x_grad_ref[...] = total_ref[...].astype(BF16)


def attention_backward(device, branch, gathered, p):
    return pl.pallas_call(
        attention_kernel,
        grid=(4,),
        in_specs=[
            pl.BlockSpec(memory_space=pltpu.SMEM),
            whole((ROWS, WIDTH)),
            pl.BlockSpec((WIDTH, BLOCK), lambda step: (0, jnp.where(step < 1, 3, step - 1))),
            whole((ROWS, 3 * WIDTH)),
        ],
        out_specs=[whole((ROWS, WIDTH))] + [whole((ROWS, QUARTER))] * 4 + [whole((8, WIDTH))],
        out_shape=[shaped(ROWS, WIDTH)] + [shaped(ROWS, QUARTER)] * 4 + [shaped(8, WIDTH, kind=F32)],
        scratch_shapes=[
            pltpu.VMEM((ROWS, WIDTH), BF16),
            pltpu.VMEM((ROWS, 3 * WIDTH), BF16),
            pltpu.VMEM((ROWS, WIDTH), F32),
        ],
        compiler_params=pltpu.CompilerParams(vmem_limit_bytes=LIMIT),
        cost_estimate=cost(0.5),
        name="attention_backward",
    )(device, branch, gathered, p)


def product(left_refs, right_refs, at=0, end=None):
    return (
        dot_rows(left_refs[0][...], right_refs[0][:, at:end])
        + dot_rows(left_refs[1][...], right_refs[1][:, at:end])
    ).astype(BF16)


def first_grads_kernel(h_ref, e_ref, c_ref, left_ref, h2_ref, e2_ref, c2_ref, right_ref, out_ref):
    both = (left_ref, right_ref)
    out_ref[:, :DOWN_AT] = product((h_ref, h2_ref), both, 0, Z_AT)
    down = product((e_ref, e2_ref), both, Z_AT, O_AT)
    for part in range(4):
        for group in range(4):
            at = part * 256 + group * 64
            out_ref[
                part * 64 : part * 64 + 64, DOWN_AT + group * 512 : DOWN_AT + (group + 1) * 512
            ] = down[at : at + 64]
    out_ref[:, OUTPUT_AT:] = product((c_ref, c2_ref), both, O_AT, FIRST_HALF)


NARROW = pl.BlockSpec((ROWS, 256), lambda step: (0, step))
WIDE = pl.BlockSpec((ROWS, 1024), lambda step: (0, step))


def first_grads(own, own_half, other, other_half):
    tokens = [NARROW, WIDE, NARROW, whole((ROWS, FIRST_HALF))]
    return pl.pallas_call(
        first_grads_kernel,
        grid=(4,),
        in_specs=[*tokens, *tokens],
        out_specs=pl.BlockSpec((256, FIRST_ALL), lambda step: (step, 0)),
        out_shape=shaped(WIDTH, FIRST_ALL),
        compiler_params=pltpu.CompilerParams(vmem_limit_bytes=LIMIT),
        cost_estimate=cost(0.7),
        name="first_grads",
    )(*own, own_half, *other, other_half)


def last_grads_kernel(place_ref, *refs):
    lefts, rights, extra_ref = refs[:4], refs[4:8], refs[8]
    left_out, right_out, block_ref = refs[9:13], refs[13:17], refs[17]

    def part(rows, columns):
        return sum(
            dot_rows(left[:, rows], right[:, columns]) for left, right in zip(lefts, rights)
        ).astype(BF16)

    for k in range(4):
        rows = pl.ds(pl.multiple_of(lax.rem(place_ref[0] + k, 4) * 256, 256), 256)
        left_out[k][...] = part(rows, slice(0, CUT))
    for z in range(4):
        rows = slice(z * 256, z * 256 + 256)
        block_ref[:, : QUARTER - CUT] = part(rows, slice(CUT, QUARTER))
        block_ref[:, QUARTER - CUT :] = extra_ref[rows]
        for k in range(4):
            y = pl.multiple_of(lax.rem(place_ref[1] + k, 4) * 64, 64)
            right_out[k][z] = block_ref[pl.ds(y, 64)]


def last_grads(place, lefts, rights, extra):
    vmem = pl.BlockSpec(memory_space=pltpu.VMEM)
    results = pl.pallas_call(
        last_grads_kernel,
        in_specs=[pl.BlockSpec(memory_space=pltpu.SMEM)] + [vmem] * 9,
        out_specs=[vmem] * 8,
        out_shape=[shaped(256, CUT)] * 4 + [shaped(4, 64, LAST_ALL - CUT)] * 4,
        scratch_shapes=[pltpu.VMEM((256, LAST_ALL - CUT), BF16)],
        compiler_params=pltpu.CompilerParams(vmem_limit_bytes=LIMIT),
        cost_estimate=cost(0.35),
        name="last_grads",
    )(place, *lefts, *rights, extra)
    return results[:4], results[4:]


def halfway_kernel(place_ref, *refs):
    lefts, rights = refs[:4], refs[4:8]
    left_out, right_out = refs[8:12], refs[12:16]
    left_ref, right_ref = refs[16:]

    def total(parts):
        return sum([part[...].astype(F32) for part in parts[1:]], parts[0][...].astype(F32)).astype(BF16)

    left_ref[...] = total(lefts)
    right_ref[...] = total(rights)
    for k in range(4):
        y = pl.multiple_of(lax.rem(place_ref[1] + k, 4) * 64, 64)
        left_out[k][...] = left_ref[pl.ds(y, 64)]
        right_out[k][...] = right_ref[lax.rem(place_ref[0] + k, 4)]


def halfway(place, lefts, rights):
    width = rights[0].shape[2]
    vmem = pl.BlockSpec(memory_space=pltpu.VMEM)
    results = pl.pallas_call(
        halfway_kernel,
        in_specs=[pl.BlockSpec(memory_space=pltpu.SMEM)] + [vmem] * 8,
        out_specs=[vmem] * 8,
        out_shape=[shaped(64, CUT)] * 4 + [shaped(64, width)] * 4,
        scratch_shapes=[pltpu.VMEM((256, CUT), BF16), pltpu.VMEM((4, 64, width), BF16)],
        compiler_params=pltpu.CompilerParams(vmem_limit_bytes=LIMIT),
        cost_estimate=cost(0.1),
        name="halfway",
    )(place, *lefts, *rights)
    return results[:4], results[4:]


def finish_kernel(
    core_ref, far_ref, first_in, first_far_in, first2_in, first2_far_in, near_in, near2_in, away_in, away2_in,
    project_ref, output_ref, up_ref, down_ref
):
    def put(half, firsts, low, high):
        first = firsts[0][...].astype(F32) + firsts[1][...].astype(F32)
        at = half * 2 * QUARTER
        project_ref[:, at : at + QUARTER] = low[:, :QUARTER].astype(F32)
        project_ref[:, at + QUARTER : at + 2 * QUARTER] = high[:, :QUARTER].astype(F32)
        output_ref[:, half * 512 : (half + 1) * 512] = first[:, OUTPUT_AT:]
        up_ref[:, half * 2048 : (half + 1) * 2048] = first[:, :DOWN_AT]
        for group in range(4):
            at = DOWN_AT + group * 512
            down_ref[group * 64 : group * 64 + 64, half * 512 : (half + 1) * 512] = first[
                :, at : at + 512
            ]

    for core in range(2):
        for far in range(2):

            @pl.when((core_ref[0] == core) & (far_ref[0] == far))
            def _():
                for half, first, near, away in (
                    (core, (first_in, first_far_in), near_in, away_in),
                    (1 - core, (first2_in, first2_far_in), near2_in, away2_in),
                ):
                    put(half, first, *((near, away) if far == 0 else (away, near)))


def finish(core, far, *totals):
    vmem = pl.BlockSpec(memory_space=pltpu.VMEM)
    smem = pl.BlockSpec(memory_space=pltpu.SMEM)
    return pl.pallas_call(
        finish_kernel,
        in_specs=[smem, smem] + [vmem] * 8,
        out_specs=[vmem] * 4,
        out_shape=[
            shaped(64, 3 * WIDTH, kind=F32),
            shaped(64, WIDTH, kind=F32),
            shaped(64, HIDDEN, kind=F32),
            shaped(256, WIDTH, kind=F32),
        ],
        compiler_params=pltpu.CompilerParams(vmem_limit_bytes=LIMIT),
        name="finish",
    )(core, far, *totals)


def gather_weights(project, output, upward, downward, vectors):
    core = lax.axis_index("core")
    half = lax.dynamic_slice_in_dim(
        jnp.concatenate([project, output, upward], 1), core * 32, 32, 0
    )
    down = lax.dynamic_slice_in_dim(downward, core * 128, 128, 0)
    down = down.reshape(4, 32, WIDTH).transpose(1, 0, 2).reshape(32, HIDDEN)
    flat = jnp.concatenate(vectors).reshape(6, 128)
    extra = jnp.concatenate([flat, jnp.zeros((26, 128), BF16)], 0)
    packed = jnp.concatenate([half, down, extra], 1)
    gathered = lax.all_gather(packed, ("z", "y", "core"), axis=0, tiled=True)
    rows = gathered[:, VECTORS_AT:].reshape(16, 64, 128)[:, :6].astype(F32)
    pairs = rows[:, :4].reshape(16, 8, 64).transpose(1, 0, 2).reshape(8, WIDTH)
    ups = rows[:, 4:].reshape(1, HIDDEN)
    biases = jnp.concatenate(
        [pairs[0:1], jnp.zeros((1, WIDTH), F32), pairs[1:2], pairs[2:3], ups], 1
    )
    return gathered, biases, pairs


def send_around(blocks, axis):
    return [blocks[0]] + [
        lax.ppermute(blocks[k], axis, [(i, (i + k) % 4) for i in range(4)]) for k in (1, 2, 3)
    ]


def after_kernel(value_ref, earlier_ref, out_ref):
    pass


def after(value, earlier):
    memory = pl.BlockSpec(memory_space=pl.ANY)
    return pl.pallas_call(
        after_kernel,
        in_specs=[memory, memory],
        out_specs=memory,
        out_shape=jax.ShapeDtypeStruct(value.shape, value.dtype),
        input_output_aliases={0: 0},
        cost_estimate=SMALL,
        name="after",
    )(value, earlier)


def scatter_direct(place, lefts, rights):
    lefts, rights = halfway(place, send_around(lefts, "z"), send_around(rights, "y"))

    def total(parts):
        return sum(part.astype(F32) for part in parts).astype(BF16)

    owned = jnp.concatenate([total(send_around(lefts, "y")), total(send_around(rights, "z"))], 1)
    return lax.optimization_barrier(owned)


def over_replicas(owned):
    owned = lax.optimization_barrier(owned)
    far = swap_far(owned)
    return owned, far, swap_cores(owned), swap_cores(far)


def gradients(core, first_section, result, own, other, upstream, gathered, pairs, kept):
    rows16, c, hidden, e = own
    rows16_2, c_2, hidden_2, e_2, rows16_far = other
    place = jnp.stack([lax.axis_index("z"), lax.axis_index("y")]).astype(jnp.int32)
    far = lax.axis_index("far").astype(jnp.int32).reshape(1)
    branch, mine, theirs, pair_grads, up_grads = hidden_backward(
        core, upstream, gathered, pairs, kept
    )
    packed = first_grads((hidden, e, c), mine, (hidden_2, e_2, c_2), swap_cores(theirs))
    packed, rows16_far = lax.optimization_barrier((packed, rows16_far))
    rows16_both = swap_cores(rows16_far)
    owned = lax.psum_scatter(packed, ("z", "y"), scatter_dimension=0, tiled=True)

    rows_grad, mine, for_far, for_core, for_both, more_grads = attention_backward(
        core * 2 + far, branch, gathered, kept[0]
    )
    pair_grads = pair_grads + more_grads
    rows = jnp.concatenate(
        [
            pair_grads.reshape(8, 16, 64).transpose(1, 0, 2).reshape(16, 4, 128),
            up_grads.reshape(16, 2, 128),
        ],
        1,
    ).astype(BF16)
    extra = jnp.concatenate([rows, jnp.zeros((16, 58, 128), BF16)], 1).reshape(WIDTH, 128)
    quarters = (mine, swap_cores(for_core), swap_far(for_far), swap_both(for_both))
    blocks = last_grads(place, (rows16, rows16_2, rows16_far, rows16_both), quarters, extra)
    seconds = jnp.concatenate([result[LEN:], rows_grad[LEN:]])
    blocks, seconds = lax.optimization_barrier((blocks, seconds))
    swapped = swap_far(seconds)
    near = scatter_direct(place, *blocks)
    away, swapped = lax.optimization_barrier((swap_far(near), swapped))
    result, rows_grad = (
        jnp.concatenate(
            [
                value[:LEN],
                jnp.where(first_section, value[LEN:], swapped[at * LEN : (at + 1) * LEN]),
            ]
        )
        for at, value in enumerate((result, rows_grad))
    )
    near2, away2 = swap_cores(near), swap_cores(away)
    firsts = over_replicas(after(owned, away))
    project, output, upward, downward = finish(
        core, far, *firsts, near, near2, away, away2
    )
    ends = [part[:6, QUARTER:].astype(F32) for part in (near, away, near2, away2)]
    vectors = ((ends[0] + ends[1]) + (ends[2] + ends[3])).reshape(768)
    narrow = [vectors[64 * k : 64 * (k + 1)][None] for k in range(8)]
    query, value, output_b, down_b, gain_one, shift_one, gain_two, shift_two = narrow
    return result, rows_grad, (
        project[None],
        output[None],
        upward[None],
        downward[None],
        query,
        value,
        output_b,
        vectors[512:768][None],
        down_b,
        gain_one,
        shift_one,
        gain_two,
        shift_two,
    )


def to_section(value, section):
    pairs = [[(0, 2), (1, 3)], [(0, 3), (1, 2)]]
    if section == 0:
        pairs = [[(target, source) for source, target in each] for each in pairs]
    return jnp.concatenate(
        [
            lax.ppermute(value[seq * LEN : (seq + 1) * LEN], ("section", "far"), pairs[seq])
            for seq in range(2)
        ]
    )


def on_device(
    layer_input,
    cotangent,
    project_weight,
    output_weight,
    up_weight,
    down_weight,
    query_bias,
    value_bias,
    output_bias,
    up_bias,
    down_bias,
    first_gain,
    first_shift,
    second_gain,
    second_shift,
):
    first_section = lax.axis_index("section") == 0
    gathered, biases, pairs = gather_weights(
        project_weight[0],
        output_weight[0],
        up_weight[0],
        down_weight[0],
        (
            query_bias[0],
            value_bias[0],
            output_bias[0],
            down_bias[0],
            first_gain[0],
            first_shift[0],
            second_gain[0],
            second_shift[0],
            up_bias[0],
        ),
    )
    shape = layer_input.shape
    own_rows = layer_input.reshape(-1, WIDTH)
    own_grad = cotangent.reshape(-1, WIDTH)
    own_grad = jnp.concatenate([own_grad[:LEN], swap_far(own_grad[LEN:])])

    early = layer_forward(own_rows, gathered, biases, pairs, False)[0]
    received = to_section(early, 1)
    rows16 = jnp.where(first_section, own_rows, received)
    result, p, c, hidden, e, slope, n_one, r_one, n_two, r_two = layer_forward(
        rows16, gathered, biases, pairs, True
    )
    kept = (p, slope, n_one, r_one, n_two, r_two)
    own = (rows16, c, hidden, e)
    other = tuple(swap_cores(array) for array in own)
    rows16_far, own_grad = lax.optimization_barrier((swap_far(rows16), own_grad))
    other = (*other, rows16_far)

    early_grad = layer_through(own_grad, gathered, pairs, kept)
    back = to_section(early_grad, 0)
    upstream = jnp.where(first_section, back, own_grad)
    core = lax.axis_index("core").astype(jnp.int32).reshape(1)
    result, rows_grad, grads = gradients(core, first_section, result, own, other, upstream, gathered, pairs, kept)
    return (result.reshape(1, *shape), rows_grad.reshape(1, *shape), *grads)


def solution(mesh):
    devices = mesh.devices.reshape(2, 2, 2, 4, 4)
    fine = Mesh(devices, ("section", "far", "core", "z", "y"))
    shard = ("z", "y")
    seqs = P(None, ("far", "core", "z", "y"), None, None)
    matrix = P("section", shard, None)
    vector = P("section", shard)
    rows = P("section", None, ("far", "core", "z", "y"), None, None)
    return jax.shard_map(
        on_device,
        mesh=fine,
        in_specs=(seqs, seqs, *([matrix] * 4), *([vector] * 9)),
        out_specs=(rows, rows, *([matrix] * 4), *([vector] * 9)),
        check_vma=False,
    )
```
